32 devices in a mesh: fsdp: 8 (over y, x, core), blk: 4 (over z).
Axes of the slice: x: 2, y: 2, z: 4, core: 2. Of those that a mesh axis runs over, the one named last changes fastest.
Arguments:
- frames: bfloat16 [2, 4096, 1024], P(None, ('fsdp', 'blk')), may hold values from -6 to 6
- skipped: bfloat16 [2, 4096, 1024], P(None, ('fsdp', 'blk')), may hold values from -6 to 6
- lengths: int32 [2, 8, 9], P(None, 'fsdp'), may hold values from 1 to 504, as said below
- merger: bfloat16 [2048, 1024], P('fsdp'), may hold values from -0.125 to 0.125
- projector: bfloat16 [1024, 3072], P('fsdp'), may hold values from -0.1875 to 0.1875
- combiner: bfloat16 [1024, 1024], P('fsdp'), may hold values from -1 to 1
- expander: bfloat16 [1024, 4096], P('fsdp'), may hold values from -0.1875 to 0.1875
- reducer: bfloat16 [4096, 1024], P('fsdp'), may hold values from -0.09375 to 0.09375
- prenorm: bfloat16 [1024], P('fsdp'), may hold values from 0.25 to 1.75
- midnorm: bfloat16 [1024], P('fsdp'), may hold values from 0.25 to 1.75
- cotangent: bfloat16 [2, 4096, 1024], P(None, ('fsdp', 'blk')), may hold values from -6 to 6
Outputs:
- result: bfloat16 [2, 4096, 1024], P(None, ('fsdp', 'blk'))
- frames_gradient: float32 [2, 4096, 1024], P(None, ('fsdp', 'blk'))
- skipped_gradient: float32 [2, 4096, 1024], P(None, ('fsdp', 'blk'))
- merger_gradient: float32 [2048, 1024], P('fsdp')
- projector_gradient: float32 [1024, 3072], P('fsdp')
- combiner_gradient: float32 [1024, 1024], P('fsdp')
- expander_gradient: float32 [1024, 4096], P('fsdp')
- reducer_gradient: float32 [4096, 1024], P('fsdp')
- prenorm_gradient: float32 [1024], P('fsdp')
- midnorm_gradient: float32 [1024], P('fsdp')
The draws below stay inside these ranges and needn't reach their ends.
Inputs may be any that keep to these rules, and one draw needn't show every extreme that they name: The 9 lengths of each row add up to 512; in each row one of them, at a place drawn from the seed, begins within the first 128 frames of the stream and ends within its last 128 frames; every other has at most 15 frames.
All inputs are finite; a program needn't handle non-finite values.
Results may differ from the reference program's by a relative error of at most 0.02.
Values may be sent and summed in bfloat16 or wider, within the bound.
No kernel may reach another device: no remote copies, remote signals or barrier semaphores. Data moves between devices by JAX's collectives and lax.ppermute only.
A program may use at most 256 MiB of HBM per device.

```python
import math
import jax
import jax.numpy as jnp
from jax import lax

D = 1024
HEADS = 16
HEAD_DIM = 64
FF = 4096
MB = 2
NUTT = 9
SHORT = 15
STREAM = 512
ROWS = 4096
N_FSDP = 8


def draw_lengths(key, part):
    key = jax.random.fold_in(key, 7)
    short_key, place_key = jax.random.split(key)
    shorts = jax.random.randint(short_key, (MB, N_FSDP, NUTT), 1, SHORT + 1, dtype=jnp.int32)
    places = jax.random.randint(place_key, (MB, N_FSDP, 1), 0, NUTT, dtype=jnp.int32)
    is_long = jnp.arange(NUTT, dtype=jnp.int32)[None, None, :] == places
    shorts = jnp.where(is_long, 0, shorts)
    long_len = STREAM - jnp.sum(shorts, -1, keepdims=True)
    return jnp.where(is_long, long_len, shorts).astype(jnp.int32)


def levels(rng, dims, shards, low, high):
    def one(dim, shards_of):
        steps = jax.random.uniform(jax.random.fold_in(jax.random.fold_in(rng, 6), dim), (shards_of,), jnp.float32, low / len(shards), high / len(shards))
        return jnp.repeat(jnp.exp(steps), dims[dim] // shards_of).reshape((-1,) + (1,) * (len(dims) - dim - 1))

    loudness = one(*shards[0])
    for cut in shards[1:]:
        loudness = loudness * one(*cut)
    return loudness


def centred(rng, extent, width, bound, cuts=(), held_as=jnp.bfloat16):
    values = width * jax.random.normal(rng, extent, jnp.float32)
    if cuts:
        values = values * levels(rng, extent, cuts, -0.22, 0.18)
    return jnp.clip(values, -bound, bound).astype(held_as)


def setup_inputs(seed: int = 0) -> dict:
    arg_keys = jax.random.split(jax.random.key(seed), 12)
    return {
        "frames": centred(arg_keys[0], (MB, ROWS, D), 1.0, 6.0, ((1, 32),)),
        "skipped": centred(arg_keys[1], (MB, ROWS, D), 1.0, 6.0, ((1, 32),)),
        "lengths": draw_lengths(jax.random.fold_in(arg_keys[11], 71), 0),
        "merger": centred(arg_keys[3], (2 * D, D), (2 * D) ** -0.5, 0.125, ((0, 8),)),
        "projector": centred(arg_keys[4], (D, 3 * D), D ** -0.5, 0.1875, ((0, 8),)),
        "combiner": centred(arg_keys[5], (D, D), (max(1, D * 16 // STREAM)) ** -0.5, 1.0, ((0, 8),)),
        "expander": centred(arg_keys[6], (D, FF), D ** -0.5, 0.1875, ((0, 8),)),
        "reducer": centred(arg_keys[7], (FF, D), FF ** -0.5, 0.09375, ((0, 8),)),
        "prenorm": jnp.clip(1.0 + 0.15 * jax.random.normal(arg_keys[8], (D,), jnp.float32), 0.25, 1.75).astype(jnp.bfloat16),
        "midnorm": jnp.clip(1.0 + 0.15 * jax.random.normal(arg_keys[9], (D,), jnp.float32), 0.25, 1.75).astype(jnp.bfloat16),
        "cotangent": centred(arg_keys[10], (MB, ROWS, D), 1.0, 6.0, ((1, 32),)),
    }


@jax.custom_vjp
def low(v):
    return lax.optimization_barrier(v.astype(jnp.bfloat16)).astype(jnp.float32)

@jax.custom_vjp
def low_back(v):
    return v

def low_keep(v):
    return (low(v), None)

def low_pass(kept, grad):
    return (grad,)

def back_keep(v):
    return (v, None)

def back_low(kept, grad):
    return (low(grad),)
low.defvjp(low_keep, low_pass)
low_back.defvjp(back_keep, back_low)
NEG_BIG = -1e+30

def matmul(left, right):
    return jnp.dot(left, right, precision=lax.Precision.HIGHEST)

def rms_scale(hidden, gain):
    return hidden * lax.rsqrt(lax.optimization_barrier(jnp.mean(hidden * hidden, -1, keepdims=True)) + 1e-06) * gain

def layout(lengths_row):
    ends = jnp.cumsum(lengths_row).astype(jnp.int32)
    offsets = jnp.arange(STREAM, dtype=jnp.int32)
    before = (ends[None, :] <= offsets[:, None]).astype(jnp.int32)
    segment = lax.optimization_barrier(jnp.sum(before, 1)).astype(jnp.int32)
    begins = lax.optimization_barrier(jnp.sum(before * lengths_row[None, :], 1)).astype(jnp.int32)
    return (segment, (offsets - begins).astype(jnp.int32))

def rotary_tables(position):
    halfway = HEAD_DIM // 2
    inverse = 10000.0 ** (-jnp.arange(halfway, dtype=jnp.float32) * 2.0 / HEAD_DIM)
    angles = position.astype(jnp.float32)[:, None] * inverse[None, :]
    return (jnp.cos(angles), jnp.sin(angles))

def rotate(tensor, cosine, sine):
    halfway = tensor.shape[-1] // 2
    first = tensor[..., :halfway]
    second = tensor[..., halfway:]
    cosine = cosine[:, None, :]
    sine = sine[:, None, :]
    return jnp.concatenate([first * cosine - second * sine, second * cosine + first * sine], -1)

def attend_block(query_block, block_seg, keys, values, segments):
    scores = low_back(jnp.einsum('qhd,khd->hqk', query_block, keys, precision=lax.Precision.HIGHEST) * HEAD_DIM ** (-0.5))
    allowed = (block_seg[:, None] == segments[None, :])[None]
    scores = jnp.where(allowed, scores, NEG_BIG)
    peak = lax.optimization_barrier(jnp.max(scores, -1, keepdims=True))
    expo = jnp.exp(scores - peak)
    probs = expo / lax.optimization_barrier(jnp.sum(expo, -1, keepdims=True))
    return jnp.einsum('hqk,khd->qhd', low(probs), values, precision=lax.Precision.HIGHEST)

def attend_stream(stream_items):
    queries, keys, values, segments = stream_items
    block_rows = math.gcd(STREAM, 512)
    count = STREAM // block_rows

    def one_block(block_items):
        return attend_block(block_items[0], block_items[1], keys, values, segments)
    outputs = lax.map(jax.checkpoint(one_block), (queries.reshape(count, block_rows, HEADS, HEAD_DIM), segments.reshape(count, block_rows)))
    return outputs.reshape(STREAM, HEADS, HEAD_DIM)

def layer(frames_f, skipped_f, merger, projector, combiner, expander, reducer, prenorm, midnorm, segment, cosine, sine):
    joined = jnp.concatenate([frames_f, skipped_f], -1)
    hidden_zero = low_back(matmul(joined, merger))
    act_first = low(rms_scale(hidden_zero, prenorm))
    united = low_back(matmul(act_first, projector))
    query = low(rotate(united[:, :D].reshape(ROWS, HEADS, HEAD_DIM), cosine, sine))
    keys = low(rotate(united[:, D:2 * D].reshape(ROWS, HEADS, HEAD_DIM), cosine, sine))
    values = low(united[:, 2 * D:].reshape(ROWS, HEADS, HEAD_DIM))
    stream_shape = (N_FSDP, STREAM, HEADS, HEAD_DIM)
    attended = lax.map(attend_stream, (query.reshape(stream_shape), keys.reshape(stream_shape), values.reshape(stream_shape), segment.reshape(N_FSDP, STREAM)))
    attended = low_back(low(attended.reshape(ROWS, D)))
    hidden_one = hidden_zero + low_back(matmul(attended, combiner))
    act_second = low(rms_scale(hidden_one, midnorm))
    upper = low_back(matmul(act_second, expander))
    activ = low(jax.nn.gelu(upper, approximate=True))
    return hidden_one + low_back(matmul(activ, reducer))

def reference(frames, skipped, lengths, merger, projector, combiner, expander, reducer, prenorm, midnorm, cotangent):
    weights = tuple((item.astype(jnp.float32) for item in (merger, projector, combiner, expander, reducer, prenorm, midnorm)))
    totals = tuple((jnp.zeros_like(item) for item in weights))
    results = []
    frame_grads = []
    skip_grads = []
    for micro in range(MB):
        segment, position = jax.vmap(layout)(lengths[micro])
        segment = segment.reshape(ROWS)
        cosine, sine = rotary_tables(position.reshape(ROWS))

        def forward_pass(frames_f, skipped_f, w_merger, w_projector, w_combiner, w_expander, w_reducer, gain_pre, gain_mid):
            return layer(frames_f, skipped_f, w_merger, w_projector, w_combiner, w_expander, w_reducer, gain_pre, gain_mid, segment, cosine, sine)
        output, pull = jax.vjp(forward_pass, frames[micro].astype(jnp.float32), skipped[micro].astype(jnp.float32), weights[0], weights[1], weights[2], weights[3], weights[4], weights[5], weights[6])
        grads = pull(cotangent[micro].astype(jnp.float32))
        results.append(output.astype(jnp.bfloat16))
        frame_grads.append(grads[0])
        skip_grads.append(grads[1])
        totals = tuple((total + grad for total, grad in zip(totals, grads[2:])))
    return (jnp.stack(results), jnp.stack(frame_grads), jnp.stack(skip_grads), totals[0], totals[1], totals[2], totals[3], totals[4], totals[5], totals[6])
```

```python
import functools
import itertools

import jax
import jax.numpy as jnp
from jax import lax
from jax.experimental import pallas as pl
from jax.experimental.pallas import tpu as pltpu
from jax.sharding import PartitionSpec as P

D = 1024
HEADS = 16
HEAD_DIM = 64
MB = 2
PAIR = 2 * HEAD_DIM
CHIPS = 4
INDEX = 8
NEG_BIG = -1e30
EPS = 1e-6
AXES = ("fsdp", "blk")
BF = jnp.bfloat16
F32 = jnp.float32
MEGA = 1024 * 1024
SMALL, LARGE, HUGE = 20 * MEGA, 30 * MEGA, 60 * MEGA

MERGE_ROWS = 256
OWN_ROWS = 128
HIDDEN_ROWS = 512
GAIN_ROWS = 16


def dot(left, right):
    return jnp.dot(left, right, preferred_element_type=F32)


def dot_rows(left, right):
    return lax.dot_general(left, right, (((0,), (0,)), ((), ())), preferred_element_type=F32)


def dot_cols(left, right):
    return lax.dot_general(left, right, (((1,), (1,)), ((), ())), preferred_element_type=F32)


def norm_scale(hidden):
    return lax.rsqrt(jnp.mean(hidden * hidden, -1, keepdims=True) + EPS)


def norm_back(grad, hidden, gain):
    scale = norm_scale(hidden)
    weighted = grad * gain
    inner = jnp.mean(weighted * hidden, -1, keepdims=True)
    back = scale * weighted - hidden * (scale * scale * scale * inner)
    gain_grad = jnp.sum(grad * hidden * scale, 0, keepdims=True)
    return back, gain_grad


def swap_halves(tensor):
    lane = lax.broadcasted_iota(jnp.int32, tensor.shape, 1)
    low = (lane % HEAD_DIM) < HEAD_DIM // 2
    return jnp.where(
        low,
        pltpu.roll(tensor, PAIR - HEAD_DIM // 2, 1),
        pltpu.roll(tensor, HEAD_DIM // 2, 1),
    )


def turn(tensor, cosine, sine):
    return tensor * cosine + swap_halves(tensor) * sine


def aligned(at, size):
    return pl.ds(pl.multiple_of(at * size, size), size)


def stacked(parts):
    return jnp.concatenate([part[...] for part in parts], 0)


def summed(parts):
    return functools.reduce(jnp.add, [part[...].astype(F32) for part in parts])


def owner_of(index, chip, other):
    return 2 * index[chip] + (1 - index[4] if other else index[4])


def merge_kernel(index, left, right, *refs):
    weights = refs[: 2 * CHIPS]
    hidden_ref, cot_ref, pre_ref, mid_ref = refs[2 * CHIPS :]
    rows = left.shape[0]
    total = None
    for at, weight in enumerate(weights):
        mine = aligned(owner_of(index, at % CHIPS, at >= CHIPS), MERGE_ROWS)
        part = dot(jnp.concatenate([left[:, mine], right[:, mine]], 0), weight[:MERGE_ROWS])
        total = part if total is None else total + part
        mine = aligned(owner_of(index, at % CHIPS, at >= CHIPS), OWN_ROWS)
        gains = weight[MERGE_ROWS:, :OWN_ROWS].astype(F32)
        pre_ref[:, mine] = gains[0:1]
        mid_ref[:, mine] = gains[1:2]
    hidden_ref[...] = total
    cot_ref[:rows] = left[:, 2 * D :]
    cot_ref[rows:] = right[:, 2 * D :]


def project_kernel(
    index, hidden, gain, w_query, w_key, w_value, cosine, sine, act, query_ref, key_ref, value_ref
):
    @pl.when(pl.program_id(0) == 0)
    def _():
        act[...] = (hidden[...] * norm_scale(hidden[...]) * gain[...]).astype(BF)

    joint = lambda weight: dot(act[...], weight[...].reshape(D, weight.shape[2]))
    query = joint(w_query)
    key = joint(w_key)
    value_ref[...] = joint(w_value).astype(BF)
    for block in range(query_ref.shape[1] // PAIR):
        cols = slice(block * PAIR, (block + 1) * PAIR)
        turned = turn(query[:, cols], cosine[...], sine[...]).astype(BF)
        query_ref[:, cols] = turned * HEAD_DIM ** (-0.5)
        key_ref[:, cols] = turn(key[:, cols], cosine[...], sine[...]).astype(BF)


def head_mask(shape, head):
    lane = lax.broadcasted_iota(jnp.int32, shape, 1)
    return (lane // HEAD_DIM) == head


def attend_kernel(pieces, index, *refs):
    query, query_seg, key_segs = refs[:3]
    keys = refs[3 : 3 + pieces]
    values = refs[3 + pieces : 3 + 2 * pieces]
    weight, hidden_zero, gain = refs[3 + 2 * pieces : 6 + 2 * pieces]
    attended_ref, hidden_ref, act_ref, probs_ref = refs[6 + 2 * pieces :]
    allowed = [key_segs[piece] == query_seg[...] for piece in range(pieces)]
    step = pl.program_id(0)
    wide = query.shape[1]
    for block in range(wide // PAIR):
        cols = slice(block * PAIR, (block + 1) * PAIR)
        query_block = query[:, cols]
        key_blocks = [key[:, cols] for key in keys]
        value_blocks = [value[:, cols] for value in values]
        mixed = None
        for head in range(2):
            mask = head_mask(query_block.shape, head)
            one_query = jnp.where(mask, query_block, jnp.zeros_like(query_block))
            scores = [
                jnp.where(a, dot_cols(key, one_query), NEG_BIG)
                for key, a in zip(key_blocks, allowed)
            ]
            peak = functools.reduce(jnp.maximum, [jnp.max(s, 0, keepdims=True) for s in scores])
            expo = [jnp.exp(s - peak) for s in scores]
            inverse = 1.0 / functools.reduce(jnp.add, [jnp.sum(e, 0, keepdims=True) for e in expo])
            for piece in range(pieces):
                probs = (expo[piece] * inverse).astype(BF)
                probs_ref[2 * block + head, piece] = probs
                value = value_blocks[piece]
                part = dot_rows(jnp.where(mask, value, jnp.zeros_like(value)), probs)
                mixed = part if mixed is None else mixed + part
        attended_ref[:, aligned(step * (wide // PAIR) + block, PAIR)] = mixed.T.astype(BF)

    @pl.when(step == pl.num_programs(0) - 1)
    def _():
        hidden = hidden_zero[...] + dot(attended_ref[...], weight[...].reshape(D, D))
        hidden_ref[...] = hidden
        act_ref[...] = (hidden * norm_scale(hidden) * gain[...]).astype(BF)


GELU_ROOT = 0.7978845608028654
GELU_CUBE = 0.044715


def feed_kernel(index, act, cot, w_up, w_down, second_ref, activ_ref, upper_ref):
    cut = 256
    for at in range(w_up.shape[1] // cut):
        cols = slice(at * cut, (at + 1) * cut)
        upper = dot(act[...], w_up[:, cols])
        square = upper * upper
        bent = jnp.tanh(GELU_ROOT * upper * (1.0 + GELU_CUBE * square))
        half = 0.5 * (1.0 + bent)
        activ_ref[:, cols] = (upper * half).astype(BF)
        slope = half + 0.5 * upper * (1.0 - bent * bent) * (
            GELU_ROOT * (1.0 + 3.0 * GELU_CUBE * square)
        )
        upper_ref[:, cols] = (dot_cols(cot[...], w_down[cols, :]) * slope).astype(BF)
    second_ref[...] = dot_cols(upper_ref[...], w_up[...]).astype(BF)


def result_parts_kernel(index, own, other, w_down, own_ref, other_ref):
    own_ref[...] = dot(own[...], w_down[...]).astype(BF)
    other_ref[...] = dot(other[...], w_down[...]).astype(BF)


def down_grad_kernel(index, activ, activ_x, cot, cot_x, keep_ref, send_ref):
    core = index[4]
    step = pl.program_id(0)
    down = dot_rows(stacked((activ, activ_x)), stacked((cot, cot_x))).astype(BF)

    @pl.when(step % 2 == core)
    def _():
        keep_ref[0] = down

    @pl.when(step % 2 != core)
    def _():
        send_ref[0] = down


def up_grad_kernel(index, act, act_x, upper, upper_x, keep_ref, send_ref, total):
    core = index[4]
    column = pl.program_id(0) % 2
    total[...] = dot_rows(stacked((act, act_x)), stacked((upper, upper_x)))
    for ref, half in ((keep_ref, core), (send_ref, 1 - core)):
        mine = aligned(half, OWN_ROWS)
        for side in range(2):
            ref[0, column, side] = total[mine, side * D : (side + 1) * D].astype(BF)


def up_chip_kernel(index, own, got, own_ref, send_ref):
    for column, ref in enumerate((own_ref, send_ref)):
        for side in range(2):
            ref[side] = summed((own.at[column, side], got.at[column, 1 - side])).astype(BF)


def feed_total_kernel(index, down, up, reducer_ref, expander_ref):
    reducer_ref[...] = down[...].astype(F32)
    for column in range(2):
        for side in range(2):
            expander_ref[:, aligned(index[column + 2 * side], D)] = up[column, side].astype(F32)


def feed_send_kernel(index, expander, reducer, own_ref, send_ref, reducer_ref):
    reducer_ref[...] = reducer[...]
    for side in range(2):
        own_ref[side] = expander[:, aligned(index[2 * side], D)]
        send_ref[side] = expander[:, aligned(index[1 + 2 * side], D)]


def up_kernel(index, own, own_y, other, other_y, out_ref):
    for core, parts in enumerate(((own, own_y), (other, other_y))):
        here = 1 - index[4] if core else index[4]
        for row, part in enumerate(parts):
            for column in range(2):
                owner = 2 * index[column + 2 * row] + here
                for side in range(2):
                    cols = slice(side * D, (side + 1) * D)
                    out_ref[owner, :, cols] = part[column, side if row == 0 else 1 - side]


def down_kernel(index, own, own_y, other, other_y, out_ref):
    for side, (mine, theirs) in enumerate(((own, other), (own_y, other_y))):
        out_ref[2 * side + index[4]] = mine[...]
        out_ref[2 * side + 1 - index[4]] = theirs[...]


def attend_back_kernel(pieces, index, *refs):
    query, probs_ref = refs[:2]
    keys = refs[2 : 2 + pieces]
    values = refs[2 + pieces : 2 + 2 * pieces]
    at = 2 + 2 * pieces
    weight, hidden_one, cot, gain, cosine, sine = refs[at : at + 6]
    seconds = refs[at + 6 : at + 8]
    at += 8
    one_ref, low_ref, gain_ref, query_ref = refs[at : at + 4]
    pair_refs = refs[at + 4 : at + 4 + pieces]
    swap_ref = pair_refs[1]
    step = pl.program_id(0)

    @pl.when(step == 0)
    def _():
        back, gain_grad = norm_back(summed(seconds), hidden_one[...], gain[...])
        one = cot[...].astype(F32) + back
        one_ref[...] = one
        gain_ref[...] = gain_grad
        low_ref[...] = one.astype(BF)

    wide = query.shape[1]
    swap_ref[3] = low_ref[:, aligned(step, wide)]
    attended_grad = dot_cols(low_ref[...], weight[...].reshape(wide, D)).astype(BF)
    for block in range(wide // PAIR):
        cols = slice(block * PAIR, (block + 1) * PAIR)
        query_block = query[:, cols]
        grad_block = attended_grad[:, cols]
        key_blocks = [key[:, cols] for key in keys]
        value_blocks = [value[:, cols] for value in values]
        query_grad = None
        key_grads = [None] * pieces
        value_grads = [None] * pieces
        for head in range(2):
            mask = head_mask(query_block.shape, head)
            one_query = jnp.where(mask, query_block, jnp.zeros_like(query_block))
            one_grad = jnp.where(mask, grad_block, jnp.zeros_like(grad_block))
            low = [probs_ref[2 * block + head, piece] for piece in range(pieces)]
            probs = [p.astype(F32) for p in low]
            probs_grad = [dot_cols(value, one_grad) for value in value_blocks]
            delta = functools.reduce(
                jnp.add,
                [jnp.sum(p * g, 0, keepdims=True) for p, g in zip(probs, probs_grad)],
            )
            for piece in range(pieces):
                scores_grad = (probs[piece] * (probs_grad[piece] - delta)).astype(BF)
                key = key_blocks[piece]
                part = dot_rows(jnp.where(mask, key, jnp.zeros_like(key)), scores_grad)
                query_grad = part if query_grad is None else query_grad + part
                key_part = dot(scores_grad, one_query)
                value_part = dot(low[piece], one_grad)
                if head:
                    key_part += key_grads[piece]
                    value_part += value_grads[piece]
                key_grads[piece] = key_part
                value_grads[piece] = value_part
        query_grad = query_grad.T * HEAD_DIM ** (-0.5)
        query_grad = turn(query_grad, cosine[0], -sine[0]).astype(BF)
        query_ref[:, cols] = query_grad
        swap_ref[2, :, cols] = query_grad
        for piece in range(pieces):
            turned = turn(key_grads[piece], cosine[piece], -sine[piece])
            pair_refs[piece][0, :, cols] = turned.astype(BF)
            pair_refs[piece][1, :, cols] = value_grads[piece].astype(BF)


def united_kernel(pieces, index, *refs):
    query_grad, mid = refs[:2]
    pairs = refs[2 : 2 + pieces]
    at = 2 + pieces
    w_query, w_key, w_value, hidden_zero, one_grad, gain = refs[at : at + 6]
    swap_ref, left_ref, right_ref, first = refs[at + 6 :]
    step = pl.program_id(0)
    tok = query_grad.shape[0]
    place = lambda which: slice(which * tok, (which + 1) * tok)

    @pl.when(step == 0)
    def _():
        for which in range(2):
            total = functools.reduce(jnp.add, [part[which].astype(F32) for part in pairs])
            swap_ref[place(which)] = total.astype(BF)

    grads = (query_grad[...], swap_ref[place(0)], swap_ref[place(1)])
    first[step] = functools.reduce(
        jnp.add,
        [
            dot_cols(grad, weight[...].reshape(2 * OWN_ROWS, D))
            for grad, weight in zip(grads, (w_query, w_key, w_value))
        ],
    )

    @pl.when(step == CHIPS - 1)
    def _():
        grad = jnp.concatenate([first[chip] for chip in range(CHIPS)], 1)
        back, gain_grad = norm_back(grad, hidden_zero[...], gain[...])
        low = (one_grad[...] + back).astype(BF)
        swap_ref[place(2)] = low
        left_ref[...] = low[: tok // 2]
        right_ref[...] = low[tok // 2 :]
        rest = jnp.zeros((GAIN_ROWS - 2, D), F32)
        swap_ref[3 * tok :] = jnp.concatenate([gain_grad, mid[...], rest], 0).astype(BF)


def of_core(ref, index, size):
    return jnp.concatenate(
        [ref[:, aligned(2 * index[chip] + index[4], size)] for chip in range(CHIPS)], 1
    )


def put_slabs(total, rows, at, order, keep_ref, send_ref):
    for ref, chips in ((keep_ref, order[:2]), (send_ref, order[2:])):
        for place, chip in enumerate(chips):
            ref[place, at : at + rows] = total[chip * rows : (chip + 1) * rows].astype(BF)


X_FIRST = (0, 2, 1, 3)
Y_FIRST = (0, 1, 2, 3)


def query_grad_kernel(
    index, act, act_c, attended, attended_c, grad, low, swapped, keep_ref, send_ref
):
    lefts = ((act, act_c), (attended, attended_c))
    rights = ((grad[...], swapped[2]), (low[...], swapped[3]))
    for which, (left, right) in enumerate(zip(lefts, rights)):
        both = jnp.concatenate([of_core(part, index, OWN_ROWS) for part in left], 0)
        total = dot_rows(both, jnp.concatenate(right, 0))
        put_slabs(total, OWN_ROWS, which * OWN_ROWS, X_FIRST, keep_ref, send_ref)


def pair_grad_kernel(index, act, act_c, own, swapped, keep_ref, send_ref):
    tok = act.shape[0]
    both = jnp.concatenate([of_core(part, index, OWN_ROWS) for part in (act, act_c)], 0)
    for which in range(2):
        place = slice(which * tok, (which + 1) * tok)
        total = dot_rows(both, jnp.concatenate([own[place], swapped[place]], 0))
        put_slabs(total, OWN_ROWS, which * OWN_ROWS, Y_FIRST, keep_ref, send_ref)


def merge_grad_kernel(index, left, right, left_c, right_c, own, swapped, keep_ref, send_ref):
    tok = 2 * left.shape[0]
    both = jnp.concatenate(
        [of_core(part, index, MERGE_ROWS) for part in (left, right, left_c, right_c)], 0
    )
    low = slice(2 * tok, 3 * tok)
    total = dot_rows(both, jnp.concatenate([own[low], swapped[low]], 0))
    put_slabs(total, MERGE_ROWS, 0, X_FIRST, keep_ref, send_ref)
    gains = own[3 * tok :].astype(F32) + swapped[3 * tok :].astype(F32)
    keep_ref[:, MERGE_ROWS:] = jnp.zeros((2, GAIN_ROWS, D), BF)
    send_ref[:, MERGE_ROWS:] = jnp.zeros((2, GAIN_ROWS, D), BF)
    for ref, chips in ((keep_ref, X_FIRST[:2]), (send_ref, X_FIRST[2:])):
        for place, chip in enumerate(chips):
            owner = 2 * index[chip] + index[4]
            lane = lax.broadcasted_iota(jnp.int32, gains.shape, 1)
            mine = jnp.where(lane // OWN_ROWS == owner, gains, 0.0)
            chosen = functools.reduce(
                jnp.add,
                [mine[:, at * OWN_ROWS : (at + 1) * OWN_ROWS] for at in range(D // OWN_ROWS)],
            )
            ref[place, MERGE_ROWS:, :OWN_ROWS] = chosen.astype(BF)


def joined_grad_kernel(index, first, second, *refs):
    weights = refs[: 2 * CHIPS]
    rows = first.shape[0]
    low = jnp.concatenate([first[...], second[...]], 0)
    micro = index[5]
    for at, weight in enumerate(weights):
        grad = dot_cols(low, weight[:MERGE_ROWS])
        owner = owner_of(index, at % CHIPS, at >= CHIPS)
        cols = aligned(owner % CHIPS, MERGE_ROWS)
        for half, out_ref in enumerate(refs[2 * CHIPS :]):

            @pl.when(owner // CHIPS == half)
            def _():
                out_ref[micro, :, cols] = grad[:rows]
                out_ref[1 - micro, :, cols] = grad[rows:]


def add_kernel(index, *refs):
    refs[-1][...] = summed(refs[:-1]).astype(BF)


def add_two_kernel(index, keep, got, own_ref, other_ref):
    own_ref[...] = summed((keep.at[0], got.at[0])).astype(BF)
    other_ref[...] = summed((keep.at[1], got.at[1])).astype(BF)


def stack_kernel(index, *refs):
    for at, part in enumerate(refs[:-1]):
        refs[-1][at] = part[...]


def result_kernel(index, *refs):
    left, right = refs[-2:]
    rows = left.shape[0]
    total = summed(refs[:-2])
    left[...] = total[:rows].astype(BF)
    right[...] = total[rows:].astype(BF)


def by_micro_kernel(index, first, second, out_ref):
    out_ref[index[5]] = first[...]
    out_ref[1 - index[5]] = second[...]


def chosen(index, array, got, ends):
    here = functools.reduce(jnp.logical_or, [index[6] == end for end in ends])
    return jnp.where(here, got[...], array[...])


def choose_kernel(ends, index, array, got, out_ref):
    out_ref[...] = chosen(index, array, got, ends)


def query_total_kernel(ends, index, array, got, query_ref, combiner_ref):
    total = chosen(index, array, got, ends).astype(F32)
    query_ref[...] = total[:OWN_ROWS]
    combiner_ref[...] = total[OWN_ROWS:]


def pair_total_kernel(ends, index, array, got, query, out_ref):
    total = chosen(index, array, got, ends).astype(F32)
    out_ref[:, :D] = query[...]
    out_ref[:, D : 2 * D] = total[:OWN_ROWS]
    out_ref[:, 2 * D :] = total[OWN_ROWS:]


def merge_total_kernel(ends, index, array, got, out_ref, gain_ref):
    total = chosen(index, array, got, ends).astype(F32)
    out_ref[...] = total[:MERGE_ROWS]
    gain_ref[...] = total[MERGE_ROWS : MERGE_ROWS + 8, :OWN_ROWS]


def call(kernel, vmem, grid, in_specs, out_specs, out_shape, scratch, index, *arrays):
    def passing(index_ref, *refs):
        inputs = len(in_specs)
        for at in range(INDEX):
            refs[inputs][at] = index_ref[at]
        kernel(index_ref, *refs[:inputs], *refs[inputs + 1 :])

    return pl.pallas_call(
        passing,
        grid_spec=pltpu.PrefetchScalarGridSpec(
            num_scalar_prefetch=1,
            grid=(grid,),
            in_specs=in_specs,
            out_specs=[pl.BlockSpec(memory_space=pltpu.SMEM)] + out_specs,
            scratch_shapes=scratch,
        ),
        out_shape=[jax.ShapeDtypeStruct((INDEX,), jnp.int32)] + out_shape,
        name=getattr(kernel, "func", kernel).__name__,
        compiler_params=pltpu.CompilerParams(
            dimension_semantics=("arbitrary",), vmem_limit_bytes=vmem
        ),
        cost_estimate=pl.CostEstimate(flops=10**12, bytes_accessed=0, transcendentals=0),
    )(index, *arrays)


def shape(*dims, dtype=BF):
    return jax.ShapeDtypeStruct(dims, dtype)


def whole(*dims):
    return pl.BlockSpec(dims, lambda *_: (0,) * len(dims))


def local(
    frames,
    skipped,
    lengths,
    merger,
    projector,
    combiner,
    expander,
    reducer,
    prenorm,
    midnorm,
    cotangent,
):
    rows = frames.shape[1]
    tok = 2 * rows
    blocks = lax.axis_size("blk")
    fsdp = lax.axis_size("fsdp")
    quarter = blocks // 4
    pieces = blocks // 2
    stream = rows * blocks

    me = lax.axis_index("fsdp")
    spot = lax.axis_index("blk")
    core = me % 2
    chip = me // 2
    unit = spot // quarter
    micro = unit // 2
    source_core = unit % 2
    half = (spot % quarter) * 2 + core

    def send(array, route, name="send"):
        pairs = []
        for y, x, c, b in itertools.product(range(2), range(2), range(2), range(blocks)):
            target = route(y, x, c, b)
            if target is not None:
                ty, tx, tc, tb = target
                pairs.append((((y * 2 + x) * 2 + c) * blocks + b, ((ty * 2 + tx) * 2 + tc) * blocks + tb))
        with jax.named_scope(name):
            return lax.ppermute(array, AXES, pairs)

    to_x = lambda y, x, c, b: (y, 1 - x, c, b)
    to_y = lambda y, x, c, b: (1 - y, x, c, b)
    to_diagonal = lambda y, x, c, b: (1 - y, 1 - x, c, b)
    to_core = lambda y, x, c, b: (y, x, 1 - c, b)
    around = (to_x, to_y, to_diagonal)

    def holder(micro_at, c, pair):
        return (2 * micro_at + c) * quarter + pair // 2, pair % 2

    def inward(other):
        def route(y, x, c, b):
            tb, tc = holder((b + other) % 2, c, b // 2)
            return (y, x, tc, tb)

        return route

    def outward(other):
        forward = inward(other)
        table = {}
        for y, x, c, b in itertools.product(range(2), range(2), range(2), range(blocks)):
            table[forward(y, x, c, b)] = (y, x, c, b)
        return lambda *at: table[at]

    def among(by):
        def route(y, x, c, b):
            at = ((b % quarter) * 2 + c) ^ by
            return (y, x, at % 2, (b // quarter) * quarter + at // 2)

        return route

    def take_in(pick, name):
        return tuple(send(pick((spot + other) % 2), inward(other), name) for other in range(2))

    def sum_blocks(array, name, last):
        middle = blocks // 2
        plans = [{step: step + 1, blocks - 1 - step: blocks - 2 - step} for step in range(middle - 1)]
        plans.append({middle - 1: middle, middle: middle - 1})
        for moves in plans:
            got = send(array, lambda y, x, c, b: (y, x, c, moves[b]) if b in moves else None, name)
            yield
            array = add(array, got)
        for step in range(middle - 1):
            moves = {middle - 1 - step: middle - 2 - step, middle + step: middle + 1 + step}
            got = send(array, lambda y, x, c, b: (y, x, c, moves[b]) if b in moves else None, name)
            yield
            ends = tuple(moves.values())
            if step == middle - 2:
                array = last(ends, array, got)
            else:
                choose = functools.partial(choose_kernel, ends)
                array = simple(choose, [shape(*array.shape)], array, got)
        yield array

    def finish(steps):
        array = None
        while array is None:
            array = next(steps)
        return array

    gathered = lax.all_gather(jnp.concatenate([projector, combiner], 1), "fsdp", axis=0)

    gain_rows = jnp.pad(jnp.stack([prenorm, midnorm]), ((0, GAIN_ROWS - 2), (0, D - OWN_ROWS)))
    merger_own = jnp.concatenate([merger, gain_rows], 0)
    mergers = [merger_own] + [send(merger_own, route, "merger_around") for route in around]
    mergers += [send(part, to_core, "merger_core") for part in mergers]

    left, right = take_in(
        lambda m: jnp.concatenate([frames[m], skipped[m], cotangent[m]], -1), "tokens_in"
    )
    other_lengths = send(lengths, to_core, "lengths_core")
    half_chunk = expander.shape[1] // 2

    mine = jnp.where(source_core == core, lengths, other_lengths)[:, 0]
    row_lengths = jnp.where(micro == 0, mine[0], mine[1])
    ends = jnp.cumsum(row_lengths)
    within = jnp.arange(rows, dtype=jnp.int32)

    def layout(at):
        offsets = jnp.concatenate(
            [(2 * at + micro) * rows + within, (2 * at + 1 - micro) * rows + within]
        )
        before = (ends[None, :] <= offsets[:, None]).astype(jnp.int32)
        return jnp.sum(before, 1), offsets - jnp.sum(before * row_lengths[None, :], 1)

    layouts = [layout(half ^ by) for by in range(pieces)]
    query_seg = layouts[0][0][None]
    key_segs = jnp.stack([segment for segment, _ in layouts])[:, :, None]
    inverse = 10000.0 ** (-jnp.arange(HEAD_DIM // 2, dtype=F32) * 2.0 / HEAD_DIM)
    positions = jnp.stack([position for _, position in layouts]).astype(F32)
    angles = positions[:, :, None] * inverse
    cosine = jnp.tile(jnp.cos(angles), (1, 1, 4))
    sine = jnp.sin(angles)
    sine = jnp.concatenate([-sine, sine, -sine, sine], -1)

    index = jnp.stack(
        [chip, chip ^ 1, chip ^ 2, chip ^ 3, core, spot % 2, spot, spot]
    ).astype(jnp.int32)
    last_index = [index]

    def run(kernel, grid, in_specs, out_specs, out_shape, scratch, *arrays, vmem=SMALL):
        last_index[0], *results = call(
            kernel, vmem, grid, in_specs, out_specs, out_shape, scratch, last_index[0], *arrays
        )
        return results[0] if len(results) == 1 else results

    def simple(kernel, outs, *arrays):
        return run(
            kernel,
            1,
            [whole(*array.shape) for array in arrays],
            [whole(*out.shape) for out in outs],
            outs,
            [],
            *arrays,
        )

    def to_total(kernel, outs):
        return lambda ends, array, got: simple(functools.partial(kernel, ends), outs, array, got)

    def add(*arrays):
        return simple(add_kernel, [shape(*arrays[0].shape)], *arrays)

    def first_step(keep, got):
        return simple(add_two_kernel, [shape(*keep.shape[1:])] * 2, keep, got)

    wide = 2 * OWN_ROWS
    cols_at = lambda height, width: pl.BlockSpec((height, width), lambda s, i: (0, s))
    cols_of = lambda height, width: pl.BlockSpec((height, width), lambda s, i: (0, i[s]))
    slab_at = lambda at: pl.BlockSpec((2, OWN_ROWS, D), lambda s, i: (s, 0, at))
    column_at = lambda at: pl.BlockSpec(
        (fsdp, OWN_ROWS, wide), lambda s, i: (0, 0, at * (D // wide) + s)
    )
    table = whole(tok, PAIR)
    tables = whole(pieces, tok, PAIR)
    own_cols = cols_at(tok, wide)

    hidden_zero, cot, gain_pre, gain_mid = simple(
        merge_kernel,
        [shape(tok, D, dtype=F32), shape(tok, D)] + [shape(1, D, dtype=F32)] * 2,
        left,
        right,
        *mergers,
    )
    cot_x = send(cot, to_x, "cot_x")

    up_own, up_send, down_own = simple(
        feed_send_kernel,
        [shape(2, OWN_ROWS, D), shape(2, OWN_ROWS, D), shape(*reducer.shape)],
        expander,
        reducer,
    )
    up_x = send(up_send, to_x, "w_up_x")
    down_y = send(down_own, to_y, "w_down_y")
    down_c = send(down_own, to_core, "w_down_core")
    act_first, query, key, value = run(
        project_kernel,
        CHIPS,
        [whole(tok, D), whole(1, D)] + [column_at(at) for at in range(3)] + [table, table],
        [whole(tok, D)] + [own_cols] * 3,
        [shape(tok, D)] * 4,
        [],
        hidden_zero,
        gain_pre,
        gathered,
        gathered,
        gathered,
        cosine[0],
        sine[0],
        vmem=LARGE,
    )
    up_pair = jnp.stack([up_own, up_x])
    up_y = send(up_pair, to_y, "w_up_y")
    up_c = send(up_pair, to_core, "w_up_core")
    keys = [key] + [send(key, among(by), "keys_core") for by in range(1, pieces)]
    values = [value] + [send(value, among(by), "values_core") for by in range(1, pieces)]
    act_first_c = send(act_first, to_core, "act_core")
    left_c = send(left, to_core, "joined_core")
    right_c = send(right, to_core, "joined_core")
    steps, vmem = (1, LARGE) if pieces == 2 else (CHIPS * 2, HUGE)
    head_cols = cols_at(tok, D // steps)
    probs_spec = pl.BlockSpec((HEADS // steps, pieces, tok, tok), lambda s, i: (s, 0, 0, 0))
    attended, hidden_one, act_second, probs = run(
        functools.partial(attend_kernel, pieces),
        steps,
        [head_cols, whole(1, tok), whole(pieces, tok, 1)]
        + [head_cols] * (2 * pieces)
        + [pl.BlockSpec((fsdp, OWN_ROWS, D), lambda s, i: (0, 0, 3)), whole(tok, D), whole(1, D)],
        [whole(tok, D), whole(tok, D), whole(tok, D), probs_spec],
        [
            shape(tok, D),
            shape(tok, D, dtype=F32),
            shape(tok, D),
            shape(HEADS, pieces, tok, tok),
        ],
        [],
        query,
        query_seg,
        key_segs,
        *keys,
        *values,
        gathered,
        hidden_zero,
        gain_mid,
        vmem=vmem,
    )
    attended_c = send(attended, to_core, "attended_core")

    down_yc = send(down_y, to_core, "w_down_core")
    w_down = simple(
        down_kernel, [shape(4, HIDDEN_ROWS, D)], reducer, down_y, down_c, down_yc
    ).reshape(half_chunk, D)

    act_x = send(act_second, to_x, "act_x")
    up_yc = send(up_y, to_core, "w_up_core")
    w_up = simple(
        up_kernel, [shape(fsdp, OWN_ROWS, half_chunk)], up_pair, up_y, up_c, up_yc
    ).reshape(D, half_chunk)

    def feed(act, grad):
        return simple(
            feed_kernel,
            [shape(tok, D), shape(tok, half_chunk), shape(tok, half_chunk)],
            act,
            grad,
            w_up,
            w_down,
        )

    second, activ, upper = feed(act_second, cot)
    second_x, activ_x, upper_x = feed(act_x, cot_x)
    second_got = send(second_x, to_x, "second_x")
    many_cols = cols_at(tok, half_chunk // CHIPS)
    near_cols = cols_of(tok, wide)
    down_half = pl.BlockSpec((1, HIDDEN_ROWS, D), lambda s, i: (s // 2, 0, 0))
    down_keep, down_send = run(
        down_grad_kernel,
        CHIPS,
        [many_cols, many_cols, whole(tok, D), whole(tok, D)],
        [down_half, down_half],
        [shape(2, HIDDEN_ROWS, D)] * 2,
        [],
        activ,
        activ_x,
        cot,
        cot_x,
    )
    down_got = send(down_send, to_core, "down_core")
    up_half = pl.BlockSpec((1, 2, 2, OWN_ROWS, D), lambda s, i: (s // 2, 0, 0, 0, 0))
    up_keep, up_send = run(
        up_grad_kernel,
        CHIPS,
        [near_cols, near_cols, whole(tok, half_chunk), whole(tok, half_chunk)],
        [up_half, up_half],
        [shape(2, 2, 2, OWN_ROWS, D)] * 2,
        [pltpu.VMEM((wide, half_chunk), F32)],
        act_second,
        act_x,
        upper,
        upper_x,
    )
    up_got = send(up_send, to_core, "up_core")
    down_one, down_two = first_step(down_keep, down_got)
    down_y = send(down_two, to_y, "down_y")

    steps = CHIPS if pieces == 2 else 2 * CHIPS
    head_cols = cols_at(tok, D // steps)
    probs_spec = pl.BlockSpec((HEADS // steps, pieces, tok, tok), lambda s, i: (s, 0, 0, 0))
    pair_cols = lambda count: pl.BlockSpec((count, tok, D // steps), lambda s, i: (0, 0, s))
    counts = [4 if by == 1 else 2 for by in range(pieces)]
    back = run(
        functools.partial(attend_back_kernel, pieces),
        steps,
        [head_cols, probs_spec]
        + [head_cols] * (2 * pieces)
        + [pl.BlockSpec((fsdp // steps, OWN_ROWS, D), lambda s, i: (s, 0, 3))]
        + [whole(tok, D), whole(tok, D), whole(1, D)]
        + [tables, tables]
        + [whole(tok, D)] * 2,
        [whole(tok, D), whole(tok, D), whole(1, D), head_cols] + [pair_cols(n) for n in counts],
        [
            shape(tok, D, dtype=F32),
            shape(tok, D),
            shape(1, D, dtype=F32),
            shape(tok, D),
        ]
        + [shape(n, tok, D) for n in counts],
        [],
        query,
        probs,
        *keys,
        *values,
        gathered,
        hidden_one,
        cot,
        gain_mid,
        cosine,
        sine,
        second,
        second_got,
        vmem=vmem,
    )
    one_grad, one_low, mid_grad, query_grad = back[:4]
    pairs = [back[4]] + [
        send(part, among(by), "pair_grads_core") for by, part in enumerate(back[5:], 1)
    ]
    up_one, up_two = first_step(up_keep, up_got)
    up_y = send(up_two, to_y, "up_y")
    swapped, zero_left, zero_right = run(
        functools.partial(united_kernel, pieces),
        CHIPS,
        [whole(tok, D), whole(1, D)]
        + [whole(n, tok, D) for n in counts]
        + [slab_at(at) for at in range(3)]
        + [whole(tok, D), whole(tok, D), whole(1, D)],
        [whole(3 * tok + GAIN_ROWS, D), whole(rows, D), whole(rows, D)],
        [shape(3 * tok + GAIN_ROWS, D), shape(rows, D), shape(rows, D)],
        [pltpu.VMEM((CHIPS, tok, wide), F32)],
        query_grad,
        mid_grad,
        *pairs,
        gathered,
        gathered,
        gathered,
        hidden_zero,
        one_grad,
        gain_pre,
        vmem=LARGE,
    )
    swapped_c = send(swapped, to_core, "zero_core")
    zero_back = [
        send(part, outward(other), "zero_out") for other, part in enumerate([zero_left, zero_right])
    ]

    def slabs_of(kernel, height, *arrays):
        return simple(kernel, [shape(2, height, D)] * 2, *arrays)

    query_keep, query_send = slabs_of(
        query_grad_kernel,
        2 * OWN_ROWS,
        act_first,
        act_first_c,
        attended,
        attended_c,
        query_grad,
        one_low,
        pairs[1],
    )
    query_got = send(query_send, to_x, "query_x")
    merge_keep, merge_send = slabs_of(
        merge_grad_kernel,
        MERGE_ROWS + GAIN_ROWS,
        left,
        right,
        left_c,
        right_c,
        swapped,
        swapped_c,
    )
    merge_got = send(merge_send, to_x, "merge_x")
    pair_keep, pair_send = slabs_of(
        pair_grad_kernel, 2 * OWN_ROWS, act_first, act_first_c, swapped, swapped_c
    )
    pair_got = send(pair_send, to_y, "pair_y")
    up_own, up_send = simple(up_chip_kernel, [shape(2, OWN_ROWS, D)] * 2, up_one, up_y)
    up_x = send(up_send, to_x, "up_x")
    down_sum = add(down_one, down_y)
    query_own, query_other = first_step(query_keep, query_got)
    query_y = send(query_other, to_y, "query_y")
    frames_grad, skipped_grad = simple(
        joined_grad_kernel, [shape(MB, rows, D, dtype=F32)] * 2, *zero_back, *mergers
    )
    up_sum = simple(stack_kernel, [shape(2, 2, OWN_ROWS, D)], up_own, up_x)
    down_total, up_total = lax.psum((down_sum, up_sum), "blk")
    merge_own, merge_other = first_step(merge_keep, merge_got)
    merge_y = send(merge_other, to_y, "merge_y")
    pair_own, pair_other = first_step(pair_keep, pair_got)
    pair_x = send(pair_other, to_x, "pair_x")
    result_own, result_other = simple(
        result_parts_kernel, [shape(tok, D)] * 2, activ, activ_x, w_down
    )
    result_x = send(result_other, to_x, "result_x")
    query_steps = sum_blocks(
        add(query_own, query_y),
        "query_blocks",
        to_total(query_total_kernel, [shape(OWN_ROWS, D, dtype=F32)] * 2),
    )
    next(query_steps)
    merge_steps = sum_blocks(
        add(merge_own, merge_y),
        "merge_blocks",
        to_total(
            merge_total_kernel,
            [shape(*merger.shape, dtype=F32), shape(8, OWN_ROWS, dtype=F32)],
        ),
    )
    next(merge_steps)
    to_projector = lambda ends, array, got: simple(
        functools.partial(pair_total_kernel, ends),
        [shape(*projector.shape, dtype=F32)],
        array,
        got,
        query_total,
    )
    pair_steps = sum_blocks(add(pair_own, pair_x), "pair_blocks", to_projector)
    next(pair_steps)
    next(query_steps)
    next(merge_steps)
    next(pair_steps)
    results = simple(result_kernel, [shape(rows, D)] * 2, result_own, result_x, hidden_one)
    results = [send(part, outward(other), "result_out") for other, part in enumerate(results)]
    next(query_steps)
    next(merge_steps)
    next(pair_steps)
    query_total, combiner_grad = finish(query_steps)
    merger_grad, gain_grads = finish(merge_steps)
    result_out = simple(by_micro_kernel, [shape(MB, rows, D)], *results)
    projector_grad = finish(pair_steps)
    reducer_grad, expander_grad = simple(
        feed_total_kernel,
        [shape(*reducer.shape, dtype=F32), shape(*expander.shape, dtype=F32)],
        down_total,
        up_total,
    )
    return (
        result_out,
        frames_grad,
        skipped_grad,
        merger_grad,
        projector_grad,
        combiner_grad,
        expander_grad,
        reducer_grad,
        gain_grads[0],
        gain_grads[1],
    )


def solution(mesh):
    tokens = P(None, ("fsdp", "blk"), None)
    weight = P("fsdp", None)
    gain = P("fsdp")
    return jax.shard_map(
        local,
        mesh=mesh,
        in_specs=(tokens, tokens, P(None, "fsdp", None))
        + (weight,) * 5
        + (gain, gain, tokens),
        out_specs=(tokens, tokens, tokens) + (weight,) * 5 + (gain, gain),
        check_vma=False,
    )
```

```python
import functools
import itertools

import jax
import jax.numpy as jnp
from jax import lax
from jax.experimental import pallas as pl
from jax.experimental.pallas import tpu as pltpu
from jax.sharding import PartitionSpec as P

D = 1024
HEADS = 16
HEAD_DIM = 64
MB = 2
PAIR = 2 * HEAD_DIM
CHIPS = 4
NEG_BIG = -1e30
EPS = 1e-6
AXES = ("fsdp", "blk")
BF = jnp.bfloat16
F32 = jnp.float32
MEGA = 1024 * 1024
SMALL, LARGE, HUGE = 20 * MEGA, 30 * MEGA, 60 * MEGA

MERGE_ROWS = 256
OWN_ROWS = 128
HIDDEN_ROWS = 512
GAIN_ROWS = 16


def dot(left, right):
    return jnp.dot(left, right, preferred_element_type=F32)


def dot_rows(left, right):
    return lax.dot_general(left, right, (((0,), (0,)), ((), ())), preferred_element_type=F32)


def dot_cols(left, right):
    return lax.dot_general(left, right, (((1,), (1,)), ((), ())), preferred_element_type=F32)


def norm_scale(hidden):
    return lax.rsqrt(jnp.mean(hidden * hidden, -1, keepdims=True) + EPS)


def norm_back(grad, hidden, gain):
    scale = norm_scale(hidden)
    weighted = grad * gain
    inner = jnp.mean(weighted * hidden, -1, keepdims=True)
    back = scale * weighted - hidden * (scale * scale * scale * inner)
    gain_grad = jnp.sum(grad * hidden * scale, 0, keepdims=True)
    return back, gain_grad


def swap_halves(tensor):
    lane = lax.broadcasted_iota(jnp.int32, tensor.shape, 1)
    low = (lane % HEAD_DIM) < HEAD_DIM // 2
    return jnp.where(
        low,
        pltpu.roll(tensor, PAIR - HEAD_DIM // 2, 1),
        pltpu.roll(tensor, HEAD_DIM // 2, 1),
    )


def turn(tensor, cosine, sine):
    return tensor * cosine + swap_halves(tensor) * sine


def aligned(at, size):
    return pl.ds(pl.multiple_of(at * size, size), size)


def stacked(parts):
    return jnp.concatenate([part[...] for part in parts], 0)


def summed(parts):
    return functools.reduce(jnp.add, [part[...].astype(F32) for part in parts])


def owner_of(index, chip, other):
    return 2 * index[chip] + (1 - index[4] if other else index[4])


def merge_kernel(index, left, right, *refs):
    weights = refs[: 2 * CHIPS]
    hidden_ref, cot_ref, joined_ref, pre_ref, mid_ref = refs[2 * CHIPS :]
    rows = left.shape[0]
    joined_ref[:rows] = left[:, : 2 * D]
    joined_ref[rows:] = right[:, : 2 * D]
    total = None
    for at, weight in enumerate(weights):
        mine = aligned(owner_of(index, at % CHIPS, at >= CHIPS), MERGE_ROWS)
        part = dot(joined_ref[:, mine], weight[:MERGE_ROWS])
        total = part if total is None else total + part
        mine = aligned(owner_of(index, at % CHIPS, at >= CHIPS), OWN_ROWS)
        gains = weight[MERGE_ROWS:, :OWN_ROWS].astype(F32)
        pre_ref[:, mine] = gains[0:1]
        mid_ref[:, mine] = gains[1:2]
    hidden_ref[...] = total
    cot_ref[:rows] = left[:, 2 * D :]
    cot_ref[rows:] = right[:, 2 * D :]


def fetch(array, at, held, sem):
    copies = [
        pltpu.make_async_copy(
            array.at[:, :, (at + which) * D : (at + which + 1) * D], held.at[which], sem.at[which]
        )
        for which in range(held.shape[0])
    ]
    for copy in copies:
        copy.start()
    return copies


def project_kernel(
    index, hidden, gain, gathered, cosine, sine, cot, act_ref, query_ref, pair_ref, cot_ref, held, sem
):
    copies = fetch(gathered, 0, held, sem)
    cot_ref[...] = cot[...]
    act = (hidden[...] * norm_scale(hidden[...]) * gain[...]).astype(BF)
    act_ref[...] = act
    for which, copy in enumerate(copies):
        copy.wait()
        for part in range(CHIPS):
            wide = slice(part * 2 * PAIR, (part + 1) * 2 * PAIR)
            united = dot(act, held[which, :, :, wide].reshape(D, 2 * PAIR))
            if which == 2:
                pair_ref[1, :, wide] = united.astype(BF)
                continue
            for block in range(2):
                cols = slice(block * PAIR, (block + 1) * PAIR)
                turned = turn(united[:, cols], cosine[...], sine[...]).astype(BF)
                cols = slice((2 * part + block) * PAIR, (2 * part + block + 1) * PAIR)
                if which == 0:
                    query_ref[:, cols] = turned * HEAD_DIM ** (-0.5)
                else:
                    pair_ref[0, :, cols] = turned


def head_mask(shape, head):
    lane = lax.broadcasted_iota(jnp.int32, shape, 1)
    return (lane // HEAD_DIM) == head


def attend_kernel(pieces, index, *refs):
    query, query_seg, key_segs = refs[:3]
    pairs = refs[3 : 3 + pieces]
    act_first, gathered, hidden_zero, gain = refs[3 + pieces : 7 + pieces]
    both_ref, hidden_ref, act_ref, probs_ref, held, sem = refs[7 + pieces :]
    weight = pltpu.make_async_copy(gathered.at[:, :, 3 * D :], held, sem)
    allowed = [key_segs[piece] == query_seg[...] for piece in range(pieces)]
    step = pl.program_id(0)

    @pl.when(step == 0)
    def _():
        weight.start()
        both_ref[0] = act_first[...]

    wide = query.shape[1]
    for block in range(wide // PAIR):
        cols = slice(block * PAIR, (block + 1) * PAIR)
        query_block = query[:, cols]
        key_blocks = [pair[0, :, cols] for pair in pairs]
        value_blocks = [pair[1, :, cols] for pair in pairs]
        mixed = None
        for head in range(2):
            mask = head_mask(query_block.shape, head)
            one_query = jnp.where(mask, query_block, jnp.zeros_like(query_block))
            scores = [
                jnp.where(a, dot_cols(key, one_query), NEG_BIG)
                for key, a in zip(key_blocks, allowed)
            ]
            peak = functools.reduce(jnp.maximum, [jnp.max(s, 0, keepdims=True) for s in scores])
            expo = [jnp.exp(s - peak) for s in scores]
            inverse = 1.0 / functools.reduce(jnp.add, [jnp.sum(e, 0, keepdims=True) for e in expo])
            for piece in range(pieces):
                probs = (expo[piece] * inverse).astype(BF)
                probs_ref[2 * block + head, piece] = probs
                value = value_blocks[piece]
                part = dot_rows(jnp.where(mask, value, jnp.zeros_like(value)), probs)
                mixed = part if mixed is None else mixed + part
        both_ref[1, :, aligned(step * (wide // PAIR) + block, PAIR)] = mixed.T.astype(BF)

    @pl.when(step == pl.num_programs(0) - 1)
    def _():
        weight.wait()
        hidden = hidden_zero[...] + dot(both_ref[1], held[...].reshape(D, D))
        hidden_ref[...] = hidden
        act_ref[...] = (hidden * norm_scale(hidden) * gain[...]).astype(BF)


GELU_ROOT = 0.7978845608028654
GELU_CUBE = 0.044715


def feed_kernel(index, act, cot, w_up, w_down, second_ref, activ_ref, upper_ref):
    cut = 256
    for at in range(w_up.shape[1] // cut):
        cols = slice(at * cut, (at + 1) * cut)
        upper = dot(act[...], w_up[:, cols])
        square = upper * upper
        bent = jnp.tanh(GELU_ROOT * upper * (1.0 + GELU_CUBE * square))
        half = 0.5 * (1.0 + bent)
        activ_ref[:, cols] = (upper * half).astype(BF)
        slope = half + 0.5 * upper * (1.0 - bent * bent) * (
            GELU_ROOT * (1.0 + 3.0 * GELU_CUBE * square)
        )
        upper_ref[:, cols] = (dot_cols(cot[...], w_down[cols, :]) * slope).astype(BF)
    second_ref[...] = dot_cols(upper_ref[...], w_up[...]).astype(BF)


def result_parts_kernel(index, *refs):
    activs, w_down = refs[:CHIPS], refs[CHIPS]
    for activ, out_ref in zip(activs, refs[CHIPS + 1 :]):
        out_ref[...] = dot(activ[...], w_down[...]).astype(BF)


def down_grad_kernel(index, *refs):
    activs, cots = stacked(refs[:CHIPS]), stacked(refs[CHIPS : 2 * CHIPS])
    keep_ref, send_ref = refs[2 * CHIPS :]
    down = [
        dot_rows(activs[:, at * HIDDEN_ROWS : (at + 1) * HIDDEN_ROWS], cots).astype(BF)
        for at in range(2)
    ]
    even = index[4] == 0
    keep_ref[...] = jnp.where(even, down[0], down[1])
    send_ref[...] = jnp.where(even, down[1], down[0])


def up_grad_kernel(index, *refs):
    acts, uppers = stacked(refs[:CHIPS]), stacked(refs[CHIPS : 2 * CHIPS])
    keep_ref, send_ref = refs[2 * CHIPS :]
    even = index[4] == 0
    for chip in range(CHIPS):
        rows = slice(chip * 2 * OWN_ROWS, (chip + 1) * 2 * OWN_ROWS)
        total = dot_rows(acts[:, rows], uppers).astype(BF)
        keep_ref[chip] = jnp.where(even, total[:OWN_ROWS], total[OWN_ROWS:])
        send_ref[chip] = jnp.where(even, total[OWN_ROWS:], total[:OWN_ROWS])


def feed_send_kernel(index, expander, up_ref):
    for chip in range(CHIPS):
        up_ref[chip] = expander[:, chip * D : (chip + 1) * D]


def three_kernel(index, *refs):
    for array, out_ref in zip(refs[:3], refs[3:]):
        out_ref[...] = array[...]


def rest_kernel(index):
    pass


def copy_kernel(index, array, out_ref):
    out_ref[...] = array[...]


def feed_total_kernel(index, down, up, reducer_ref, expander_ref):
    reducer_ref[...] = down[...].astype(F32)
    for chip in range(CHIPS):
        expander_ref[:, chip * D : (chip + 1) * D] = up[chip].astype(F32)


def up_kernel(index, mine, other, out_ref):
    for chip in range(CHIPS):
        out_ref[2 * chip + index[4]] = mine[chip]
        out_ref[2 * chip + 1 - index[4]] = other[chip]


def down_kernel(index, mine, other, out_ref):
    out_ref[index[4]] = mine[...]
    out_ref[1 - index[4]] = other[...]


def attend_back_kernel(pieces, index, *refs):
    query, probs_ref = refs[:2]
    pairs = refs[2 : 2 + pieces]
    at = 2 + pieces
    gathered, hidden_one, cot, gain, cosine, sine = refs[at : at + 6]
    seconds = refs[at + 6 : at + 8]
    at += 8
    one_ref, low_ref, gain_ref, query_ref = refs[at : at + 4]
    pair_refs = refs[at + 4 : at + 4 + pieces]
    held, sem = refs[at + 4 + pieces :]
    swap_ref = pair_refs[1]
    step = pl.program_id(0)
    weight = pltpu.make_async_copy(gathered.at[:, :, 3 * D :], held, sem)

    @pl.when(step == 0)
    def _():
        weight.start()
        back, gain_grad = norm_back(summed(seconds), hidden_one[...], gain[...])
        one = cot[...].astype(F32) + back
        one_ref[...] = one
        gain_ref[...] = gain_grad
        low_ref[...] = one.astype(BF)
        weight.wait()

    wide = query.shape[1]
    swap_ref[3] = low_ref[:, aligned(step, wide)]
    attended_grad = dot_cols(low_ref[...], held.reshape(D, D)[aligned(step, wide), :]).astype(BF)
    for block in range(wide // PAIR):
        cols = slice(block * PAIR, (block + 1) * PAIR)
        query_block = query[:, cols]
        grad_block = attended_grad[:, cols]
        key_blocks = [pair[0, :, cols] for pair in pairs]
        value_blocks = [pair[1, :, cols] for pair in pairs]
        query_grad = None
        key_grads = [None] * pieces
        value_grads = [None] * pieces
        for head in range(2):
            mask = head_mask(query_block.shape, head)
            one_query = jnp.where(mask, query_block, jnp.zeros_like(query_block))
            one_grad = jnp.where(mask, grad_block, jnp.zeros_like(grad_block))
            low = [probs_ref[2 * block + head, piece] for piece in range(pieces)]
            probs = [p.astype(F32) for p in low]
            probs_grad = [dot_cols(value, one_grad) for value in value_blocks]
            delta = functools.reduce(
                jnp.add,
                [jnp.sum(p * g, 0, keepdims=True) for p, g in zip(probs, probs_grad)],
            )
            for piece in range(pieces):
                scores_grad = (probs[piece] * (probs_grad[piece] - delta)).astype(BF)
                key = key_blocks[piece]
                part = dot_rows(jnp.where(mask, key, jnp.zeros_like(key)), scores_grad)
                query_grad = part if query_grad is None else query_grad + part
                key_part = dot(scores_grad, one_query)
                value_part = dot(low[piece], one_grad)
                if head:
                    key_part += key_grads[piece]
                    value_part += value_grads[piece]
                key_grads[piece] = key_part
                value_grads[piece] = value_part
        query_grad = query_grad.T * HEAD_DIM ** (-0.5)
        query_grad = turn(query_grad, cosine[0], -sine[0]).astype(BF)
        query_ref[:, cols] = query_grad
        swap_ref[2, :, cols] = query_grad
        for piece in range(pieces):
            turned = turn(key_grads[piece], cosine[piece], -sine[piece])
            pair_refs[piece][0, :, cols] = turned.astype(BF)
            pair_refs[piece][1, :, cols] = value_grads[piece].astype(BF)


def united_kernel(pieces, index, *refs):
    query_grad, mid = refs[:2]
    pairs = refs[2 : 2 + pieces]
    at = 2 + pieces
    gathered, hidden_zero, one_grad, gain = refs[at : at + 4]
    swap_ref, held, sem = refs[at + 4 :]
    copies = fetch(gathered, 0, held, sem)
    tok = query_grad.shape[0]
    place = lambda which: slice(which * tok, (which + 1) * tok)
    for which in range(2):
        total = functools.reduce(jnp.add, [part[which].astype(F32) for part in pairs])
        swap_ref[place(which)] = total.astype(BF)
    grads = (query_grad[...], swap_ref[place(0)], swap_ref[place(1)])
    grad = None
    for which, copy in enumerate(copies):
        copy.wait()
        part = dot_cols(grads[which], held[which].reshape(D, D))
        grad = part if grad is None else grad + part
    back, gain_grad = norm_back(grad, hidden_zero[...], gain[...])
    swap_ref[place(2)] = (one_grad[...] + back).astype(BF)
    rest = jnp.zeros((GAIN_ROWS - 2, D), F32)
    swap_ref[3 * tok :] = jnp.concatenate([gain_grad, mid[...], rest], 0).astype(BF)


def of_core(ref, index, size):
    return jnp.concatenate(
        [ref[:, aligned(2 * index[chip] + index[4], size)] for chip in range(CHIPS)], 1
    )


def put_slabs(total, rows, at, order, keep_ref, send_ref):
    for ref, chips in ((keep_ref, order[:2]), (send_ref, order[2:])):
        for place, chip in enumerate(chips):
            ref[place, at : at + rows] = total[chip * rows : (chip + 1) * rows].astype(BF)


X_FIRST = (0, 2, 1, 3)
Y_FIRST = (0, 1, 2, 3)


def query_grad_kernel(index, both, both_c, grad, low, swapped, keep_ref, send_ref):
    rights = ((grad[...], swapped[2]), (low[...], swapped[3]))
    for which, right in enumerate(rights):
        left = [of_core(part.at[which], index, OWN_ROWS) for part in (both, both_c)]
        total = dot_rows(jnp.concatenate(left, 0), jnp.concatenate(right, 0))
        put_slabs(total, OWN_ROWS, which * OWN_ROWS, X_FIRST, keep_ref, send_ref)


def pair_grad_kernel(index, both, both_c, own, swapped, keep_ref, send_ref):
    tok = both.shape[1]
    left = jnp.concatenate([of_core(part.at[0], index, OWN_ROWS) for part in (both, both_c)], 0)
    for which in range(2):
        place = slice(which * tok, (which + 1) * tok)
        total = dot_rows(left, jnp.concatenate([own[place], swapped[place]], 0))
        put_slabs(total, OWN_ROWS, which * OWN_ROWS, Y_FIRST, keep_ref, send_ref)


def merge_grad_kernel(index, joined, joined_c, own, swapped, keep_ref, send_ref):
    tok = joined.shape[0]
    both = jnp.concatenate(
        [of_core(part, index, MERGE_ROWS) for part in (joined, joined_c)], 0
    )
    low = slice(2 * tok, 3 * tok)
    total = dot_rows(both, jnp.concatenate([own[low], swapped[low]], 0))
    put_slabs(total, MERGE_ROWS, 0, X_FIRST, keep_ref, send_ref)
    gains = own[3 * tok :].astype(F32) + swapped[3 * tok :].astype(F32)
    keep_ref[:, MERGE_ROWS:] = jnp.zeros((2, GAIN_ROWS, D), BF)
    send_ref[:, MERGE_ROWS:] = jnp.zeros((2, GAIN_ROWS, D), BF)
    for ref, chips in ((keep_ref, X_FIRST[:2]), (send_ref, X_FIRST[2:])):
        for place, chip in enumerate(chips):
            owner = 2 * index[chip] + index[4]
            lane = lax.broadcasted_iota(jnp.int32, gains.shape, 1)
            mine = jnp.where(lane // OWN_ROWS == owner, gains, 0.0)
            chosen = functools.reduce(
                jnp.add,
                [mine[:, at * OWN_ROWS : (at + 1) * OWN_ROWS] for at in range(D // OWN_ROWS)],
            )
            ref[place, MERGE_ROWS:, :OWN_ROWS] = chosen.astype(BF)


def joined_grad_kernel(index, first, second, *refs):
    weights = refs[: 2 * CHIPS]
    rows = first.shape[0]
    low = jnp.concatenate([first[...], second[...]], 0)
    micro = index[5]
    for at, weight in enumerate(weights):
        grad = dot_cols(low, weight[:MERGE_ROWS])
        owner = owner_of(index, at % CHIPS, at >= CHIPS)
        cols = aligned(owner % CHIPS, MERGE_ROWS)
        for half, out_ref in enumerate(refs[2 * CHIPS :]):

            @pl.when(owner // CHIPS == half)
            def _():
                out_ref[micro, :, cols] = grad[:rows]
                out_ref[1 - micro, :, cols] = grad[rows:]


def sum_kernel(index, *refs):
    refs[-1][...] = summed(refs[:-1])


def add_kernel(index, *refs):
    refs[-1][...] = summed(refs[:-1]).astype(BF)


def add_two_kernel(index, keep, got, own_ref, other_ref):
    own_ref[...] = summed((keep.at[0], got.at[0])).astype(BF)
    other_ref[...] = summed((keep.at[1], got.at[1])).astype(BF)


def stack_kernel(index, *refs):
    for at, part in enumerate(refs[:-1]):
        refs[-1][at] = part[...]


def result_kernel(index, *refs):
    left, right = refs[-2:]
    rows = left.shape[0]
    total = summed(refs[:-2])
    left[...] = total[:rows].astype(BF)
    right[...] = total[rows:].astype(BF)


def zero_kernel(index, swapped, left_ref, right_ref):
    rows = left_ref.shape[0]
    left_ref[...] = swapped[4 * rows : 5 * rows]
    right_ref[...] = swapped[5 * rows : 6 * rows]


def by_micro_kernel(index, first, second, out_ref):
    out_ref[index[5]] = first[...]
    out_ref[1 - index[5]] = second[...]


def total_kernel(index, query, merge, pair, merger_ref, projector_ref, combiner_ref, gain_ref):
    merger_ref[...] = merge[:MERGE_ROWS].astype(F32)
    gain_ref[...] = merge[MERGE_ROWS : MERGE_ROWS + 16, :OWN_ROWS].astype(F32)[:8]
    combiner_ref[...] = query[OWN_ROWS:].astype(F32)
    parts = (query[:OWN_ROWS], pair[:OWN_ROWS], pair[OWN_ROWS:])
    for which, part in enumerate(parts):
        projector_ref[:, which * D : (which + 1) * D] = part.astype(F32)


def call(kernel, vmem, grid, in_specs, out_specs, out_shape, scratch, index, token, *arrays):
    scalars = 0 if index is None else 1

    def passing(*refs):
        index_ref, refs = (refs[0], refs[1:]) if scalars else (None, refs)
        inputs = 1 + len(in_specs)
        kernel(index_ref, *refs[1:inputs], *refs[inputs + 1 :])

    anywhere = pl.BlockSpec(memory_space=pl.ANY)
    return pl.pallas_call(
        passing,
        grid_spec=pltpu.PrefetchScalarGridSpec(
            num_scalar_prefetch=scalars,
            grid=grid,
            in_specs=[anywhere] + in_specs,
            out_specs=[anywhere] + out_specs,
            scratch_shapes=scratch,
        ),
        out_shape=[jax.ShapeDtypeStruct(token.shape, token.dtype)] + out_shape,
        input_output_aliases={scalars: 0},
        name=getattr(kernel, "func", kernel).__name__,
        compiler_params=pltpu.CompilerParams(
            dimension_semantics=("arbitrary",) * len(grid), vmem_limit_bytes=vmem
        ),
        cost_estimate=pl.CostEstimate(flops=10**12, bytes_accessed=0, transcendentals=0),
    )(*([index] if scalars else []), token, *arrays)


def shape(*dims, dtype=BF):
    return jax.ShapeDtypeStruct(dims, dtype)


def whole(*dims):
    return pl.BlockSpec(dims, lambda *_: (0,) * len(dims))


def local(
    frames,
    skipped,
    lengths,
    merger,
    projector,
    combiner,
    expander,
    reducer,
    prenorm,
    midnorm,
    cotangent,
):
    rows = frames.shape[1]
    tok = 2 * rows
    blocks = lax.axis_size("blk")
    fsdp = lax.axis_size("fsdp")
    quarter = blocks // 4
    pieces = blocks // 2
    stream = rows * blocks

    me = lax.axis_index("fsdp")
    spot = lax.axis_index("blk")
    core = me % 2
    chip = me // 2
    unit = spot // quarter
    micro = unit // 2
    source_core = unit % 2
    half = (spot % quarter) * 2 + core

    def send(array, route, name="send"):
        pairs = []
        for y, x, c, b in itertools.product(range(2), range(2), range(2), range(blocks)):
            target = route(y, x, c, b)
            if target is not None:
                ty, tx, tc, tb = target
                pairs.append((((y * 2 + x) * 2 + c) * blocks + b, ((ty * 2 + tx) * 2 + tc) * blocks + tb))
        with jax.named_scope(name):
            return lax.ppermute(array, AXES, pairs)

    to_x = lambda y, x, c, b: (y, 1 - x, c, b)
    to_y = lambda y, x, c, b: (1 - y, x, c, b)
    to_diagonal = lambda y, x, c, b: (1 - y, 1 - x, c, b)
    to_core = lambda y, x, c, b: (y, x, 1 - c, b)
    around = (to_x, to_y, to_diagonal)
    over_plane = (to_x, to_diagonal, to_y)

    def holder(micro_at, c, pair):
        return (2 * micro_at + c) * quarter + pair // 2, pair % 2

    def inward(other):
        def route(y, x, c, b):
            tb, tc = holder((b + other) % 2, c, b // 2)
            return (y, x, tc, tb)

        return route

    def outward(other):
        forward = inward(other)
        table = {}
        for y, x, c, b in itertools.product(range(2), range(2), range(2), range(blocks)):
            table[forward(y, x, c, b)] = (y, x, c, b)
        return lambda *at: table[at]

    def among(by):
        def route(y, x, c, b):
            at = ((b % quarter) * 2 + c) ^ by
            return (y, x, at % 2, (b // quarter) * quarter + at // 2)

        return route

    def take_in(pick, name):
        return tuple(send(pick((spot + other) % 2), inward(other), name) for other in range(2))

    gathered = lax.all_gather(jnp.concatenate([projector, combiner], 1), "fsdp", axis=0)

    gain_rows = jnp.pad(jnp.stack([prenorm, midnorm]), ((0, GAIN_ROWS - 2), (0, D - OWN_ROWS)))
    merger_own = jnp.concatenate([merger, gain_rows], 0)
    mergers = [merger_own] + [send(merger_own, route, "merger_around") for route in around]
    mergers += [send(part, to_core, "merger_core") for part in mergers]

    left, right = take_in(
        lambda m: jnp.concatenate([frames[m], skipped[m], cotangent[m]], -1), "tokens_in"
    )
    other_lengths = send(lengths, to_core, "lengths_core")

    mine = jnp.where(source_core == core, lengths, other_lengths)[:, 0]
    row_lengths = jnp.where(micro == 0, mine[0], mine[1])
    ends = jnp.cumsum(row_lengths)
    within = jnp.arange(rows, dtype=jnp.int32)

    def layout(at):
        offsets = jnp.concatenate(
            [(2 * at + micro) * rows + within, (2 * at + 1 - micro) * rows + within]
        )
        before = (ends[None, :] <= offsets[:, None]).astype(jnp.int32)
        return jnp.sum(before, 1), offsets - jnp.sum(before * row_lengths[None, :], 1)

    layouts = [layout(half ^ by) for by in range(pieces)]
    query_seg = layouts[0][0][None]
    key_segs = jnp.stack([segment for segment, _ in layouts])[:, :, None]
    inverse = 10000.0 ** (-jnp.arange(HEAD_DIM // 2, dtype=F32) * 2.0 / HEAD_DIM)
    positions = jnp.stack([position for _, position in layouts]).astype(F32)
    angles = positions[:, :, None] * inverse
    cosine = jnp.tile(jnp.cos(angles), (1, 1, 4))
    sine = jnp.sin(angles)
    sine = jnp.concatenate([-sine, sine, -sine, sine], -1)

    index = jnp.stack(
        [chip, chip ^ 1, chip ^ 2, chip ^ 3, core, spot % 2, spot, spot]
    ).astype(jnp.int32)
    last_token = [jnp.zeros((8, 128), F32)]

    def run(
        kernel, grid, in_specs, out_specs, out_shape, scratch, *arrays, vmem=SMALL, scalars=index
    ):
        last_token[0], *results = call(
            kernel,
            vmem,
            (grid,) if grid else (),
            in_specs,
            out_specs,
            out_shape,
            scratch,
            scalars,
            last_token[0],
            *arrays,
        )
        return results[0] if len(results) == 1 else results

    def rest():
        run(rest_kernel, 0, [], [], [], [], scalars=None)

    def meet():
        last_token[0] = send(last_token[0], to_core, "order")

    def simple(kernel, outs, *arrays, scalars=index):
        held = pl.BlockSpec(memory_space=pltpu.VMEM)
        return run(
            kernel,
            0,
            [held] * len(arrays),
            [held] * len(outs),
            outs,
            [],
            *arrays,
            scalars=scalars,
        )

    def add(*arrays):
        return simple(add_kernel, [shape(*arrays[0].shape)], *arrays, scalars=None)

    def first_step(keep, got):
        return simple(add_two_kernel, [shape(*keep.shape[1:])] * 2, keep, got, scalars=None)

    wide = 2 * OWN_ROWS
    cols_at = lambda height, width: pl.BlockSpec((height, width), lambda s, *_: (0, s))
    cols_of = lambda height, width: pl.BlockSpec((height, width), lambda s, i: (0, i[s]))
    table = whole(tok, PAIR)
    tables = whole(pieces, tok, PAIR)

    down_c = send(reducer, to_core, "w_down_core")
    chunk = expander.shape[1] // CHIPS
    w_down = simple(down_kernel, [shape(2, HIDDEN_ROWS, D)], reducer, down_c).reshape(chunk, D)
    hidden_zero, cot, joined, gain_pre, gain_mid = simple(
        merge_kernel,
        [shape(tok, D, dtype=F32), shape(tok, D), shape(tok, 2 * D)]
        + [shape(1, D, dtype=F32)] * 2,
        left,
        right,
        *mergers,
    )
    joined_c = send(joined, to_core, "joined_core")

    groups = [[c + 2 * at for at in range(CHIPS)] for c in range(2)]
    swap_chunks = lambda parts: lax.all_to_all(
        parts, "fsdp", 0, 0, axis_index_groups=groups, tiled=True
    )
    up_swapped = swap_chunks(
        simple(feed_send_kernel, [shape(CHIPS, OWN_ROWS, chunk)], expander, scalars=None)
    )
    fetched = pl.BlockSpec(memory_space=pltpu.HBM)
    act_first, query, pair, cot_again = run(
        project_kernel,
        1,
        [whole(tok, D), whole(1, D), fetched, table, table, whole(tok, D)],
        [whole(tok, D), whole(tok, D), whole(2, tok, D), whole(tok, D)],
        [shape(tok, D), shape(tok, D), shape(2, tok, D), shape(tok, D)],
        [pltpu.VMEM((3, fsdp, OWN_ROWS, D), BF), pltpu.SemaphoreType.DMA((3,))],
        hidden_zero,
        gain_pre,
        gathered,
        cosine[0],
        sine[0],
        cot,
        vmem=LARGE,
        scalars=None,
    )
    cots = [send(cot_again, route, "cot_around") for route in over_plane]
    up_mine = simple(copy_kernel, [shape(CHIPS, OWN_ROWS, chunk)], up_swapped, scalars=None)
    up_c = send(up_mine, to_core, "w_up_core")
    pairs = [pair] + [send(pair, among(by), "pair_core") for by in range(1, pieces)]
    steps, vmem = (1, LARGE) if pieces == 2 else (CHIPS * 2, HUGE)
    head_cols = cols_at(tok, D // steps)
    pair_cols = lambda count: pl.BlockSpec((count, tok, D // steps), lambda s, *_: (0, 0, s))
    probs_spec = pl.BlockSpec((HEADS // steps, pieces, tok, tok), lambda s, *_: (s, 0, 0, 0))
    combiner_held = [pltpu.VMEM((fsdp, OWN_ROWS, D), BF), pltpu.SemaphoreType.DMA]
    attended, hidden_one, act_second, probs = run(
        functools.partial(attend_kernel, pieces),
        steps,
        [head_cols, whole(1, tok), whole(pieces, tok, 1)]
        + [pair_cols(2)] * pieces
        + [whole(tok, D), fetched, whole(tok, D), whole(1, D)],
        [whole(2, tok, D), whole(tok, D), whole(tok, D), probs_spec],
        [
            shape(2, tok, D),
            shape(tok, D, dtype=F32),
            shape(tok, D),
            shape(HEADS, pieces, tok, tok),
        ],
        combiner_held,
        query,
        query_seg,
        key_segs,
        *pairs,
        act_first,
        gathered,
        hidden_zero,
        gain_mid,
        vmem=vmem,
        scalars=None,
    )
    acts = [act_second] + [send(act_second, route, "act_around") for route in over_plane]
    attended_c = send(attended, to_core, "attended_core")
    w_up = simple(up_kernel, [shape(fsdp, OWN_ROWS, chunk)], up_mine, up_c).reshape(D, chunk)
    cots = [cot] + simple(three_kernel, [shape(tok, D)] * 3, *cots, scalars=None)

    fed = [
        simple(
            feed_kernel,
            [shape(tok, D), shape(tok, chunk), shape(tok, chunk)],
            act,
            grad,
            w_up,
            w_down,
            scalars=None,
        )
        for act, grad in zip(acts, cots)
    ]
    seconds = [fed[0][0]] + [
        send(part[0], route, "second_around") for part, route in zip(fed[1:], over_plane)
    ]
    activs = [part[1] for part in fed]
    down_keep, down_send = simple(
        down_grad_kernel, [shape(HIDDEN_ROWS, D)] * 2, *activs, *cots
    )
    down_got = send(down_send, to_core, "down_core")
    up_keep, up_send = simple(
        up_grad_kernel, [shape(CHIPS, OWN_ROWS, chunk)] * 2, *acts, *[part[2] for part in fed]
    )
    up_got = send(up_send, to_core, "up_core")

    second = simple(
        sum_kernel, [shape(tok, D, dtype=F32)], seconds[0], seconds[1], scalars=None
    )
    second = simple(sum_kernel, [shape(tok, D, dtype=F32)], second, seconds[2], scalars=None)

    steps = CHIPS if pieces == 2 else 2 * CHIPS
    head_cols = cols_at(tok, D // steps)
    pair_cols = lambda count: pl.BlockSpec((count, tok, D // steps), lambda s, *_: (0, 0, s))
    probs_spec = pl.BlockSpec((HEADS // steps, pieces, tok, tok), lambda s, *_: (s, 0, 0, 0))
    counts = [4 if by == 1 else 2 for by in range(pieces)]
    back = run(
        functools.partial(attend_back_kernel, pieces),
        steps,
        [head_cols, probs_spec]
        + [pair_cols(2)] * pieces
        + [fetched, whole(tok, D), whole(tok, D), whole(1, D)]
        + [tables, tables]
        + [whole(tok, D)] * 2,
        [whole(tok, D), whole(tok, D), whole(1, D), head_cols] + [pair_cols(n) for n in counts],
        [
            shape(tok, D, dtype=F32),
            shape(tok, D),
            shape(1, D, dtype=F32),
            shape(tok, D),
        ]
        + [shape(n, tok, D) for n in counts],
        combiner_held,
        query,
        probs,
        *pairs,
        gathered,
        hidden_one,
        cot,
        gain_mid,
        cosine,
        sine,
        second,
        seconds[3],
        vmem=vmem,
        scalars=None,
    )
    one_grad, one_low, mid_grad, query_grad = back[:4]
    pair_grads = [back[4]] + [
        send(part, among(by), "pair_grads_core") for by, part in enumerate(back[5:], 1)
    ]
    reversed_blocks = [list(reversed(range(blocks)))]
    down_total = lax.psum(add(down_keep, down_got), "blk", axis_index_groups=reversed_blocks)
    swapped = run(
        functools.partial(united_kernel, pieces),
        1,
        [whole(tok, D), whole(1, D)]
        + [whole(n, tok, D) for n in counts]
        + [fetched, whole(tok, D), whole(tok, D), whole(1, D)],
        [whole(3 * tok + GAIN_ROWS, D)],
        [shape(3 * tok + GAIN_ROWS, D)],
        [pltpu.VMEM((3, fsdp, OWN_ROWS, D), BF), pltpu.SemaphoreType.DMA((3,))],
        query_grad,
        mid_grad,
        *pair_grads,
        gathered,
        hidden_zero,
        one_grad,
        gain_pre,
        vmem=LARGE if pieces == 2 else HUGE,
        scalars=None,
    )
    swapped_c = send(swapped, to_core, "zero_core")
    up_swapped = swap_chunks(add(up_keep, up_got))

    def slabs_of(kernel, height, *arrays):
        return simple(kernel, [shape(2, height, D)] * 2, *arrays)

    query_keep, query_send = slabs_of(
        query_grad_kernel,
        2 * OWN_ROWS,
        attended,
        attended_c,
        query_grad,
        one_low,
        pair_grads[1],
    )
    query_got = send(query_send, to_x, "query_x")
    merge_keep, merge_send = slabs_of(
        merge_grad_kernel, MERGE_ROWS + GAIN_ROWS, joined, joined_c, swapped, swapped_c
    )
    merge_got = send(merge_send, to_x, "merge_x")
    pair_keep, pair_send = slabs_of(
        pair_grad_kernel, 2 * OWN_ROWS, attended, attended_c, swapped, swapped_c
    )
    pair_got = send(pair_send, to_y, "pair_y")
    other_order = [blocks // 2 + at if at < blocks // 2 else at - blocks // 2 for at in range(blocks)]
    up_total = lax.psum(
        simple(copy_kernel, [shape(CHIPS, OWN_ROWS, chunk)], up_swapped, scalars=None),
        "blk",
        axis_index_groups=[other_order],
    )
    query_own, query_other = first_step(query_keep, query_got)
    query_y = send(query_other, to_y, "query_y")
    merge_own, merge_other = first_step(merge_keep, merge_got)
    merge_y = send(merge_other, to_y, "merge_y")
    pair_own, pair_other = first_step(pair_keep, pair_got)
    pair_x = send(pair_other, to_x, "pair_x")
    query_sum = add(query_own, query_y)
    merge_sum = add(merge_own, merge_y)
    pair_sum = add(pair_own, pair_x)
    sums = lax.psum((query_sum, merge_sum, pair_sum), "blk")
    meet()
    zero_back = [
        send(part, outward(other), "zero_out")
        for other, part in enumerate(
            simple(zero_kernel, [shape(rows, D)] * 2, swapped, scalars=None)
        )
    ]
    result_parts = simple(
        result_parts_kernel, [shape(tok, D)] * CHIPS, *activs, w_down, scalars=None
    )
    result_parts = [result_parts[0]] + [
        send(part, route, "result_around") for part, route in zip(result_parts[1:], over_plane)
    ]
    frames_grad, skipped_grad = simple(
        joined_grad_kernel, [shape(MB, rows, D, dtype=F32)] * 2, *zero_back, *mergers
    )
    rest()
    results = simple(
        result_kernel, [shape(rows, D)] * 2, *result_parts, hidden_one, scalars=None
    )
    results = [send(part, outward(other), "result_out") for other, part in enumerate(results)]
    rest()
    result_out = simple(by_micro_kernel, [shape(MB, rows, D)], *results)
    reducer_grad, expander_grad = simple(
        feed_total_kernel,
        [shape(*reducer.shape, dtype=F32), shape(*expander.shape, dtype=F32)],
        down_total,
        up_total,
        scalars=None,
    )
    merger_grad, projector_grad, combiner_grad, gain_grads = simple(
        total_kernel,
        [
            shape(*merger.shape, dtype=F32),
            shape(*projector.shape, dtype=F32),
            shape(*combiner.shape, dtype=F32),
            shape(8, OWN_ROWS, dtype=F32),
        ],
        *sums,
        scalars=None,
    )
    return (
        result_out,
        frames_grad,
        skipped_grad,
        merger_grad,
        projector_grad,
        combiner_grad,
        expander_grad,
        reducer_grad,
        gain_grads[0],
        gain_grads[1],
    )


def solution(mesh):
    tokens = P(None, ("fsdp", "blk"), None)
    weight = P("fsdp", None)
    gain = P("fsdp")
    return jax.shard_map(
        local,
        mesh=mesh,
        in_specs=(tokens, tokens, P(None, "fsdp", None))
        + (weight,) * 5
        + (gain, gain, tokens),
        out_specs=(tokens, tokens, tokens) + (weight,) * 5 + (gain, gain),
        check_vma=False,
    )
```

```python
import functools
import itertools

import jax
import jax.numpy as jnp
from jax import lax
from jax.experimental import pallas as pl
from jax.experimental.pallas import tpu as pltpu
from jax.sharding import PartitionSpec as P

D = 1024
HEADS = 16
HEAD_DIM = 64
MB = 2
PAIR = 2 * HEAD_DIM
CHIPS = 4
NEG_BIG = -1e30
EPS = 1e-6
AXES = ("fsdp", "blk")
BF = jnp.bfloat16
F32 = jnp.float32
MEGA = 1024 * 1024
SMALL, LARGE, HUGE = 20 * MEGA, 30 * MEGA, 57 * MEGA

MERGE_ROWS = 256
OWN_ROWS = 128
HIDDEN_ROWS = 512
GAIN_ROWS = 16


def dot(left, right):
    return jnp.dot(left, right, preferred_element_type=F32)


def dot_rows(left, right):
    return lax.dot_general(left, right, (((0,), (0,)), ((), ())), preferred_element_type=F32)


def dot_cols(left, right):
    return lax.dot_general(left, right, (((1,), (1,)), ((), ())), preferred_element_type=F32)


def norm_scale(hidden):
    return lax.rsqrt(jnp.mean(hidden * hidden, -1, keepdims=True) + EPS)


def norm_back(grad, hidden, gain):
    scale = norm_scale(hidden)
    weighted = grad * gain
    inner = jnp.mean(weighted * hidden, -1, keepdims=True)
    back = scale * weighted - hidden * (scale * scale * scale * inner)
    gain_grad = jnp.sum(grad * hidden * scale, 0, keepdims=True)
    return back, gain_grad


def swap_halves(tensor):
    lane = lax.broadcasted_iota(jnp.int32, tensor.shape, 1)
    low = (lane % HEAD_DIM) < HEAD_DIM // 2
    return jnp.where(
        low,
        pltpu.roll(tensor, PAIR - HEAD_DIM // 2, 1),
        pltpu.roll(tensor, HEAD_DIM // 2, 1),
    )


def turn(tensor, cosine, sine):
    return tensor * cosine + swap_halves(tensor) * sine


def aligned(at, size):
    return pl.ds(pl.multiple_of(at * size, size), size)


def stacked(parts):
    return jnp.concatenate([part[...] for part in parts], 0)


def summed(parts):
    return functools.reduce(jnp.add, [part[...].astype(F32) for part in parts])


def owner_of(index, chip, other):
    return 2 * index[chip] + (1 - index[4] if other else index[4])


def merge_kernel(index, left, right, *refs):
    weights = refs[: 2 * CHIPS]
    hidden_ref, cot_ref, joined_ref, pre_ref, mid_ref = refs[2 * CHIPS :]
    rows = left.shape[0]
    joined_ref[:rows] = left[:, : 2 * D]
    joined_ref[rows:] = right[:, : 2 * D]
    total = None
    for at, weight in enumerate(weights):
        mine = aligned(owner_of(index, at % CHIPS, at >= CHIPS), MERGE_ROWS)
        part = dot(joined_ref[:, mine], weight[:MERGE_ROWS])
        total = part if total is None else total + part
        mine = aligned(owner_of(index, at % CHIPS, at >= CHIPS), OWN_ROWS)
        gains = weight[MERGE_ROWS:, :OWN_ROWS].astype(F32)
        pre_ref[:, mine] = gains[0:1]
        mid_ref[:, mine] = gains[1:2]
    hidden_ref[...] = total
    cot_ref[:rows] = left[:, 2 * D :]
    cot_ref[rows:] = right[:, 2 * D :]


def fetch(array, at, held, sem):
    copies = [
        pltpu.make_async_copy(
            array.at[:, :, (at + which) * D : (at + which + 1) * D], held.at[which], sem.at[which]
        )
        for which in range(held.shape[0])
    ]
    for copy in copies:
        copy.start()
    return copies


def project_kernel(
    index, hidden, gain, gathered, cosine, sine, cot, act_ref, query_ref, pair_ref, cot_ref, held, sem
):
    copies = fetch(gathered, 0, held, sem)
    cot_ref[...] = cot[...]
    act = (hidden[...] * norm_scale(hidden[...]) * gain[...]).astype(BF)
    act_ref[...] = act
    for which, copy in enumerate(copies):
        copy.wait()
        for part in range(CHIPS):
            wide = slice(part * 2 * PAIR, (part + 1) * 2 * PAIR)
            united = dot(act, held[which, :, :, wide].reshape(D, 2 * PAIR))
            if which == 2:
                pair_ref[1, :, wide] = united.astype(BF)
                continue
            for block in range(2):
                cols = slice(block * PAIR, (block + 1) * PAIR)
                turned = turn(united[:, cols], cosine[...], sine[...]).astype(BF)
                cols = slice((2 * part + block) * PAIR, (2 * part + block + 1) * PAIR)
                if which == 0:
                    query_ref[:, cols] = turned * HEAD_DIM ** (-0.5)
                else:
                    pair_ref[0, :, cols] = turned


def head_mask(shape, head):
    lane = lax.broadcasted_iota(jnp.int32, shape, 1)
    return (lane // HEAD_DIM) == head


def attend_kernel(pieces, index, *refs):
    query, query_seg, key_segs = refs[:3]
    pairs = refs[3 : 3 + pieces]
    act_first, gathered, hidden_zero, gain = refs[3 + pieces : 7 + pieces]
    both_ref, hidden_ref, act_ref, probs_ref, held, sem = refs[7 + pieces :]
    weight = pltpu.make_async_copy(gathered.at[:, :, 3 * D :], held, sem)
    allowed = [key_segs[piece] == query_seg[...] for piece in range(pieces)]
    step = pl.program_id(0)

    @pl.when(step == 0)
    def _():
        weight.start()
        both_ref[0] = act_first[...]

    wide = query.shape[1]
    for block in range(wide // PAIR):
        cols = slice(block * PAIR, (block + 1) * PAIR)
        query_block = query[:, cols]
        key_blocks = [pair[0, :, cols] for pair in pairs]
        value_blocks = [pair[1, :, cols] for pair in pairs]
        mixed = None
        for head in range(2):
            mask = head_mask(query_block.shape, head)
            one_query = jnp.where(mask, query_block, jnp.zeros_like(query_block))
            scores = [
                jnp.where(a, dot_cols(key, one_query), NEG_BIG)
                for key, a in zip(key_blocks, allowed)
            ]
            peak = functools.reduce(jnp.maximum, [jnp.max(s, 0, keepdims=True) for s in scores])
            expo = [jnp.exp(s - peak) for s in scores]
            inverse = 1.0 / functools.reduce(jnp.add, [jnp.sum(e, 0, keepdims=True) for e in expo])
            for piece in range(pieces):
                probs = (expo[piece] * inverse).astype(BF)
                probs_ref[2 * block + head, piece] = probs
                value = value_blocks[piece]
                part = dot_rows(jnp.where(mask, value, jnp.zeros_like(value)), probs)
                mixed = part if mixed is None else mixed + part
        both_ref[1, :, aligned(step * (wide // PAIR) + block, PAIR)] = mixed.T.astype(BF)

    @pl.when(step == pl.num_programs(0) - 1)
    def _():
        weight.wait()
        hidden = hidden_zero[...] + dot(both_ref[1], held[...].reshape(D, D))
        hidden_ref[...] = hidden
        act_ref[...] = (hidden * norm_scale(hidden) * gain[...]).astype(BF)


GELU_ROOT = 0.7978845608028654
GELU_CUBE = 0.044715


def feed_kernel(index, act, cot, w_up, w_down, second_ref, activ_ref, upper_ref):
    cut = 256
    for at in range(w_up.shape[1] // cut):
        cols = slice(at * cut, (at + 1) * cut)
        upper = dot(act[...], w_up[:, cols])
        square = upper * upper
        bent = jnp.tanh(GELU_ROOT * upper * (1.0 + GELU_CUBE * square))
        half = 0.5 * (1.0 + bent)
        activ_ref[:, cols] = (upper * half).astype(BF)
        slope = half + 0.5 * upper * (1.0 - bent * bent) * (
            GELU_ROOT * (1.0 + 3.0 * GELU_CUBE * square)
        )
        upper_ref[:, cols] = (dot_cols(cot[...], w_down[cols, :]) * slope).astype(BF)
    second_ref[...] = dot_cols(upper_ref[...], w_up[...]).astype(BF)


def result_parts_kernel(index, *refs):
    activs, w_down, out_ref = refs[:CHIPS], refs[CHIPS], refs[CHIPS + 1]
    for activ, distance in zip(activs, (0, 1, 3, 2)):
        out_ref[index[distance]] = dot(activ[...], w_down[...]).astype(BF)


def down_grad_kernel(index, *refs):
    activs, cots = stacked(refs[:CHIPS]), stacked(refs[CHIPS : 2 * CHIPS])
    out_ref = refs[2 * CHIPS]
    for core in range(2):
        cols = slice(core * HIDDEN_ROWS, (core + 1) * HIDDEN_ROWS)
        out_ref[core] = dot_rows(activs[:, cols], cots).astype(BF)


def halves_kernel(index, got, out_ref):
    out_ref[...] = summed((got.at[0], got.at[1])).astype(BF)


def up_grad_kernel(index, *refs):
    acts, uppers = stacked(refs[:CHIPS]), stacked(refs[CHIPS : 2 * CHIPS])
    keep_ref, send_ref = refs[2 * CHIPS :]
    even = index[4] == 0
    for chip in range(CHIPS):
        rows = slice(chip * 2 * OWN_ROWS, (chip + 1) * 2 * OWN_ROWS)
        total = dot_rows(acts[:, rows], uppers).astype(BF)
        keep_ref[chip] = jnp.where(even, total[:OWN_ROWS], total[OWN_ROWS:])
        send_ref[chip] = jnp.where(even, total[OWN_ROWS:], total[:OWN_ROWS])


def feed_send_kernel(index, expander, up_ref):
    for chip in range(CHIPS):
        up_ref[chip] = expander[:, chip * D : (chip + 1) * D]


def three_kernel(index, *refs):
    for array, out_ref in zip(refs[:3], refs[3:]):
        out_ref[...] = array[...]


def rest_kernel(index):
    pass


def copy_kernel(index, array, out_ref):
    out_ref[...] = array[...]


def feed_total_kernel(index, down, up, reducer_ref, expander_ref):
    reducer_ref[...] = down[...].astype(F32)
    for chip in range(CHIPS):
        expander_ref[:, chip * D : (chip + 1) * D] = up[chip].astype(F32)


def up_kernel(index, mine, other, out_ref):
    for chip in range(CHIPS):
        out_ref[2 * chip + index[4]] = mine[chip]
        out_ref[2 * chip + 1 - index[4]] = other[chip]


def down_kernel(index, mine, other, out_ref):
    out_ref[index[4]] = mine[...]
    out_ref[1 - index[4]] = other[...]


def attend_back_kernel(pieces, index, *refs):
    query, probs_ref = refs[:2]
    pairs = refs[2 : 2 + pieces]
    at = 2 + pieces
    gathered, hidden_one, cot, gain, cosine, sine = refs[at : at + 6]
    seconds = refs[at + 6 : at + 8]
    at += 8
    one_ref, low_ref, gain_ref, query_ref = refs[at : at + 4]
    pair_refs = refs[at + 4 : at + 4 + pieces]
    held, sem = refs[at + 4 + pieces :]
    swap_ref = pair_refs[1]
    step = pl.program_id(0)
    weight = pltpu.make_async_copy(gathered.at[:, :, 3 * D :], held, sem)

    @pl.when(step == 0)
    def _():
        weight.start()
        back, gain_grad = norm_back(summed(seconds), hidden_one[...], gain[...])
        one = cot[...].astype(F32) + back
        one_ref[...] = one
        gain_ref[...] = gain_grad
        low_ref[...] = one.astype(BF)
        weight.wait()

    wide = query.shape[1]
    swap_ref[3] = low_ref[:, aligned(step, wide)]
    attended_grad = dot_cols(low_ref[...], held.reshape(D, D)[aligned(step, wide), :]).astype(BF)
    for block in range(wide // PAIR):
        cols = slice(block * PAIR, (block + 1) * PAIR)
        query_block = query[:, cols]
        grad_block = attended_grad[:, cols]
        key_blocks = [pair[0, :, cols] for pair in pairs]
        value_blocks = [pair[1, :, cols] for pair in pairs]
        query_grad = None
        key_grads = [None] * pieces
        value_grads = [None] * pieces
        for head in range(2):
            mask = head_mask(query_block.shape, head)
            one_query = jnp.where(mask, query_block, jnp.zeros_like(query_block))
            one_grad = jnp.where(mask, grad_block, jnp.zeros_like(grad_block))
            low = [probs_ref[2 * block + head, piece] for piece in range(pieces)]
            probs = [p.astype(F32) for p in low]
            probs_grad = [dot_cols(value, one_grad) for value in value_blocks]
            delta = functools.reduce(
                jnp.add,
                [jnp.sum(p * g, 0, keepdims=True) for p, g in zip(probs, probs_grad)],
            )
            for piece in range(pieces):
                scores_grad = (probs[piece] * (probs_grad[piece] - delta)).astype(BF)
                key = key_blocks[piece]
                part = dot_rows(jnp.where(mask, key, jnp.zeros_like(key)), scores_grad)
                query_grad = part if query_grad is None else query_grad + part
                key_part = dot(scores_grad, one_query)
                value_part = dot(low[piece], one_grad)
                if head:
                    key_part += key_grads[piece]
                    value_part += value_grads[piece]
                key_grads[piece] = key_part
                value_grads[piece] = value_part
        query_grad = query_grad.T * HEAD_DIM ** (-0.5)
        query_grad = turn(query_grad, cosine[0], -sine[0]).astype(BF)
        query_ref[:, cols] = query_grad
        swap_ref[2, :, cols] = query_grad
        for piece in range(pieces):
            turned = turn(key_grads[piece], cosine[piece], -sine[piece])
            pair_refs[piece][0, :, cols] = turned.astype(BF)
            pair_refs[piece][1, :, cols] = value_grads[piece].astype(BF)


def united_kernel(pieces, index, *refs):
    query_grad, mid = refs[:2]
    pairs = refs[2 : 2 + pieces]
    at = 2 + pieces
    gathered, hidden_zero, one_grad, gain = refs[at : at + 4]
    swap_ref, held, sem = refs[at + 4 :]
    copies = fetch(gathered, 0, held, sem)
    tok = query_grad.shape[0]
    place = lambda which: slice(which * tok, (which + 1) * tok)
    for which in range(2):
        total = functools.reduce(jnp.add, [part[which].astype(F32) for part in pairs])
        swap_ref[place(which)] = total.astype(BF)
    grads = (query_grad[...], swap_ref[place(0)], swap_ref[place(1)])
    grad = None
    for which, copy in enumerate(copies):
        copy.wait()
        part = dot_cols(grads[which], held[which].reshape(D, D))
        grad = part if grad is None else grad + part
    back, gain_grad = norm_back(grad, hidden_zero[...], gain[...])
    swap_ref[place(2)] = (one_grad[...] + back).astype(BF)
    rest = jnp.zeros((GAIN_ROWS - 2, D), F32)
    swap_ref[3 * tok :] = jnp.concatenate([gain_grad, mid[...], rest], 0).astype(BF)


def of_core(ref, index, size):
    return jnp.concatenate(
        [ref[:, aligned(2 * index[chip] + index[4], size)] for chip in range(CHIPS)], 1
    )


def put_slabs(total, rows, at, order, keep_ref, send_ref):
    for ref, chips in ((keep_ref, order[:2]), (send_ref, order[2:])):
        for place, chip in enumerate(chips):
            ref[place, at : at + rows] = total[chip * rows : (chip + 1) * rows].astype(BF)


X_FIRST = (0, 2, 1, 3)
Y_FIRST = (0, 1, 2, 3)


def query_grad_kernel(index, both, both_c, grad, low, swapped, keep_ref, send_ref):
    rights = ((grad[...], swapped[2]), (low[...], swapped[3]))
    for which, right in enumerate(rights):
        left = [of_core(part.at[which], index, OWN_ROWS) for part in (both, both_c)]
        total = dot_rows(jnp.concatenate(left, 0), jnp.concatenate(right, 0))
        put_slabs(total, OWN_ROWS, which * OWN_ROWS, X_FIRST, keep_ref, send_ref)


def pair_grad_kernel(index, both, both_c, own, swapped, keep_ref, send_ref):
    tok = both.shape[1]
    left = jnp.concatenate([of_core(part.at[0], index, OWN_ROWS) for part in (both, both_c)], 0)
    for which in range(2):
        place = slice(which * tok, (which + 1) * tok)
        total = dot_rows(left, jnp.concatenate([own[place], swapped[place]], 0))
        put_slabs(total, OWN_ROWS, which * OWN_ROWS, Y_FIRST, keep_ref, send_ref)


def merge_grad_kernel(index, joined, joined_c, own, swapped, keep_ref, send_ref):
    tok = joined.shape[0]
    both = jnp.concatenate(
        [of_core(part, index, MERGE_ROWS) for part in (joined, joined_c)], 0
    )
    low = slice(2 * tok, 3 * tok)
    total = dot_rows(both, jnp.concatenate([own[low], swapped[low]], 0))
    put_slabs(total, MERGE_ROWS, 0, X_FIRST, keep_ref, send_ref)
    gains = own[3 * tok :].astype(F32) + swapped[3 * tok :].astype(F32)
    keep_ref[:, MERGE_ROWS:] = jnp.zeros((2, GAIN_ROWS, D), BF)
    send_ref[:, MERGE_ROWS:] = jnp.zeros((2, GAIN_ROWS, D), BF)
    for ref, chips in ((keep_ref, X_FIRST[:2]), (send_ref, X_FIRST[2:])):
        for place, chip in enumerate(chips):
            owner = 2 * index[chip] + index[4]
            lane = lax.broadcasted_iota(jnp.int32, gains.shape, 1)
            mine = jnp.where(lane // OWN_ROWS == owner, gains, 0.0)
            chosen = functools.reduce(
                jnp.add,
                [mine[:, at * OWN_ROWS : (at + 1) * OWN_ROWS] for at in range(D // OWN_ROWS)],
            )
            ref[place, MERGE_ROWS:, :OWN_ROWS] = chosen.astype(BF)


def joined_grad_kernel(index, first, second, *refs):
    weights = refs[: 2 * CHIPS]
    rows = first.shape[0]
    low = jnp.concatenate([first[...], second[...]], 0)
    micro = index[5]
    for at, weight in enumerate(weights):
        grad = dot_cols(low, weight[:MERGE_ROWS])
        owner = owner_of(index, at % CHIPS, at >= CHIPS)
        cols = aligned(owner % CHIPS, MERGE_ROWS)
        for half, out_ref in enumerate(refs[2 * CHIPS :]):

            @pl.when(owner // CHIPS == half)
            def _():
                out_ref[micro, :, cols] = grad[:rows]
                out_ref[1 - micro, :, cols] = grad[rows:]


def sum_kernel(index, *refs):
    refs[-1][...] = summed(refs[:-1])


def add_kernel(index, *refs):
    refs[-1][...] = summed(refs[:-1]).astype(BF)


def add_two_kernel(index, keep, got, own_ref, other_ref):
    own_ref[...] = summed((keep.at[0], got.at[0])).astype(BF)
    other_ref[...] = summed((keep.at[1], got.at[1])).astype(BF)


def stack_kernel(index, *refs):
    for at, part in enumerate(refs[:-1]):
        refs[-1][at] = part[...]


def result_kernel(index, *refs):
    left, right = refs[-2:]
    rows = left.shape[0]
    total = summed(refs[:-2])
    left[...] = total[:rows].astype(BF)
    right[...] = total[rows:].astype(BF)


def zero_kernel(index, swapped, left_ref, right_ref):
    rows = left_ref.shape[0]
    left_ref[...] = swapped[4 * rows : 5 * rows]
    right_ref[...] = swapped[5 * rows : 6 * rows]


def by_micro_kernel(index, first, second, out_ref):
    out_ref[index[5]] = first[...]
    out_ref[1 - index[5]] = second[...]


def chosen(index, array, got, ends):
    here = functools.reduce(jnp.logical_or, [index[6] == end for end in ends])
    return jnp.where(here, got[...], array[...])


def choose_kernel(ends, index, array, got, out_ref):
    out_ref[...] = chosen(index, array, got, ends)


def query_total_kernel(ends, index, array, got, query_ref, combiner_ref):
    total = chosen(index, array, got, ends).astype(F32)
    query_ref[...] = total[:OWN_ROWS]
    combiner_ref[...] = total[OWN_ROWS:]


def pair_total_kernel(ends, index, array, got, query, out_ref):
    total = chosen(index, array, got, ends).astype(F32)
    out_ref[:, :D] = query[...]
    out_ref[:, D : 2 * D] = total[:OWN_ROWS]
    out_ref[:, 2 * D :] = total[OWN_ROWS:]


def merge_total_kernel(ends, index, array, got, out_ref, gain_ref):
    total = chosen(index, array, got, ends).astype(F32)
    out_ref[...] = total[:MERGE_ROWS]
    gain_ref[...] = total[MERGE_ROWS : MERGE_ROWS + 8, :OWN_ROWS]


def call(kernel, vmem, grid, in_specs, out_specs, out_shape, scratch, index, token, *arrays):
    scalars = 0 if index is None else 1

    def passing(*refs):
        index_ref, refs = (refs[0], refs[1:]) if scalars else (None, refs)
        inputs = 1 + len(in_specs)
        kernel(index_ref, *refs[1:inputs], *refs[inputs + 1 :])

    anywhere = pl.BlockSpec(memory_space=pl.ANY)
    return pl.pallas_call(
        passing,
        grid_spec=pltpu.PrefetchScalarGridSpec(
            num_scalar_prefetch=scalars,
            grid=grid,
            in_specs=[anywhere] + in_specs,
            out_specs=[anywhere] + out_specs,
            scratch_shapes=scratch,
        ),
        out_shape=[jax.ShapeDtypeStruct(token.shape, token.dtype)] + out_shape,
        input_output_aliases={scalars: 0},
        name=getattr(kernel, "func", kernel).__name__,
        compiler_params=pltpu.CompilerParams(
            dimension_semantics=("arbitrary",) * len(grid), vmem_limit_bytes=vmem
        ),
        cost_estimate=pl.CostEstimate(flops=10**12, bytes_accessed=0, transcendentals=0),
    )(*([index] if scalars else []), token, *arrays)


def shape(*dims, dtype=BF):
    return jax.ShapeDtypeStruct(dims, dtype)


def whole(*dims):
    return pl.BlockSpec(dims, lambda *_: (0,) * len(dims))


def local(
    frames,
    skipped,
    lengths,
    merger,
    projector,
    combiner,
    expander,
    reducer,
    prenorm,
    midnorm,
    cotangent,
):
    rows = frames.shape[1]
    tok = 2 * rows
    blocks = lax.axis_size("blk")
    fsdp = lax.axis_size("fsdp")
    quarter = blocks // 4
    pieces = blocks // 2
    stream = rows * blocks

    me = lax.axis_index("fsdp")
    spot = lax.axis_index("blk")
    core = me % 2
    chip = me // 2
    unit = spot // quarter
    micro = unit // 2
    source_core = unit % 2
    half = (spot % quarter) * 2 + core

    def send(array, route, name="send"):
        pairs = []
        for y, x, c, b in itertools.product(range(2), range(2), range(2), range(blocks)):
            target = route(y, x, c, b)
            if target is not None:
                ty, tx, tc, tb = target
                pairs.append((((y * 2 + x) * 2 + c) * blocks + b, ((ty * 2 + tx) * 2 + tc) * blocks + tb))
        with jax.named_scope(name):
            return lax.ppermute(array, AXES, pairs)

    to_x = lambda y, x, c, b: (y, 1 - x, c, b)
    to_y = lambda y, x, c, b: (1 - y, x, c, b)
    to_diagonal = lambda y, x, c, b: (1 - y, 1 - x, c, b)
    to_core = lambda y, x, c, b: (y, x, 1 - c, b)
    around = (to_x, to_y, to_diagonal)
    over_plane = (to_x, to_diagonal, to_y)

    def holder(micro_at, c, pair):
        return (2 * micro_at + c) * quarter + pair // 2, pair % 2

    def inward(other):
        def route(y, x, c, b):
            tb, tc = holder((b + other) % 2, c, b // 2)
            return (y, x, tc, tb)

        return route

    def outward(other):
        forward = inward(other)
        table = {}
        for y, x, c, b in itertools.product(range(2), range(2), range(2), range(blocks)):
            table[forward(y, x, c, b)] = (y, x, c, b)
        return lambda *at: table[at]

    def among(by):
        def route(y, x, c, b):
            at = ((b % quarter) * 2 + c) ^ by
            return (y, x, at % 2, (b // quarter) * quarter + at // 2)

        return route

    def take_in(pick, name):
        return tuple(send(pick((spot + other) % 2), inward(other), name) for other in range(2))

    def sum_blocks(array, name, last):
        middle = blocks // 2
        plans = [{step: step + 1, blocks - 1 - step: blocks - 2 - step} for step in range(middle - 1)]
        plans.append({middle - 1: middle, middle: middle - 1})
        for moves in plans:
            got = send(array, lambda y, x, c, b: (y, x, c, moves[b]) if b in moves else None, name)
            yield
            array = add(array, got)
        for step in range(middle - 1):
            moves = {middle - 1 - step: middle - 2 - step, middle + step: middle + 1 + step}
            got = send(array, lambda y, x, c, b: (y, x, c, moves[b]) if b in moves else None, name)
            yield
            ends = tuple(moves.values())
            if step == middle - 2:
                array = last(ends, array, got)
            else:
                choose = functools.partial(choose_kernel, ends)
                array = simple(choose, [shape(*array.shape)], array, got)
        yield array

    def finish(steps):
        array = None
        while array is None:
            array = next(steps)
        return array

    gathered = lax.all_gather(jnp.concatenate([projector, combiner], 1), "fsdp", axis=0)

    gain_rows = jnp.pad(jnp.stack([prenorm, midnorm]), ((0, GAIN_ROWS - 2), (0, D - OWN_ROWS)))
    merger_own = jnp.concatenate([merger, gain_rows], 0)
    mergers = [merger_own] + [send(merger_own, route, "merger_around") for route in around]
    mergers += [send(part, to_core, "merger_core") for part in mergers]

    left, right = take_in(
        lambda m: jnp.concatenate([frames[m], skipped[m], cotangent[m]], -1), "tokens_in"
    )
    other_lengths = send(lengths, to_core, "lengths_core")

    mine = jnp.where(source_core == core, lengths, other_lengths)[:, 0]
    row_lengths = jnp.where(micro == 0, mine[0], mine[1])
    ends = jnp.cumsum(row_lengths)
    within = jnp.arange(rows, dtype=jnp.int32)

    def layout(at):
        offsets = jnp.concatenate(
            [(2 * at + micro) * rows + within, (2 * at + 1 - micro) * rows + within]
        )
        before = (ends[None, :] <= offsets[:, None]).astype(jnp.int32)
        return jnp.sum(before, 1), offsets - jnp.sum(before * row_lengths[None, :], 1)

    layouts = [layout(half ^ by) for by in range(pieces)]
    query_seg = layouts[0][0][None]
    key_segs = jnp.stack([segment for segment, _ in layouts])[:, :, None]
    inverse = 10000.0 ** (-jnp.arange(HEAD_DIM // 2, dtype=F32) * 2.0 / HEAD_DIM)
    positions = jnp.stack([position for _, position in layouts]).astype(F32)
    angles = positions[:, :, None] * inverse
    cosine = jnp.tile(jnp.cos(angles), (1, 1, 4))
    sine = jnp.sin(angles)
    sine = jnp.concatenate([-sine, sine, -sine, sine], -1)

    index = jnp.stack(
        [chip, chip ^ 1, chip ^ 2, chip ^ 3, core, spot % 2, spot, spot]
    ).astype(jnp.int32)
    last_token = [jnp.zeros((8, 128), F32)]

    def run(
        kernel, grid, in_specs, out_specs, out_shape, scratch, *arrays, vmem=SMALL, scalars=index
    ):
        last_token[0], *results = call(
            kernel,
            vmem,
            (grid,) if grid else (),
            in_specs,
            out_specs,
            out_shape,
            scratch,
            scalars,
            last_token[0],
            *arrays,
        )
        return results[0] if len(results) == 1 else results

    def rest():
        run(rest_kernel, 0, [], [], [], [], scalars=None)

    def meet():
        last_token[0] = send(last_token[0], to_core, "order")

    def simple(kernel, outs, *arrays, scalars=index):
        held = pl.BlockSpec(memory_space=pltpu.VMEM)
        return run(
            kernel,
            0,
            [held] * len(arrays),
            [held] * len(outs),
            outs,
            [],
            *arrays,
            scalars=scalars,
        )

    def to_total(kernel, outs):
        return lambda ends, array, got: simple(functools.partial(kernel, ends), outs, array, got)

    def add(*arrays):
        return simple(add_kernel, [shape(*arrays[0].shape)], *arrays, scalars=None)

    def first_step(keep, got):
        return simple(add_two_kernel, [shape(*keep.shape[1:])] * 2, keep, got, scalars=None)

    wide = 2 * OWN_ROWS
    cols_at = lambda height, width: pl.BlockSpec((height, width), lambda s, *_: (0, s))
    cols_of = lambda height, width: pl.BlockSpec((height, width), lambda s, i: (0, i[s]))
    table = whole(tok, PAIR)
    tables = whole(pieces, tok, PAIR)

    down_c = send(reducer, to_core, "w_down_core")
    chunk = expander.shape[1] // CHIPS
    w_down = simple(down_kernel, [shape(2, HIDDEN_ROWS, D)], reducer, down_c).reshape(chunk, D)
    hidden_zero, cot, joined, gain_pre, gain_mid = simple(
        merge_kernel,
        [shape(tok, D, dtype=F32), shape(tok, D), shape(tok, 2 * D)]
        + [shape(1, D, dtype=F32)] * 2,
        left,
        right,
        *mergers,
    )
    joined_c = send(joined, to_core, "joined_core")

    groups = [[c + 2 * at for at in range(CHIPS)] for c in range(2)]
    swap_chunks = lambda parts: lax.all_to_all(
        parts, "fsdp", 0, 0, axis_index_groups=groups, tiled=True
    )
    up_swapped = swap_chunks(
        simple(feed_send_kernel, [shape(CHIPS, OWN_ROWS, chunk)], expander, scalars=None)
    )
    fetched = pl.BlockSpec(memory_space=pltpu.HBM)
    act_first, query, pair, cot_again = run(
        project_kernel,
        1,
        [whole(tok, D), whole(1, D), fetched, table, table, whole(tok, D)],
        [whole(tok, D), whole(tok, D), whole(2, tok, D), whole(tok, D)],
        [shape(tok, D), shape(tok, D), shape(2, tok, D), shape(tok, D)],
        [pltpu.VMEM((3, fsdp, OWN_ROWS, D), BF), pltpu.SemaphoreType.DMA((3,))],
        hidden_zero,
        gain_pre,
        gathered,
        cosine[0],
        sine[0],
        cot,
        vmem=LARGE,
        scalars=None,
    )
    cots = [send(cot_again, route, "cot_around") for route in over_plane]
    up_mine = simple(copy_kernel, [shape(CHIPS, OWN_ROWS, chunk)], up_swapped, scalars=None)
    up_c = send(up_mine, to_core, "w_up_core")
    pairs = [pair] + [send(pair, among(by), "pair_core") for by in range(1, pieces)]
    steps, vmem = (1, LARGE) if pieces == 2 else (CHIPS * 2, HUGE)
    head_cols = cols_at(tok, D // steps)
    pair_cols = lambda count: pl.BlockSpec((count, tok, D // steps), lambda s, *_: (0, 0, s))
    probs_spec = pl.BlockSpec((HEADS // steps, pieces, tok, tok), lambda s, *_: (s, 0, 0, 0))
    combiner_held = [pltpu.VMEM((fsdp, OWN_ROWS, D), BF), pltpu.SemaphoreType.DMA]
    attended, hidden_one, act_second, probs = run(
        functools.partial(attend_kernel, pieces),
        steps,
        [head_cols, whole(1, tok), whole(pieces, tok, 1)]
        + [pair_cols(2)] * pieces
        + [whole(tok, D), fetched, whole(tok, D), whole(1, D)],
        [whole(2, tok, D), whole(tok, D), whole(tok, D), probs_spec],
        [
            shape(2, tok, D),
            shape(tok, D, dtype=F32),
            shape(tok, D),
            shape(HEADS, pieces, tok, tok),
        ],
        combiner_held,
        query,
        query_seg,
        key_segs,
        *pairs,
        act_first,
        gathered,
        hidden_zero,
        gain_mid,
        vmem=vmem,
        scalars=None,
    )
    acts = [act_second] + [send(act_second, route, "act_around") for route in over_plane]
    attended_c = send(attended, to_core, "attended_core")
    w_up = simple(up_kernel, [shape(fsdp, OWN_ROWS, chunk)], up_mine, up_c).reshape(D, chunk)
    cots = [cot] + simple(three_kernel, [shape(tok, D)] * 3, *cots, scalars=None)

    fed = [
        simple(
            feed_kernel,
            [shape(tok, D), shape(tok, chunk), shape(tok, chunk)],
            act,
            grad,
            w_up,
            w_down,
            scalars=None,
        )
        for act, grad in zip(acts, cots)
    ]
    seconds = [fed[0][0]] + [
        send(part[0], route, "second_around") for part, route in zip(fed[1:], over_plane)
    ]
    activs = [part[1] for part in fed]
    down_parts = simple(
        down_grad_kernel, [shape(2, HIDDEN_ROWS, D)], *activs, *cots, scalars=None
    )
    core_groups = [[at, at + 1] for at in range(0, fsdp, 2)]
    down_halves = lax.all_to_all(
        down_parts, "fsdp", 0, 0, axis_index_groups=core_groups, tiled=True
    )
    up_keep, up_send = simple(
        up_grad_kernel, [shape(CHIPS, OWN_ROWS, chunk)] * 2, *acts, *[part[2] for part in fed]
    )
    up_got = send(up_send, to_core, "up_core")

    second = simple(
        sum_kernel, [shape(tok, D, dtype=F32)], seconds[0], seconds[1], scalars=None
    )
    second = simple(sum_kernel, [shape(tok, D, dtype=F32)], second, seconds[2], scalars=None)

    reversed_blocks = [list(reversed(range(blocks)))]
    down_total = lax.psum(
        simple(halves_kernel, [shape(HIDDEN_ROWS, D)], down_halves, scalars=None),
        "blk",
        axis_index_groups=reversed_blocks,
    )
    meet()

    steps = CHIPS if pieces == 2 else 2 * CHIPS
    head_cols = cols_at(tok, D // steps)
    pair_cols = lambda count: pl.BlockSpec((count, tok, D // steps), lambda s, *_: (0, 0, s))
    probs_spec = pl.BlockSpec((HEADS // steps, pieces, tok, tok), lambda s, *_: (s, 0, 0, 0))
    counts = [4 if by == 1 else 2 for by in range(pieces)]
    back = run(
        functools.partial(attend_back_kernel, pieces),
        steps,
        [head_cols, probs_spec]
        + [pair_cols(2)] * pieces
        + [fetched, whole(tok, D), whole(tok, D), whole(1, D)]
        + [tables, tables]
        + [whole(tok, D)] * 2,
        [whole(tok, D), whole(tok, D), whole(1, D), head_cols] + [pair_cols(n) for n in counts],
        [
            shape(tok, D, dtype=F32),
            shape(tok, D),
            shape(1, D, dtype=F32),
            shape(tok, D),
        ]
        + [shape(n, tok, D) for n in counts],
        combiner_held,
        query,
        probs,
        *pairs,
        gathered,
        hidden_one,
        cot,
        gain_mid,
        cosine,
        sine,
        second,
        seconds[3],
        vmem=vmem,
        scalars=None,
    )
    one_grad, one_low, mid_grad, query_grad = back[:4]
    pair_grads = [back[4]] + [
        send(part, among(by), "pair_grads_core") for by, part in enumerate(back[5:], 1)
    ]
    up_swapped = swap_chunks(add(up_keep, up_got))
    swapped = run(
        functools.partial(united_kernel, pieces),
        1,
        [whole(tok, D), whole(1, D)]
        + [whole(n, tok, D) for n in counts]
        + [fetched, whole(tok, D), whole(tok, D), whole(1, D)],
        [whole(3 * tok + GAIN_ROWS, D)],
        [shape(3 * tok + GAIN_ROWS, D)],
        [pltpu.VMEM((3, fsdp, OWN_ROWS, D), BF), pltpu.SemaphoreType.DMA((3,))],
        query_grad,
        mid_grad,
        *pair_grads,
        gathered,
        hidden_zero,
        one_grad,
        gain_pre,
        vmem=HUGE,
        scalars=None,
    )
    swapped_c = send(swapped, to_core, "zero_core")

    def slabs_of(kernel, height, *arrays):
        return simple(kernel, [shape(2, height, D)] * 2, *arrays)

    query_keep, query_send = slabs_of(
        query_grad_kernel,
        2 * OWN_ROWS,
        attended,
        attended_c,
        query_grad,
        one_low,
        pair_grads[1],
    )
    query_got = send(query_send, to_x, "query_x")
    other_order = [blocks // 2 + at if at < blocks // 2 else at - blocks // 2 for at in range(blocks)]
    up_total = lax.psum(
        simple(copy_kernel, [shape(CHIPS, OWN_ROWS, chunk)], up_swapped, scalars=None),
        "blk",
        axis_index_groups=[other_order],
    )
    merge_keep, merge_send = slabs_of(
        merge_grad_kernel, MERGE_ROWS + GAIN_ROWS, joined, joined_c, swapped, swapped_c
    )
    merge_got = send(merge_send, to_x, "merge_x")
    pair_keep, pair_send = slabs_of(
        pair_grad_kernel, 2 * OWN_ROWS, attended, attended_c, swapped, swapped_c
    )
    pair_got = send(pair_send, to_y, "pair_y")
    zero_back = [
        send(part, outward(other), "zero_out")
        for other, part in enumerate(
            simple(zero_kernel, [shape(rows, D)] * 2, swapped, scalars=None)
        )
    ]
    result_parts = simple(result_parts_kernel, [shape(CHIPS, tok, D)], *activs, w_down)
    result_sum = lax.psum_scatter(
        result_parts, "fsdp", scatter_dimension=0, axis_index_groups=groups, tiled=True
    )
    query_own, query_other = first_step(query_keep, query_got)
    query_y = send(query_other, to_y, "query_y")
    merge_own, merge_other = first_step(merge_keep, merge_got)
    merge_y = send(merge_other, to_y, "merge_y")
    pair_own, pair_other = first_step(pair_keep, pair_got)
    pair_x = send(pair_other, to_x, "pair_x")
    frames_grad, skipped_grad = simple(
        joined_grad_kernel, [shape(MB, rows, D, dtype=F32)] * 2, *zero_back, *mergers
    )
    query_steps = sum_blocks(
        add(query_own, query_y),
        "query_blocks",
        to_total(query_total_kernel, [shape(OWN_ROWS, D, dtype=F32)] * 2),
    )
    next(query_steps)
    merge_steps = sum_blocks(
        add(merge_own, merge_y),
        "merge_blocks",
        to_total(
            merge_total_kernel,
            [shape(*merger.shape, dtype=F32), shape(8, OWN_ROWS, dtype=F32)],
        ),
    )
    next(merge_steps)
    to_projector = lambda ends, array, got: simple(
        functools.partial(pair_total_kernel, ends),
        [shape(*projector.shape, dtype=F32)],
        array,
        got,
        query_total,
    )
    pair_steps = sum_blocks(add(pair_own, pair_x), "pair_blocks", to_projector)
    next(pair_steps)
    reducer_grad, expander_grad = simple(
        feed_total_kernel,
        [shape(*reducer.shape, dtype=F32), shape(*expander.shape, dtype=F32)],
        down_total,
        up_total,
        scalars=None,
    )
    next(query_steps)
    next(merge_steps)
    next(pair_steps)
    next(query_steps)
    next(merge_steps)
    next(pair_steps)
    results = simple(
        result_kernel, [shape(rows, D)] * 2, result_sum[0], hidden_one, scalars=None
    )
    results = [send(part, outward(other), "result_out") for other, part in enumerate(results)]
    query_total, combiner_grad = finish(query_steps)
    merger_grad, gain_grads = finish(merge_steps)
    projector_grad = finish(pair_steps)
    result_out = simple(by_micro_kernel, [shape(MB, rows, D)], *results)
    return (
        result_out,
        frames_grad,
        skipped_grad,
        merger_grad,
        projector_grad,
        combiner_grad,
        expander_grad,
        reducer_grad,
        gain_grads[0],
        gain_grads[1],
    )


def solution(mesh):
    tokens = P(None, ("fsdp", "blk"), None)
    weight = P("fsdp", None)
    gain = P("fsdp")
    return jax.shard_map(
        local,
        mesh=mesh,
        in_specs=(tokens, tokens, P(None, "fsdp", None))
        + (weight,) * 5
        + (gain, gain, tokens),
        out_specs=(tokens, tokens, tokens) + (weight,) * 5 + (gain, gain),
        check_vma=False,
    )
```

```python
import functools
import itertools

import jax
import jax.numpy as jnp
from jax import lax
from jax.experimental import pallas as pl
from jax.experimental.pallas import tpu as pltpu
from jax.sharding import PartitionSpec as P

D = 1024
HEADS = 16
HEAD_DIM = 64
MB = 2
PAIR = 2 * HEAD_DIM
CHIPS = 4
NEG_BIG = -1e30
EPS = 1e-6
AXES = ("fsdp", "blk")
BF = jnp.bfloat16
F32 = jnp.float32
MEGA = 1024 * 1024
SMALL, LARGE, HUGE = 20 * MEGA, 30 * MEGA, 57 * MEGA

MERGE_ROWS = 256
OWN_ROWS = 128
HIDDEN_ROWS = 512
GAIN_ROWS = 16


def dot(left, right):
    return jnp.dot(left, right, preferred_element_type=F32)


def dot_rows(left, right):
    return lax.dot_general(left, right, (((0,), (0,)), ((), ())), preferred_element_type=F32)


def dot_cols(left, right):
    return lax.dot_general(left, right, (((1,), (1,)), ((), ())), preferred_element_type=F32)


def norm_scale(hidden):
    return lax.rsqrt(jnp.mean(hidden * hidden, -1, keepdims=True) + EPS)


def norm_back(grad, hidden, gain):
    scale = norm_scale(hidden)
    weighted = grad * gain
    inner = jnp.mean(weighted * hidden, -1, keepdims=True)
    back = scale * weighted - hidden * (scale * scale * scale * inner)
    gain_grad = jnp.sum(grad * hidden * scale, 0, keepdims=True)
    return back, gain_grad


def swap_halves(tensor):
    lane = lax.broadcasted_iota(jnp.int32, tensor.shape, 1)
    low = (lane % HEAD_DIM) < HEAD_DIM // 2
    return jnp.where(
        low,
        pltpu.roll(tensor, PAIR - HEAD_DIM // 2, 1),
        pltpu.roll(tensor, HEAD_DIM // 2, 1),
    )


def turn(tensor, cosine, sine):
    return tensor * cosine + swap_halves(tensor) * sine


def aligned(at, size):
    return pl.ds(pl.multiple_of(at * size, size), size)


def stacked(parts):
    return jnp.concatenate([part[...] for part in parts], 0)


def summed(parts):
    return functools.reduce(jnp.add, [part[...].astype(F32) for part in parts])


def owner_of(index, chip, other):
    return 2 * index[chip] + (1 - index[4] if other else index[4])


def merge_kernel(index, left, right, *refs):
    weights = refs[: 2 * CHIPS]
    hidden_ref, cot_ref, joined_ref, pre_ref, mid_ref = refs[2 * CHIPS :]
    rows = left.shape[0]
    joined_ref[:rows] = left[:, : 2 * D]
    joined_ref[rows:] = right[:, : 2 * D]
    total = None
    for at, weight in enumerate(weights):
        mine = aligned(owner_of(index, at % CHIPS, at >= CHIPS), MERGE_ROWS)
        part = dot(joined_ref[:, mine], weight[:MERGE_ROWS])
        total = part if total is None else total + part
        mine = aligned(owner_of(index, at % CHIPS, at >= CHIPS), OWN_ROWS)
        gains = weight[MERGE_ROWS:, :OWN_ROWS].astype(F32)
        pre_ref[:, mine] = gains[0:1]
        mid_ref[:, mine] = gains[1:2]
    hidden_ref[...] = total
    cot_ref[:rows] = left[:, 2 * D :]
    cot_ref[rows:] = right[:, 2 * D :]


def fetch(array, at, held, sem):
    copies = [
        pltpu.make_async_copy(
            array.at[:, :, (at + which) * D : (at + which + 1) * D], held.at[which], sem.at[which]
        )
        for which in range(held.shape[0])
    ]
    for copy in copies:
        copy.start()
    return copies


def project_kernel(
    index, hidden, gain, gathered, cosine, sine, cot, act_ref, query_ref, pair_ref, cot_ref, held, sem
):
    copies = fetch(gathered, 0, held, sem)
    cot_ref[...] = cot[...]
    act = (hidden[...] * norm_scale(hidden[...]) * gain[...]).astype(BF)
    act_ref[...] = act
    for which, copy in enumerate(copies):
        copy.wait()
        for part in range(CHIPS):
            wide = slice(part * 2 * PAIR, (part + 1) * 2 * PAIR)
            united = dot(act, held[which, :, :, wide].reshape(D, 2 * PAIR))
            if which == 2:
                pair_ref[1, :, wide] = united.astype(BF)
                continue
            for block in range(2):
                cols = slice(block * PAIR, (block + 1) * PAIR)
                turned = turn(united[:, cols], cosine[...], sine[...]).astype(BF)
                cols = slice((2 * part + block) * PAIR, (2 * part + block + 1) * PAIR)
                if which == 0:
                    query_ref[:, cols] = turned * HEAD_DIM ** (-0.5)
                else:
                    pair_ref[0, :, cols] = turned


def head_mask(shape, head):
    lane = lax.broadcasted_iota(jnp.int32, shape, 1)
    return (lane // HEAD_DIM) == head


def attend_kernel(pieces, index, *refs):
    query, query_seg, key_segs = refs[:3]
    pairs = refs[3 : 3 + pieces]
    act_first, gathered, hidden_zero, gain = refs[3 + pieces : 7 + pieces]
    both_ref, hidden_ref, act_ref, probs_ref, held, sem = refs[7 + pieces :]
    weight = pltpu.make_async_copy(gathered.at[:, :, 3 * D :], held, sem)
    allowed = [key_segs[piece] == query_seg[...] for piece in range(pieces)]
    step = pl.program_id(0)

    @pl.when(step == 0)
    def _():
        weight.start()
        both_ref[0] = act_first[...]

    wide = query.shape[1]
    for block in range(wide // PAIR):
        cols = slice(block * PAIR, (block + 1) * PAIR)
        query_block = query[:, cols]
        key_blocks = [pair[0, :, cols] for pair in pairs]
        value_blocks = [pair[1, :, cols] for pair in pairs]
        mixed = None
        for head in range(2):
            mask = head_mask(query_block.shape, head)
            one_query = jnp.where(mask, query_block, jnp.zeros_like(query_block))
            scores = [
                jnp.where(a, dot_cols(key, one_query), NEG_BIG)
                for key, a in zip(key_blocks, allowed)
            ]
            peak = functools.reduce(jnp.maximum, [jnp.max(s, 0, keepdims=True) for s in scores])
            expo = [jnp.exp(s - peak) for s in scores]
            inverse = 1.0 / functools.reduce(jnp.add, [jnp.sum(e, 0, keepdims=True) for e in expo])
            for piece in range(pieces):
                probs = (expo[piece] * inverse).astype(BF)
                probs_ref[2 * block + head, piece] = probs
                value = value_blocks[piece]
                part = dot_rows(jnp.where(mask, value, jnp.zeros_like(value)), probs)
                mixed = part if mixed is None else mixed + part
        both_ref[1, :, aligned(step * (wide // PAIR) + block, PAIR)] = mixed.T.astype(BF)

    @pl.when(step == pl.num_programs(0) - 1)
    def _():
        weight.wait()
        hidden = hidden_zero[...] + dot(both_ref[1], held[...].reshape(D, D))
        hidden_ref[...] = hidden
        act_ref[...] = (hidden * norm_scale(hidden) * gain[...]).astype(BF)


GELU_ROOT = 0.7978845608028654
GELU_CUBE = 0.044715


def feed_kernel(index, act, cot, w_up, w_down, second_ref, activ_ref, upper_ref):
    cut = 256
    for at in range(w_up.shape[1] // cut):
        cols = slice(at * cut, (at + 1) * cut)
        upper = dot(act[...], w_up[:, cols])
        square = upper * upper
        bent = jnp.tanh(GELU_ROOT * upper * (1.0 + GELU_CUBE * square))
        half = 0.5 * (1.0 + bent)
        activ_ref[:, cols] = (upper * half).astype(BF)
        slope = half + 0.5 * upper * (1.0 - bent * bent) * (
            GELU_ROOT * (1.0 + 3.0 * GELU_CUBE * square)
        )
        upper_ref[:, cols] = (dot_cols(cot[...], w_down[cols, :]) * slope).astype(BF)
    second_ref[...] = dot_cols(upper_ref[...], w_up[...]).astype(BF)


def result_parts_kernel(index, *refs):
    activs, w_down, out_ref = refs[:CHIPS], refs[CHIPS], refs[CHIPS + 1]
    for activ, distance in zip(activs, (0, 1, 3, 2)):
        out_ref[index[distance]] = dot(activ[...], w_down[...]).astype(BF)


def down_grad_kernel(index, *refs):
    activs, cots = stacked(refs[:CHIPS]), stacked(refs[CHIPS : 2 * CHIPS])
    out_ref = refs[2 * CHIPS]
    for core in range(2):
        cols = slice(core * HIDDEN_ROWS, (core + 1) * HIDDEN_ROWS)
        out_ref[core] = dot_rows(activs[:, cols], cots).astype(BF)


def halves_kernel(index, got, out_ref):
    out_ref[...] = summed((got.at[0], got.at[1])).astype(BF)


def up_grad_kernel(index, *refs):
    acts, uppers = stacked(refs[:CHIPS]), stacked(refs[CHIPS : 2 * CHIPS])
    keep_ref, send_ref = refs[2 * CHIPS :]
    even = index[4] == 0
    for chip in range(CHIPS):
        rows = slice(chip * 2 * OWN_ROWS, (chip + 1) * 2 * OWN_ROWS)
        total = dot_rows(acts[:, rows], uppers).astype(BF)
        keep_ref[chip] = jnp.where(even, total[:OWN_ROWS], total[OWN_ROWS:])
        send_ref[chip] = jnp.where(even, total[OWN_ROWS:], total[:OWN_ROWS])


def feed_send_kernel(index, expander, up_ref):
    for chip in range(CHIPS):
        up_ref[chip] = expander[:, chip * D : (chip + 1) * D]


def three_kernel(index, *refs):
    for array, out_ref in zip(refs[:3], refs[3:]):
        out_ref[...] = array[...]


def rest_kernel(index):
    pass


def copy_kernel(index, array, out_ref):
    out_ref[...] = array[...]


def feed_total_kernel(index, down, up, reducer_ref, expander_ref):
    reducer_ref[...] = down[...].astype(F32)
    for chip in range(CHIPS):
        expander_ref[:, chip * D : (chip + 1) * D] = up[chip].astype(F32)


def up_kernel(index, mine, other, out_ref):
    for chip in range(CHIPS):
        out_ref[2 * chip + index[4]] = mine[chip]
        out_ref[2 * chip + 1 - index[4]] = other[chip]


def down_kernel(index, mine, other, out_ref):
    out_ref[index[4]] = mine[...]
    out_ref[1 - index[4]] = other[...]


def attend_back_kernel(pieces, index, *refs):
    query, probs_ref = refs[:2]
    pairs = refs[2 : 2 + pieces]
    at = 2 + pieces
    gathered, hidden_one, cot, gain, cosine, sine = refs[at : at + 6]
    seconds = refs[at + 6 : at + 8]
    at += 8
    one_ref, low_ref, gain_ref, query_ref = refs[at : at + 4]
    pair_refs = refs[at + 4 : at + 4 + pieces]
    held, sem = refs[at + 4 + pieces :]
    swap_ref = pair_refs[1]
    step = pl.program_id(0)
    weight = pltpu.make_async_copy(gathered.at[:, :, 3 * D :], held, sem)

    @pl.when(step == 0)
    def _():
        weight.start()
        back, gain_grad = norm_back(summed(seconds), hidden_one[...], gain[...])
        one = cot[...].astype(F32) + back
        one_ref[...] = one
        gain_ref[...] = gain_grad
        low_ref[...] = one.astype(BF)
        weight.wait()

    wide = query.shape[1]
    swap_ref[3] = low_ref[:, aligned(step, wide)]
    attended_grad = dot_cols(low_ref[...], held.reshape(D, D)[aligned(step, wide), :]).astype(BF)
    for block in range(wide // PAIR):
        cols = slice(block * PAIR, (block + 1) * PAIR)
        query_block = query[:, cols]
        grad_block = attended_grad[:, cols]
        key_blocks = [pair[0, :, cols] for pair in pairs]
        value_blocks = [pair[1, :, cols] for pair in pairs]
        query_grad = None
        key_grads = [None] * pieces
        value_grads = [None] * pieces
        for head in range(2):
            mask = head_mask(query_block.shape, head)
            one_query = jnp.where(mask, query_block, jnp.zeros_like(query_block))
            one_grad = jnp.where(mask, grad_block, jnp.zeros_like(grad_block))
            low = [probs_ref[2 * block + head, piece] for piece in range(pieces)]
            probs = [p.astype(F32) for p in low]
            probs_grad = [dot_cols(value, one_grad) for value in value_blocks]
            delta = functools.reduce(
                jnp.add,
                [jnp.sum(p * g, 0, keepdims=True) for p, g in zip(probs, probs_grad)],
            )
            for piece in range(pieces):
                scores_grad = (probs[piece] * (probs_grad[piece] - delta)).astype(BF)
                key = key_blocks[piece]
                part = dot_rows(jnp.where(mask, key, jnp.zeros_like(key)), scores_grad)
                query_grad = part if query_grad is None else query_grad + part
                key_part = dot(scores_grad, one_query)
                value_part = dot(low[piece], one_grad)
                if head:
                    key_part += key_grads[piece]
                    value_part += value_grads[piece]
                key_grads[piece] = key_part
                value_grads[piece] = value_part
        query_grad = query_grad.T * HEAD_DIM ** (-0.5)
        query_grad = turn(query_grad, cosine[0], -sine[0]).astype(BF)
        query_ref[:, cols] = query_grad
        swap_ref[2, :, cols] = query_grad
        for piece in range(pieces):
            turned = turn(key_grads[piece], cosine[piece], -sine[piece])
            pair_refs[piece][0, :, cols] = turned.astype(BF)
            pair_refs[piece][1, :, cols] = value_grads[piece].astype(BF)


def united_kernel(pieces, index, *refs):
    query_grad, mid = refs[:2]
    pairs = refs[2 : 2 + pieces]
    at = 2 + pieces
    gathered, hidden_zero, one_grad, gain = refs[at : at + 4]
    swap_ref, held, sem = refs[at + 4 :]
    copies = fetch(gathered, 0, held, sem)
    tok = query_grad.shape[0]
    place = lambda which: slice(which * tok, (which + 1) * tok)
    for which in range(2):
        total = functools.reduce(jnp.add, [part[which].astype(F32) for part in pairs])
        swap_ref[place(which)] = total.astype(BF)
    grads = (query_grad[...], swap_ref[place(0)], swap_ref[place(1)])
    grad = None
    for which, copy in enumerate(copies):
        copy.wait()
        part = dot_cols(grads[which], held[which].reshape(D, D))
        grad = part if grad is None else grad + part
    back, gain_grad = norm_back(grad, hidden_zero[...], gain[...])
    swap_ref[place(2)] = (one_grad[...] + back).astype(BF)
    rest = jnp.zeros((GAIN_ROWS - 2, D), F32)
    swap_ref[3 * tok :] = jnp.concatenate([gain_grad, mid[...], rest], 0).astype(BF)


def of_core(ref, index, size):
    return jnp.concatenate(
        [ref[:, aligned(2 * index[chip] + index[4], size)] for chip in range(CHIPS)], 1
    )


def put_slabs(total, rows, at, order, keep_ref, send_ref):
    for ref, chips in ((keep_ref, order[:2]), (send_ref, order[2:])):
        for place, chip in enumerate(chips):
            ref[place, at : at + rows] = total[chip * rows : (chip + 1) * rows].astype(BF)


X_FIRST = (0, 2, 1, 3)
Y_FIRST = (0, 1, 2, 3)


def query_grad_kernel(index, both, both_c, grad, low, swapped, keep_ref, send_ref):
    rights = ((grad[...], swapped[2]), (low[...], swapped[3]))
    for which, right in enumerate(rights):
        left = [of_core(part.at[which], index, OWN_ROWS) for part in (both, both_c)]
        total = dot_rows(jnp.concatenate(left, 0), jnp.concatenate(right, 0))
        put_slabs(total, OWN_ROWS, which * OWN_ROWS, X_FIRST, keep_ref, send_ref)


def pair_grad_kernel(index, both, both_c, own, swapped, keep_ref, send_ref):
    tok = both.shape[1]
    left = jnp.concatenate([of_core(part.at[0], index, OWN_ROWS) for part in (both, both_c)], 0)
    for which in range(2):
        place = slice(which * tok, (which + 1) * tok)
        total = dot_rows(left, jnp.concatenate([own[place], swapped[place]], 0))
        put_slabs(total, OWN_ROWS, which * OWN_ROWS, Y_FIRST, keep_ref, send_ref)


def merge_grad_kernel(index, joined, joined_c, own, swapped, keep_ref, send_ref):
    tok = joined.shape[0]
    both = jnp.concatenate(
        [of_core(part, index, MERGE_ROWS) for part in (joined, joined_c)], 0
    )
    low = slice(2 * tok, 3 * tok)
    total = dot_rows(both, jnp.concatenate([own[low], swapped[low]], 0))
    put_slabs(total, MERGE_ROWS, 0, X_FIRST, keep_ref, send_ref)
    gains = own[3 * tok :].astype(F32) + swapped[3 * tok :].astype(F32)
    keep_ref[:, MERGE_ROWS:] = jnp.zeros((2, GAIN_ROWS, D), BF)
    send_ref[:, MERGE_ROWS:] = jnp.zeros((2, GAIN_ROWS, D), BF)
    for ref, chips in ((keep_ref, X_FIRST[:2]), (send_ref, X_FIRST[2:])):
        for place, chip in enumerate(chips):
            owner = 2 * index[chip] + index[4]
            lane = lax.broadcasted_iota(jnp.int32, gains.shape, 1)
            mine = jnp.where(lane // OWN_ROWS == owner, gains, 0.0)
            chosen = functools.reduce(
                jnp.add,
                [mine[:, at * OWN_ROWS : (at + 1) * OWN_ROWS] for at in range(D // OWN_ROWS)],
            )
            ref[place, MERGE_ROWS:, :OWN_ROWS] = chosen.astype(BF)


def joined_grad_kernel(index, first, second, *refs):
    weights = refs[: 2 * CHIPS]
    rows = first.shape[0]
    low = jnp.concatenate([first[...], second[...]], 0)
    micro = index[5]
    for at, weight in enumerate(weights):
        grad = dot_cols(low, weight[:MERGE_ROWS])
        owner = owner_of(index, at % CHIPS, at >= CHIPS)
        cols = aligned(owner % CHIPS, MERGE_ROWS)
        for half, out_ref in enumerate(refs[2 * CHIPS :]):

            @pl.when(owner // CHIPS == half)
            def _():
                out_ref[micro, :, cols] = grad[:rows]
                out_ref[1 - micro, :, cols] = grad[rows:]


def sum_kernel(index, *refs):
    refs[-1][...] = summed(refs[:-1])


def add_kernel(index, *refs):
    refs[-1][...] = summed(refs[:-1]).astype(BF)


def add_two_kernel(index, keep, got, own_ref, other_ref):
    own_ref[...] = summed((keep.at[0], got.at[0])).astype(BF)
    other_ref[...] = summed((keep.at[1], got.at[1])).astype(BF)


def stack_kernel(index, *refs):
    for at, part in enumerate(refs[:-1]):
        refs[-1][at] = part[...]


def result_kernel(index, *refs):
    left, right = refs[-2:]
    rows = left.shape[0]
    total = summed(refs[:-2])
    left[...] = total[:rows].astype(BF)
    right[...] = total[rows:].astype(BF)


def zero_kernel(index, swapped, left_ref, right_ref):
    rows = left_ref.shape[0]
    left_ref[...] = swapped[4 * rows : 5 * rows]
    right_ref[...] = swapped[5 * rows : 6 * rows]


def by_micro_kernel(index, first, second, out_ref):
    out_ref[index[5]] = first[...]
    out_ref[1 - index[5]] = second[...]


def chosen(index, array, got, ends):
    here = functools.reduce(jnp.logical_or, [index[6] == end for end in ends])
    return jnp.where(here, got[...], array[...])


def choose_kernel(ends, index, array, got, out_ref):
    out_ref[...] = chosen(index, array, got, ends)


def query_total_kernel(ends, index, array, got, query_ref, combiner_ref):
    total = chosen(index, array, got, ends).astype(F32)
    query_ref[...] = total[:OWN_ROWS]
    combiner_ref[...] = total[OWN_ROWS:]


def pair_total_kernel(ends, index, array, got, query, out_ref):
    total = chosen(index, array, got, ends).astype(F32)
    out_ref[:, :D] = query[...]
    out_ref[:, D : 2 * D] = total[:OWN_ROWS]
    out_ref[:, 2 * D :] = total[OWN_ROWS:]


def merge_total_kernel(ends, index, array, got, out_ref, gain_ref):
    total = chosen(index, array, got, ends).astype(F32)
    out_ref[...] = total[:MERGE_ROWS]
    gain_ref[...] = total[MERGE_ROWS : MERGE_ROWS + 8, :OWN_ROWS]


def call(kernel, vmem, grid, in_specs, out_specs, out_shape, scratch, index, token, *arrays):
    scalars = 0 if index is None else 1

    def passing(*refs):
        index_ref, refs = (refs[0], refs[1:]) if scalars else (None, refs)
        inputs = 1 + len(in_specs)
        kernel(index_ref, *refs[1:inputs], *refs[inputs + 1 :])

    anywhere = pl.BlockSpec(memory_space=pl.ANY)
    return pl.pallas_call(
        passing,
        grid_spec=pltpu.PrefetchScalarGridSpec(
            num_scalar_prefetch=scalars,
            grid=grid,
            in_specs=[anywhere] + in_specs,
            out_specs=[anywhere] + out_specs,
            scratch_shapes=scratch,
        ),
        out_shape=[jax.ShapeDtypeStruct(token.shape, token.dtype)] + out_shape,
        input_output_aliases={scalars: 0},
        name=getattr(kernel, "func", kernel).__name__,
        compiler_params=pltpu.CompilerParams(
            dimension_semantics=("arbitrary",) * len(grid), vmem_limit_bytes=vmem
        ),
        cost_estimate=pl.CostEstimate(flops=10**12, bytes_accessed=0, transcendentals=0),
    )(*([index] if scalars else []), token, *arrays)


def shape(*dims, dtype=BF):
    return jax.ShapeDtypeStruct(dims, dtype)


def whole(*dims):
    return pl.BlockSpec(dims, lambda *_: (0,) * len(dims))


def local(
    frames,
    skipped,
    lengths,
    merger,
    projector,
    combiner,
    expander,
    reducer,
    prenorm,
    midnorm,
    cotangent,
):
    rows = frames.shape[1]
    tok = 2 * rows
    blocks = lax.axis_size("blk")
    fsdp = lax.axis_size("fsdp")
    quarter = blocks // 4
    pieces = blocks // 2
    stream = rows * blocks

    me = lax.axis_index("fsdp")
    spot = lax.axis_index("blk")
    core = me % 2
    chip = me // 2
    unit = spot // quarter
    micro = unit // 2
    source_core = unit % 2
    half = (spot % quarter) * 2 + core

    def send(array, route, name="send"):
        pairs = []
        for y, x, c, b in itertools.product(range(2), range(2), range(2), range(blocks)):
            target = route(y, x, c, b)
            if target is not None:
                ty, tx, tc, tb = target
                pairs.append((((y * 2 + x) * 2 + c) * blocks + b, ((ty * 2 + tx) * 2 + tc) * blocks + tb))
        with jax.named_scope(name):
            return lax.ppermute(array, AXES, pairs)

    to_x = lambda y, x, c, b: (y, 1 - x, c, b)
    to_y = lambda y, x, c, b: (1 - y, x, c, b)
    to_diagonal = lambda y, x, c, b: (1 - y, 1 - x, c, b)
    to_core = lambda y, x, c, b: (y, x, 1 - c, b)
    around = (to_x, to_y, to_diagonal)
    over_plane = (to_x, to_diagonal, to_y)

    def holder(micro_at, c, pair):
        return (2 * micro_at + c) * quarter + pair // 2, pair % 2

    def inward(other):
        def route(y, x, c, b):
            tb, tc = holder((b + other) % 2, c, b // 2)
            return (y, x, tc, tb)

        return route

    def outward(other):
        forward = inward(other)
        table = {}
        for y, x, c, b in itertools.product(range(2), range(2), range(2), range(blocks)):
            table[forward(y, x, c, b)] = (y, x, c, b)
        return lambda *at: table[at]

    def among(by):
        def route(y, x, c, b):
            at = ((b % quarter) * 2 + c) ^ by
            return (y, x, at % 2, (b // quarter) * quarter + at // 2)

        return route

    def take_in(pick, name):
        return tuple(send(pick((spot + other) % 2), inward(other), name) for other in range(2))

    def sum_blocks(array, name, last):
        middle = blocks // 2
        plans = [{step: step + 1, blocks - 1 - step: blocks - 2 - step} for step in range(middle - 1)]
        plans.append({middle - 1: middle, middle: middle - 1})
        for moves in plans:
            got = send(array, lambda y, x, c, b: (y, x, c, moves[b]) if b in moves else None, name)
            yield
            array = add(array, got)
        for step in range(middle - 1):
            moves = {middle - 1 - step: middle - 2 - step, middle + step: middle + 1 + step}
            got = send(array, lambda y, x, c, b: (y, x, c, moves[b]) if b in moves else None, name)
            yield
            ends = tuple(moves.values())
            if step == middle - 2:
                array = last(ends, array, got)
            else:
                choose = functools.partial(choose_kernel, ends)
                array = simple(choose, [shape(*array.shape)], array, got)
        yield array

    def finish(steps):
        array = None
        while array is None:
            array = next(steps)
        return array

    gathered = lax.all_gather(jnp.concatenate([projector, combiner], 1), "fsdp", axis=0)

    gain_rows = jnp.pad(jnp.stack([prenorm, midnorm]), ((0, GAIN_ROWS - 2), (0, D - OWN_ROWS)))
    merger_own = jnp.concatenate([merger, gain_rows], 0)
    mergers = [merger_own] + [send(merger_own, route, "merger_around") for route in around]
    mergers += [send(part, to_core, "merger_core") for part in mergers]

    left, right = take_in(
        lambda m: jnp.concatenate([frames[m], skipped[m], cotangent[m]], -1), "tokens_in"
    )
    other_lengths = send(lengths, to_core, "lengths_core")

    mine = jnp.where(source_core == core, lengths, other_lengths)[:, 0]
    row_lengths = jnp.where(micro == 0, mine[0], mine[1])
    ends = jnp.cumsum(row_lengths)
    within = jnp.arange(rows, dtype=jnp.int32)

    def layout(at):
        offsets = jnp.concatenate(
            [(2 * at + micro) * rows + within, (2 * at + 1 - micro) * rows + within]
        )
        before = (ends[None, :] <= offsets[:, None]).astype(jnp.int32)
        return jnp.sum(before, 1), offsets - jnp.sum(before * row_lengths[None, :], 1)

    layouts = [layout(half ^ by) for by in range(pieces)]
    query_seg = layouts[0][0][None]
    key_segs = jnp.stack([segment for segment, _ in layouts])[:, :, None]
    inverse = 10000.0 ** (-jnp.arange(HEAD_DIM // 2, dtype=F32) * 2.0 / HEAD_DIM)
    positions = jnp.stack([position for _, position in layouts]).astype(F32)
    angles = positions[:, :, None] * inverse
    cosine = jnp.tile(jnp.cos(angles), (1, 1, 4))
    sine = jnp.sin(angles)
    sine = jnp.concatenate([-sine, sine, -sine, sine], -1)

    index = jnp.stack(
        [chip, chip ^ 1, chip ^ 2, chip ^ 3, core, spot % 2, spot, spot]
    ).astype(jnp.int32)
    last_token = [jnp.zeros((8, 128), F32)]

    def run(
        kernel, grid, in_specs, out_specs, out_shape, scratch, *arrays, vmem=SMALL, scalars=index
    ):
        last_token[0], *results = call(
            kernel,
            vmem,
            (grid,) if grid else (),
            in_specs,
            out_specs,
            out_shape,
            scratch,
            scalars,
            last_token[0],
            *arrays,
        )
        return results[0] if len(results) == 1 else results

    def rest():
        run(rest_kernel, 0, [], [], [], [], scalars=None)

    def meet():
        last_token[0] = send(last_token[0], to_core, "order")

    def simple(kernel, outs, *arrays, scalars=index):
        held = pl.BlockSpec(memory_space=pltpu.VMEM)
        return run(
            kernel,
            0,
            [held] * len(arrays),
            [held] * len(outs),
            outs,
            [],
            *arrays,
            scalars=scalars,
        )

    def to_total(kernel, outs):
        return lambda ends, array, got: simple(functools.partial(kernel, ends), outs, array, got)

    def add(*arrays):
        return simple(add_kernel, [shape(*arrays[0].shape)], *arrays, scalars=None)

    def first_step(keep, got):
        return simple(add_two_kernel, [shape(*keep.shape[1:])] * 2, keep, got, scalars=None)

    wide = 2 * OWN_ROWS
    cols_at = lambda height, width: pl.BlockSpec((height, width), lambda s, *_: (0, s))
    cols_of = lambda height, width: pl.BlockSpec((height, width), lambda s, i: (0, i[s]))
    table = whole(tok, PAIR)
    tables = whole(pieces, tok, PAIR)

    down_c = send(reducer, to_core, "w_down_core")
    chunk = expander.shape[1] // CHIPS
    w_down = simple(down_kernel, [shape(2, HIDDEN_ROWS, D)], reducer, down_c).reshape(chunk, D)
    hidden_zero, cot, joined, gain_pre, gain_mid = simple(
        merge_kernel,
        [shape(tok, D, dtype=F32), shape(tok, D), shape(tok, 2 * D)]
        + [shape(1, D, dtype=F32)] * 2,
        left,
        right,
        *mergers,
    )
    joined_c = send(joined, to_core, "joined_core")

    groups = [[c + 2 * at for at in range(CHIPS)] for c in range(2)]
    swap_chunks = lambda parts: lax.all_to_all(
        parts, "fsdp", 0, 0, axis_index_groups=groups, tiled=True
    )
    up_swapped = swap_chunks(
        simple(feed_send_kernel, [shape(CHIPS, OWN_ROWS, chunk)], expander, scalars=None)
    )
    fetched = pl.BlockSpec(memory_space=pltpu.HBM)
    act_first, query, pair, cot_again = run(
        project_kernel,
        1,
        [whole(tok, D), whole(1, D), fetched, table, table, whole(tok, D)],
        [whole(tok, D), whole(tok, D), whole(2, tok, D), whole(tok, D)],
        [shape(tok, D), shape(tok, D), shape(2, tok, D), shape(tok, D)],
        [pltpu.VMEM((3, fsdp, OWN_ROWS, D), BF), pltpu.SemaphoreType.DMA((3,))],
        hidden_zero,
        gain_pre,
        gathered,
        cosine[0],
        sine[0],
        cot,
        vmem=HUGE,
        scalars=None,
    )
    cots = [send(cot_again, route, "cot_around") for route in over_plane]
    up_mine = simple(copy_kernel, [shape(CHIPS, OWN_ROWS, chunk)], up_swapped, scalars=None)
    up_c = send(up_mine, to_core, "w_up_core")
    pairs = [pair] + [send(pair, among(by), "pair_core") for by in range(1, pieces)]
    steps, vmem = (1, LARGE) if pieces == 2 else (CHIPS * 2, HUGE)
    head_cols = cols_at(tok, D // steps)
    pair_cols = lambda count: pl.BlockSpec((count, tok, D // steps), lambda s, *_: (0, 0, s))
    probs_spec = pl.BlockSpec((HEADS // steps, pieces, tok, tok), lambda s, *_: (s, 0, 0, 0))
    combiner_held = [pltpu.VMEM((fsdp, OWN_ROWS, D), BF), pltpu.SemaphoreType.DMA]
    attended, hidden_one, act_second, probs = run(
        functools.partial(attend_kernel, pieces),
        steps,
        [head_cols, whole(1, tok), whole(pieces, tok, 1)]
        + [pair_cols(2)] * pieces
        + [whole(tok, D), fetched, whole(tok, D), whole(1, D)],
        [whole(2, tok, D), whole(tok, D), whole(tok, D), probs_spec],
        [
            shape(2, tok, D),
            shape(tok, D, dtype=F32),
            shape(tok, D),
            shape(HEADS, pieces, tok, tok),
        ],
        combiner_held,
        query,
        query_seg,
        key_segs,
        *pairs,
        act_first,
        gathered,
        hidden_zero,
        gain_mid,
        vmem=vmem,
        scalars=None,
    )
    acts = [act_second] + [send(act_second, route, "act_around") for route in over_plane]
    attended_c = send(attended, to_core, "attended_core")
    w_up = simple(up_kernel, [shape(fsdp, OWN_ROWS, chunk)], up_mine, up_c).reshape(D, chunk)
    cots = [cot] + simple(three_kernel, [shape(tok, D)] * 3, *cots, scalars=None)

    fed = [
        simple(
            feed_kernel,
            [shape(tok, D), shape(tok, chunk), shape(tok, chunk)],
            act,
            grad,
            w_up,
            w_down,
            scalars=None,
        )
        for act, grad in zip(acts, cots)
    ]
    seconds = [fed[0][0]] + [
        send(part[0], route, "second_around") for part, route in zip(fed[1:], over_plane)
    ]
    activs = [part[1] for part in fed]
    down_parts = simple(
        down_grad_kernel, [shape(2, HIDDEN_ROWS, D)], *activs, *cots, scalars=None
    )
    core_groups = [[at, at + 1] for at in range(0, fsdp, 2)]
    down_halves = lax.all_to_all(
        down_parts, "fsdp", 0, 0, axis_index_groups=core_groups, tiled=True
    )
    up_keep, up_send = simple(
        up_grad_kernel, [shape(CHIPS, OWN_ROWS, chunk)] * 2, *acts, *[part[2] for part in fed]
    )
    up_got = send(up_send, to_core, "up_core")

    second = simple(
        sum_kernel, [shape(tok, D, dtype=F32)], seconds[0], seconds[1], scalars=None
    )
    second = simple(sum_kernel, [shape(tok, D, dtype=F32)], second, seconds[2], scalars=None)

    reversed_blocks = [list(reversed(range(blocks)))]
    down_total = lax.psum(
        simple(halves_kernel, [shape(HIDDEN_ROWS, D)], down_halves, scalars=None),
        "blk",
        axis_index_groups=reversed_blocks,
    )
    meet()

    steps = CHIPS if pieces == 2 else 2 * CHIPS
    head_cols = cols_at(tok, D // steps)
    pair_cols = lambda count: pl.BlockSpec((count, tok, D // steps), lambda s, *_: (0, 0, s))
    probs_spec = pl.BlockSpec((HEADS // steps, pieces, tok, tok), lambda s, *_: (s, 0, 0, 0))
    counts = [4 if by == 1 else 2 for by in range(pieces)]
    back = run(
        functools.partial(attend_back_kernel, pieces),
        steps,
        [head_cols, probs_spec]
        + [pair_cols(2)] * pieces
        + [fetched, whole(tok, D), whole(tok, D), whole(1, D)]
        + [tables, tables]
        + [whole(tok, D)] * 2,
        [whole(tok, D), whole(tok, D), whole(1, D), head_cols] + [pair_cols(n) for n in counts],
        [
            shape(tok, D, dtype=F32),
            shape(tok, D),
            shape(1, D, dtype=F32),
            shape(tok, D),
        ]
        + [shape(n, tok, D) for n in counts],
        combiner_held,
        query,
        probs,
        *pairs,
        gathered,
        hidden_one,
        cot,
        gain_mid,
        cosine,
        sine,
        second,
        seconds[3],
        vmem=HUGE,
        scalars=None,
    )
    one_grad, one_low, mid_grad, query_grad = back[:4]
    pair_grads = [back[4]] + [
        send(part, among(by), "pair_grads_core") for by, part in enumerate(back[5:], 1)
    ]
    up_swapped = swap_chunks(add(up_keep, up_got))
    swapped = run(
        functools.partial(united_kernel, pieces),
        1,
        [whole(tok, D), whole(1, D)]
        + [whole(n, tok, D) for n in counts]
        + [fetched, whole(tok, D), whole(tok, D), whole(1, D)],
        [whole(3 * tok + GAIN_ROWS, D)],
        [shape(3 * tok + GAIN_ROWS, D)],
        [pltpu.VMEM((3, fsdp, OWN_ROWS, D), BF), pltpu.SemaphoreType.DMA((3,))],
        query_grad,
        mid_grad,
        *pair_grads,
        gathered,
        hidden_zero,
        one_grad,
        gain_pre,
        vmem=HUGE,
        scalars=None,
    )
    swapped_c = send(swapped, to_core, "zero_core")

    def slabs_of(kernel, height, *arrays):
        return simple(kernel, [shape(2, height, D)] * 2, *arrays)

    query_keep, query_send = slabs_of(
        query_grad_kernel,
        2 * OWN_ROWS,
        attended,
        attended_c,
        query_grad,
        one_low,
        pair_grads[1],
    )
    query_got = send(query_send, to_x, "query_x")
    other_order = [blocks // 2 + at if at < blocks // 2 else at - blocks // 2 for at in range(blocks)]
    up_total = lax.psum(
        simple(copy_kernel, [shape(CHIPS, OWN_ROWS, chunk)], up_swapped, scalars=None),
        "blk",
        axis_index_groups=[other_order],
    )
    merge_keep, merge_send = slabs_of(
        merge_grad_kernel, MERGE_ROWS + GAIN_ROWS, joined, joined_c, swapped, swapped_c
    )
    merge_got = send(merge_send, to_x, "merge_x")
    pair_keep, pair_send = slabs_of(
        pair_grad_kernel, 2 * OWN_ROWS, attended, attended_c, swapped, swapped_c
    )
    pair_got = send(pair_send, to_y, "pair_y")
    zero_back = [
        send(part, outward(other), "zero_out")
        for other, part in enumerate(
            simple(zero_kernel, [shape(rows, D)] * 2, swapped, scalars=None)
        )
    ]
    result_parts = simple(result_parts_kernel, [shape(CHIPS, tok, D)], *activs, w_down)
    result_sum = lax.psum_scatter(
        result_parts, "fsdp", scatter_dimension=0, axis_index_groups=groups, tiled=True
    )
    query_own, query_other = first_step(query_keep, query_got)
    query_y = send(query_other, to_y, "query_y")
    merge_own, merge_other = first_step(merge_keep, merge_got)
    merge_y = send(merge_other, to_y, "merge_y")
    pair_own, pair_other = first_step(pair_keep, pair_got)
    pair_x = send(pair_other, to_x, "pair_x")
    query_steps = sum_blocks(
        add(query_own, query_y),
        "query_blocks",
        to_total(query_total_kernel, [shape(OWN_ROWS, D, dtype=F32)] * 2),
    )
    next(query_steps)
    frames_grad, skipped_grad = simple(
        joined_grad_kernel, [shape(MB, rows, D, dtype=F32)] * 2, *zero_back, *mergers
    )
    merge_steps = sum_blocks(
        add(merge_own, merge_y),
        "merge_blocks",
        to_total(
            merge_total_kernel,
            [shape(*merger.shape, dtype=F32), shape(8, OWN_ROWS, dtype=F32)],
        ),
    )
    next(merge_steps)
    to_projector = lambda ends, array, got: simple(
        functools.partial(pair_total_kernel, ends),
        [shape(*projector.shape, dtype=F32)],
        array,
        got,
        query_total,
    )
    pair_steps = sum_blocks(add(pair_own, pair_x), "pair_blocks", to_projector)
    next(pair_steps)
    next(query_steps)
    next(merge_steps)
    next(pair_steps)
    next(query_steps)
    next(merge_steps)
    next(pair_steps)
    reducer_grad, expander_grad = simple(
        feed_total_kernel,
        [shape(*reducer.shape, dtype=F32), shape(*expander.shape, dtype=F32)],
        down_total,
        up_total,
        scalars=None,
    )
    results = simple(
        result_kernel, [shape(rows, D)] * 2, result_sum[0], hidden_one, scalars=None
    )
    results = [send(part, outward(other), "result_out") for other, part in enumerate(results)]
    query_total, combiner_grad = finish(query_steps)
    merger_grad, gain_grads = finish(merge_steps)
    projector_grad = finish(pair_steps)
    result_out = simple(by_micro_kernel, [shape(MB, rows, D)], *results)
    return (
        result_out,
        frames_grad,
        skipped_grad,
        merger_grad,
        projector_grad,
        combiner_grad,
        expander_grad,
        reducer_grad,
        gain_grads[0],
        gain_grads[1],
    )


def solution(mesh):
    tokens = P(None, ("fsdp", "blk"), None)
    weight = P("fsdp", None)
    gain = P("fsdp")
    return jax.shard_map(
        local,
        mesh=mesh,
        in_specs=(tokens, tokens, P(None, "fsdp", None))
        + (weight,) * 5
        + (gain, gain, tokens),
        out_specs=(tokens, tokens, tokens) + (weight,) * 5 + (gain, gain),
        check_vma=False,
    )
```

```python
import functools
import itertools

import jax
import jax.numpy as jnp
from jax import lax
from jax.experimental import pallas as pl
from jax.experimental.pallas import tpu as pltpu
from jax.sharding import PartitionSpec as P

D = 1024
HEADS = 16
HEAD_DIM = 64
MB = 2
PAIR = 2 * HEAD_DIM
CHIPS = 4
NEG_BIG = -1e30
EPS = 1e-6
AXES = ("fsdp", "blk")
BF = jnp.bfloat16
F32 = jnp.float32
MEGA = 1024 * 1024
SMALL, LARGE, HUGE = 20 * MEGA, 30 * MEGA, 57 * MEGA

MERGE_ROWS = 256
OWN_ROWS = 128
HIDDEN_ROWS = 512
GAIN_ROWS = 16


def dot(left, right):
    return jnp.dot(left, right, preferred_element_type=F32)


def dot_rows(left, right):
    return lax.dot_general(left, right, (((0,), (0,)), ((), ())), preferred_element_type=F32)


def dot_cols(left, right):
    return lax.dot_general(left, right, (((1,), (1,)), ((), ())), preferred_element_type=F32)


def norm_scale(hidden):
    return lax.rsqrt(jnp.mean(hidden * hidden, -1, keepdims=True) + EPS)


def norm_back(grad, hidden, gain):
    scale = norm_scale(hidden)
    weighted = grad * gain
    inner = jnp.mean(weighted * hidden, -1, keepdims=True)
    back = scale * weighted - hidden * (scale * scale * scale * inner)
    gain_grad = jnp.sum(grad * hidden * scale, 0, keepdims=True)
    return back, gain_grad


def swap_halves(tensor):
    lane = lax.broadcasted_iota(jnp.int32, tensor.shape, 1)
    low = (lane % HEAD_DIM) < HEAD_DIM // 2
    return jnp.where(
        low,
        pltpu.roll(tensor, PAIR - HEAD_DIM // 2, 1),
        pltpu.roll(tensor, HEAD_DIM // 2, 1),
    )


def turn(tensor, cosine, sine):
    return tensor * cosine + swap_halves(tensor) * sine


def aligned(at, size):
    return pl.ds(pl.multiple_of(at * size, size), size)


def stacked(parts):
    return jnp.concatenate([part[...] for part in parts], 0)


def summed(parts):
    return functools.reduce(jnp.add, [part[...].astype(F32) for part in parts])


def owner_of(index, chip, other):
    return 2 * index[chip] + (1 - index[4] if other else index[4])


def merge_kernel(index, left, right, *refs):
    weights = refs[: 2 * CHIPS]
    hidden_ref, cot_ref, joined_ref, pre_ref, mid_ref = refs[2 * CHIPS :]
    rows = left.shape[0]
    joined_ref[:rows] = left[:, : 2 * D]
    joined_ref[rows:] = right[:, : 2 * D]
    total = None
    for at, weight in enumerate(weights):
        mine = aligned(owner_of(index, at % CHIPS, at >= CHIPS), MERGE_ROWS)
        part = dot(joined_ref[:, mine], weight[:MERGE_ROWS])
        total = part if total is None else total + part
        mine = aligned(owner_of(index, at % CHIPS, at >= CHIPS), OWN_ROWS)
        gains = weight[MERGE_ROWS:, :OWN_ROWS].astype(F32)
        pre_ref[:, mine] = gains[0:1]
        mid_ref[:, mine] = gains[1:2]
    hidden_ref[...] = total
    cot_ref[:rows] = left[:, 2 * D :]
    cot_ref[rows:] = right[:, 2 * D :]


def fetch(array, at, held, sem):
    copies = [
        pltpu.make_async_copy(
            array.at[:, :, (at + which) * D : (at + which + 1) * D], held.at[which], sem.at[which]
        )
        for which in range(held.shape[0])
    ]
    for copy in copies:
        copy.start()
    return copies


def project_kernel(
    index, hidden, gain, gathered, cosine, sine, cot, act_ref, query_ref, pair_ref, cot_ref, held, sem
):
    copies = fetch(gathered, 0, held, sem)
    cot_ref[...] = cot[...]
    act = (hidden[...] * norm_scale(hidden[...]) * gain[...]).astype(BF)
    act_ref[...] = act
    for which, copy in enumerate(copies):
        copy.wait()
        for part in range(CHIPS):
            wide = slice(part * 2 * PAIR, (part + 1) * 2 * PAIR)
            united = dot(act, held[which, :, :, wide].reshape(D, 2 * PAIR))
            if which == 2:
                pair_ref[1, :, wide] = united.astype(BF)
                continue
            for block in range(2):
                cols = slice(block * PAIR, (block + 1) * PAIR)
                turned = turn(united[:, cols], cosine[...], sine[...]).astype(BF)
                cols = slice((2 * part + block) * PAIR, (2 * part + block + 1) * PAIR)
                if which == 0:
                    query_ref[:, cols] = turned * HEAD_DIM ** (-0.5)
                else:
                    pair_ref[0, :, cols] = turned


def head_mask(shape, head):
    lane = lax.broadcasted_iota(jnp.int32, shape, 1)
    return (lane // HEAD_DIM) == head


def attend_kernel(pieces, index, *refs):
    query, query_seg, key_segs = refs[:3]
    pairs = refs[3 : 3 + pieces]
    act_first, gathered, hidden_zero, gain = refs[3 + pieces : 7 + pieces]
    both_ref, hidden_ref, act_ref, probs_ref, held, sem = refs[7 + pieces :]
    weight = pltpu.make_async_copy(gathered.at[:, :, 3 * D :], held, sem)
    allowed = [key_segs[piece] == query_seg[...] for piece in range(pieces)]
    step = pl.program_id(0)

    @pl.when(step == 0)
    def _():
        weight.start()
        both_ref[0] = act_first[...]

    wide = query.shape[1]
    for block in range(wide // PAIR):
        cols = slice(block * PAIR, (block + 1) * PAIR)
        query_block = query[:, cols]
        key_blocks = [pair[0, :, cols] for pair in pairs]
        value_blocks = [pair[1, :, cols] for pair in pairs]
        mixed = None
        for head in range(2):
            mask = head_mask(query_block.shape, head)
            one_query = jnp.where(mask, query_block, jnp.zeros_like(query_block))
            scores = [
                jnp.where(a, dot_cols(key, one_query), NEG_BIG)
                for key, a in zip(key_blocks, allowed)
            ]
            peak = functools.reduce(jnp.maximum, [jnp.max(s, 0, keepdims=True) for s in scores])
            expo = [jnp.exp(s - peak) for s in scores]
            inverse = 1.0 / functools.reduce(jnp.add, [jnp.sum(e, 0, keepdims=True) for e in expo])
            for piece in range(pieces):
                probs = (expo[piece] * inverse).astype(BF)
                probs_ref[2 * block + head, piece] = probs
                value = value_blocks[piece]
                part = dot_rows(jnp.where(mask, value, jnp.zeros_like(value)), probs)
                mixed = part if mixed is None else mixed + part
        both_ref[1, :, aligned(step * (wide // PAIR) + block, PAIR)] = mixed.T.astype(BF)

    @pl.when(step == pl.num_programs(0) - 1)
    def _():
        weight.wait()
        hidden = hidden_zero[...] + dot(both_ref[1], held[...].reshape(D, D))
        hidden_ref[...] = hidden
        act_ref[...] = (hidden * norm_scale(hidden) * gain[...]).astype(BF)


GELU_ROOT = 0.7978845608028654
GELU_CUBE = 0.044715


def feed_kernel(index, act, cot, w_up, w_down, second_ref, activ_ref, upper_ref):
    cut = 256
    for at in range(w_up.shape[1] // cut):
        cols = slice(at * cut, (at + 1) * cut)
        upper = dot(act[...], w_up[:, cols])
        square = upper * upper
        bent = jnp.tanh(GELU_ROOT * upper * (1.0 + GELU_CUBE * square))
        half = 0.5 * (1.0 + bent)
        activ_ref[:, cols] = (upper * half).astype(BF)
        slope = half + 0.5 * upper * (1.0 - bent * bent) * (
            GELU_ROOT * (1.0 + 3.0 * GELU_CUBE * square)
        )
        upper_ref[:, cols] = (dot_cols(cot[...], w_down[cols, :]) * slope).astype(BF)
    second_ref[...] = dot_cols(upper_ref[...], w_up[...]).astype(BF)


def result_parts_kernel(index, *refs):
    activs, w_down, out_ref = refs[:CHIPS], refs[CHIPS], refs[CHIPS + 1]
    for activ, distance in zip(activs, (0, 1, 3, 2)):
        out_ref[index[distance]] = dot(activ[...], w_down[...]).astype(BF)


def down_grad_kernel(index, *refs):
    activs, cots = stacked(refs[:CHIPS]), stacked(refs[CHIPS : 2 * CHIPS])
    out_ref = refs[2 * CHIPS]
    for core in range(2):
        cols = slice(core * HIDDEN_ROWS, (core + 1) * HIDDEN_ROWS)
        out_ref[core] = dot_rows(activs[:, cols], cots).astype(BF)


def halves_kernel(index, got, out_ref):
    out_ref[...] = summed((got.at[0], got.at[1])).astype(BF)


def up_grad_kernel(index, *refs):
    acts, uppers = stacked(refs[:CHIPS]), stacked(refs[CHIPS : 2 * CHIPS])
    keep_ref, send_ref = refs[2 * CHIPS :]
    even = index[4] == 0
    for chip in range(CHIPS):
        rows = slice(chip * 2 * OWN_ROWS, (chip + 1) * 2 * OWN_ROWS)
        total = dot_rows(acts[:, rows], uppers).astype(BF)
        keep_ref[chip] = jnp.where(even, total[:OWN_ROWS], total[OWN_ROWS:])
        send_ref[chip] = jnp.where(even, total[OWN_ROWS:], total[:OWN_ROWS])


def feed_send_kernel(index, expander, up_ref):
    for chip in range(CHIPS):
        up_ref[chip] = expander[:, chip * D : (chip + 1) * D]


def three_kernel(index, *refs):
    for array, out_ref in zip(refs[:3], refs[3:]):
        out_ref[...] = array[...]


def rest_kernel(index):
    pass


def copy_kernel(index, array, out_ref):
    out_ref[...] = array[...]


def feed_total_kernel(index, down, up, reducer_ref, expander_ref):
    reducer_ref[...] = down[...].astype(F32)
    for chip in range(CHIPS):
        expander_ref[:, chip * D : (chip + 1) * D] = up[chip].astype(F32)


def up_kernel(index, mine, other, out_ref):
    for chip in range(CHIPS):
        out_ref[2 * chip + index[4]] = mine[chip]
        out_ref[2 * chip + 1 - index[4]] = other[chip]


def down_kernel(index, mine, other, out_ref):
    out_ref[index[4]] = mine[...]
    out_ref[1 - index[4]] = other[...]


def attend_back_kernel(pieces, index, *refs):
    query, probs_ref = refs[:2]
    pairs = refs[2 : 2 + pieces]
    at = 2 + pieces
    gathered, hidden_one, cot, gain, cosine, sine = refs[at : at + 6]
    seconds = refs[at + 6 : at + 8]
    at += 8
    one_ref, low_ref, gain_ref, query_ref = refs[at : at + 4]
    pair_refs = refs[at + 4 : at + 4 + pieces]
    held, sem = refs[at + 4 + pieces :]
    swap_ref = pair_refs[1]
    step = pl.program_id(0)
    weight = pltpu.make_async_copy(gathered.at[:, :, 3 * D :], held, sem)

    @pl.when(step == 0)
    def _():
        weight.start()
        back, gain_grad = norm_back(summed(seconds), hidden_one[...], gain[...])
        one = cot[...].astype(F32) + back
        one_ref[...] = one
        gain_ref[...] = gain_grad
        low_ref[...] = one.astype(BF)
        weight.wait()

    wide = query.shape[1]
    swap_ref[3] = low_ref[:, aligned(step, wide)]
    attended_grad = dot_cols(low_ref[...], held.reshape(D, D)[aligned(step, wide), :]).astype(BF)
    for block in range(wide // PAIR):
        cols = slice(block * PAIR, (block + 1) * PAIR)
        query_block = query[:, cols]
        grad_block = attended_grad[:, cols]
        key_blocks = [pair[0, :, cols] for pair in pairs]
        value_blocks = [pair[1, :, cols] for pair in pairs]
        query_grad = None
        key_grads = [None] * pieces
        value_grads = [None] * pieces
        for head in range(2):
            mask = head_mask(query_block.shape, head)
            one_query = jnp.where(mask, query_block, jnp.zeros_like(query_block))
            one_grad = jnp.where(mask, grad_block, jnp.zeros_like(grad_block))
            low = [probs_ref[2 * block + head, piece] for piece in range(pieces)]
            probs = [p.astype(F32) for p in low]
            probs_grad = [dot_cols(value, one_grad) for value in value_blocks]
            delta = functools.reduce(
                jnp.add,
                [jnp.sum(p * g, 0, keepdims=True) for p, g in zip(probs, probs_grad)],
            )
            for piece in range(pieces):
                scores_grad = (probs[piece] * (probs_grad[piece] - delta)).astype(BF)
                key = key_blocks[piece]
                part = dot_rows(jnp.where(mask, key, jnp.zeros_like(key)), scores_grad)
                query_grad = part if query_grad is None else query_grad + part
                key_part = dot(scores_grad, one_query)
                value_part = dot(low[piece], one_grad)
                if head:
                    key_part += key_grads[piece]
                    value_part += value_grads[piece]
                key_grads[piece] = key_part
                value_grads[piece] = value_part
        query_grad = query_grad.T * HEAD_DIM ** (-0.5)
        query_grad = turn(query_grad, cosine[0], -sine[0]).astype(BF)
        query_ref[:, cols] = query_grad
        swap_ref[2, :, cols] = query_grad
        for piece in range(pieces):
            turned = turn(key_grads[piece], cosine[piece], -sine[piece])
            pair_refs[piece][0, :, cols] = turned.astype(BF)
            pair_refs[piece][1, :, cols] = value_grads[piece].astype(BF)


def united_kernel(pieces, index, *refs):
    query_grad, mid = refs[:2]
    pairs = refs[2 : 2 + pieces]
    at = 2 + pieces
    gathered, hidden_zero, one_grad, gain = refs[at : at + 4]
    swap_ref, held, sem = refs[at + 4 :]
    copies = fetch(gathered, 0, held, sem)
    tok = query_grad.shape[0]
    place = lambda which: slice(which * tok, (which + 1) * tok)
    for which in range(2):
        total = functools.reduce(jnp.add, [part[which].astype(F32) for part in pairs])
        swap_ref[place(which)] = total.astype(BF)
    grads = (query_grad[...], swap_ref[place(0)], swap_ref[place(1)])
    grad = None
    for which, copy in enumerate(copies):
        copy.wait()
        part = dot_cols(grads[which], held[which].reshape(D, D))
        grad = part if grad is None else grad + part
    back, gain_grad = norm_back(grad, hidden_zero[...], gain[...])
    swap_ref[place(2)] = (one_grad[...] + back).astype(BF)
    rest = jnp.zeros((GAIN_ROWS - 2, D), F32)
    swap_ref[3 * tok :] = jnp.concatenate([gain_grad, mid[...], rest], 0).astype(BF)


def of_core(ref, index, size):
    return jnp.concatenate(
        [ref[:, aligned(2 * index[chip] + index[4], size)] for chip in range(CHIPS)], 1
    )


def put_slabs(total, rows, at, order, keep_ref, send_ref):
    for ref, chips in ((keep_ref, order[:2]), (send_ref, order[2:])):
        for place, chip in enumerate(chips):
            ref[place, at : at + rows] = total[chip * rows : (chip + 1) * rows].astype(BF)


X_FIRST = (0, 2, 1, 3)
Y_FIRST = (0, 1, 2, 3)


def query_grad_kernel(index, both, both_c, grad, low, swapped, keep_ref, send_ref):
    rights = ((grad[...], swapped[2]), (low[...], swapped[3]))
    for which, right in enumerate(rights):
        left = [of_core(part.at[which], index, OWN_ROWS) for part in (both, both_c)]
        total = dot_rows(jnp.concatenate(left, 0), jnp.concatenate(right, 0))
        put_slabs(total, OWN_ROWS, which * OWN_ROWS, X_FIRST, keep_ref, send_ref)


def pair_grad_kernel(index, both, both_c, own, swapped, keep_ref, send_ref):
    tok = both.shape[1]
    left = jnp.concatenate([of_core(part.at[0], index, OWN_ROWS) for part in (both, both_c)], 0)
    for which in range(2):
        place = slice(which * tok, (which + 1) * tok)
        total = dot_rows(left, jnp.concatenate([own[place], swapped[place]], 0))
        put_slabs(total, OWN_ROWS, which * OWN_ROWS, Y_FIRST, keep_ref, send_ref)


def merge_grad_kernel(index, joined, joined_c, own, swapped, keep_ref, send_ref):
    tok = joined.shape[0]
    both = jnp.concatenate(
        [of_core(part, index, MERGE_ROWS) for part in (joined, joined_c)], 0
    )
    low = slice(2 * tok, 3 * tok)
    total = dot_rows(both, jnp.concatenate([own[low], swapped[low]], 0))
    put_slabs(total, MERGE_ROWS, 0, X_FIRST, keep_ref, send_ref)
    gains = own[3 * tok :].astype(F32) + swapped[3 * tok :].astype(F32)
    keep_ref[:, MERGE_ROWS:] = jnp.zeros((2, GAIN_ROWS, D), BF)
    send_ref[:, MERGE_ROWS:] = jnp.zeros((2, GAIN_ROWS, D), BF)
    for ref, chips in ((keep_ref, X_FIRST[:2]), (send_ref, X_FIRST[2:])):
        for place, chip in enumerate(chips):
            owner = 2 * index[chip] + index[4]
            lane = lax.broadcasted_iota(jnp.int32, gains.shape, 1)
            mine = jnp.where(lane // OWN_ROWS == owner, gains, 0.0)
            chosen = functools.reduce(
                jnp.add,
                [mine[:, at * OWN_ROWS : (at + 1) * OWN_ROWS] for at in range(D // OWN_ROWS)],
            )
            ref[place, MERGE_ROWS:, :OWN_ROWS] = chosen.astype(BF)


def joined_grad_kernel(index, first, second, *refs):
    weights = refs[: 2 * CHIPS]
    rows = first.shape[0]
    low = jnp.concatenate([first[...], second[...]], 0)
    micro = index[5]
    for at, weight in enumerate(weights):
        grad = dot_cols(low, weight[:MERGE_ROWS])
        owner = owner_of(index, at % CHIPS, at >= CHIPS)
        cols = aligned(owner % CHIPS, MERGE_ROWS)
        for half, out_ref in enumerate(refs[2 * CHIPS :]):

            @pl.when(owner // CHIPS == half)
            def _():
                out_ref[micro, :, cols] = grad[:rows]
                out_ref[1 - micro, :, cols] = grad[rows:]


def sum_kernel(index, *refs):
    refs[-1][...] = summed(refs[:-1])


def add_kernel(index, *refs):
    refs[-1][...] = summed(refs[:-1]).astype(BF)


def add_two_kernel(index, keep, got, own_ref, other_ref):
    own_ref[...] = summed((keep.at[0], got.at[0])).astype(BF)
    other_ref[...] = summed((keep.at[1], got.at[1])).astype(BF)


def stack_kernel(index, *refs):
    for at, part in enumerate(refs[:-1]):
        refs[-1][at] = part[...]


def result_kernel(index, *refs):
    left, right = refs[-2:]
    rows = left.shape[0]
    total = summed(refs[:-2])
    left[...] = total[:rows].astype(BF)
    right[...] = total[rows:].astype(BF)


def zero_kernel(index, swapped, left_ref, right_ref):
    rows = left_ref.shape[0]
    left_ref[...] = swapped[4 * rows : 5 * rows]
    right_ref[...] = swapped[5 * rows : 6 * rows]


def by_micro_kernel(index, first, second, out_ref):
    out_ref[index[5]] = first[...]
    out_ref[1 - index[5]] = second[...]


def chosen(index, array, got, ends):
    here = functools.reduce(jnp.logical_or, [index[6] == end for end in ends])
    return jnp.where(here, got[...], array[...])


def choose_kernel(ends, index, array, got, out_ref):
    out_ref[...] = chosen(index, array, got, ends)


def query_total_kernel(ends, index, array, got, query_ref, combiner_ref):
    total = chosen(index, array, got, ends).astype(F32)
    query_ref[...] = total[:OWN_ROWS]
    combiner_ref[...] = total[OWN_ROWS:]


def pair_total_kernel(ends, index, array, got, query, out_ref):
    total = chosen(index, array, got, ends).astype(F32)
    out_ref[:, :D] = query[...]
    out_ref[:, D : 2 * D] = total[:OWN_ROWS]
    out_ref[:, 2 * D :] = total[OWN_ROWS:]


def merge_total_kernel(ends, index, array, got, out_ref, gain_ref):
    total = chosen(index, array, got, ends).astype(F32)
    out_ref[...] = total[:MERGE_ROWS]
    gain_ref[...] = total[MERGE_ROWS : MERGE_ROWS + 8, :OWN_ROWS]


def call(kernel, vmem, grid, in_specs, out_specs, out_shape, scratch, index, token, *arrays):
    scalars = 0 if index is None else 1

    def passing(*refs):
        index_ref, refs = (refs[0], refs[1:]) if scalars else (None, refs)
        inputs = 1 + len(in_specs)
        kernel(index_ref, *refs[1:inputs], *refs[inputs + 1 :])

    anywhere = pl.BlockSpec(memory_space=pl.ANY)
    return pl.pallas_call(
        passing,
        grid_spec=pltpu.PrefetchScalarGridSpec(
            num_scalar_prefetch=scalars,
            grid=grid,
            in_specs=[anywhere] + in_specs,
            out_specs=[anywhere] + out_specs,
            scratch_shapes=scratch,
        ),
        out_shape=[jax.ShapeDtypeStruct(token.shape, token.dtype)] + out_shape,
        input_output_aliases={scalars: 0},
        name=getattr(kernel, "func", kernel).__name__,
        compiler_params=pltpu.CompilerParams(
            dimension_semantics=("arbitrary",) * len(grid), vmem_limit_bytes=vmem
        ),
        cost_estimate=pl.CostEstimate(flops=10**12, bytes_accessed=0, transcendentals=0),
    )(*([index] if scalars else []), token, *arrays)


def shape(*dims, dtype=BF):
    return jax.ShapeDtypeStruct(dims, dtype)


def whole(*dims):
    return pl.BlockSpec(dims, lambda *_: (0,) * len(dims))


def local(
    frames,
    skipped,
    lengths,
    merger,
    projector,
    combiner,
    expander,
    reducer,
    prenorm,
    midnorm,
    cotangent,
):
    rows = frames.shape[1]
    tok = 2 * rows
    blocks = lax.axis_size("blk")
    fsdp = lax.axis_size("fsdp")
    quarter = blocks // 4
    pieces = blocks // 2
    stream = rows * blocks

    me = lax.axis_index("fsdp")
    spot = lax.axis_index("blk")
    core = me % 2
    chip = me // 2
    unit = spot // quarter
    micro = unit // 2
    source_core = unit % 2
    half = (spot % quarter) * 2 + core

    def send(array, route, name="send"):
        pairs = []
        for y, x, c, b in itertools.product(range(2), range(2), range(2), range(blocks)):
            target = route(y, x, c, b)
            if target is not None:
                ty, tx, tc, tb = target
                pairs.append((((y * 2 + x) * 2 + c) * blocks + b, ((ty * 2 + tx) * 2 + tc) * blocks + tb))
        with jax.named_scope(name):
            return lax.ppermute(array, AXES, pairs)

    to_x = lambda y, x, c, b: (y, 1 - x, c, b)
    to_y = lambda y, x, c, b: (1 - y, x, c, b)
    to_diagonal = lambda y, x, c, b: (1 - y, 1 - x, c, b)
    to_core = lambda y, x, c, b: (y, x, 1 - c, b)
    around = (to_x, to_y, to_diagonal)
    over_plane = (to_x, to_diagonal, to_y)

    def holder(micro_at, c, pair):
        return (2 * micro_at + c) * quarter + pair // 2, pair % 2

    def inward(other):
        def route(y, x, c, b):
            tb, tc = holder((b + other) % 2, c, b // 2)
            return (y, x, tc, tb)

        return route

    def outward(other):
        forward = inward(other)
        table = {}
        for y, x, c, b in itertools.product(range(2), range(2), range(2), range(blocks)):
            table[forward(y, x, c, b)] = (y, x, c, b)
        return lambda *at: table[at]

    def among(by):
        def route(y, x, c, b):
            at = ((b % quarter) * 2 + c) ^ by
            return (y, x, at % 2, (b // quarter) * quarter + at // 2)

        return route

    def take_in(pick, name):
        return tuple(send(pick((spot + other) % 2), inward(other), name) for other in range(2))

    def sum_blocks(array, name, last):
        middle = blocks // 2
        plans = [{step: step + 1, blocks - 1 - step: blocks - 2 - step} for step in range(middle - 1)]
        plans.append({middle - 1: middle, middle: middle - 1})
        for moves in plans:
            got = send(array, lambda y, x, c, b: (y, x, c, moves[b]) if b in moves else None, name)
            yield
            array = add(array, got)
        for step in range(middle - 1):
            moves = {middle - 1 - step: middle - 2 - step, middle + step: middle + 1 + step}
            got = send(array, lambda y, x, c, b: (y, x, c, moves[b]) if b in moves else None, name)
            yield
            ends = tuple(moves.values())
            if step == middle - 2:
                array = last(ends, array, got)
            else:
                choose = functools.partial(choose_kernel, ends)
                array = simple(choose, [shape(*array.shape)], array, got)
        yield array

    def finish(steps):
        array = None
        while array is None:
            array = next(steps)
        return array

    gathered = lax.all_gather(jnp.concatenate([projector, combiner], 1), "fsdp", axis=0)

    gain_rows = jnp.pad(jnp.stack([prenorm, midnorm]), ((0, GAIN_ROWS - 2), (0, D - OWN_ROWS)))
    merger_own = jnp.concatenate([merger, gain_rows], 0)
    mergers = [merger_own] + [send(merger_own, route, "merger_around") for route in around]
    mergers += [send(part, to_core, "merger_core") for part in mergers]

    left, right = take_in(
        lambda m: jnp.concatenate([frames[m], skipped[m], cotangent[m]], -1), "tokens_in"
    )
    other_lengths = send(lengths, to_core, "lengths_core")

    mine = jnp.where(source_core == core, lengths, other_lengths)[:, 0]
    row_lengths = jnp.where(micro == 0, mine[0], mine[1])
    ends = jnp.cumsum(row_lengths)
    within = jnp.arange(rows, dtype=jnp.int32)

    def layout(at):
        offsets = jnp.concatenate(
            [(2 * at + micro) * rows + within, (2 * at + 1 - micro) * rows + within]
        )
        before = (ends[None, :] <= offsets[:, None]).astype(jnp.int32)
        return jnp.sum(before, 1), offsets - jnp.sum(before * row_lengths[None, :], 1)

    layouts = [layout(half ^ by) for by in range(pieces)]
    query_seg = layouts[0][0][None]
    key_segs = jnp.stack([segment for segment, _ in layouts])[:, :, None]
    inverse = 10000.0 ** (-jnp.arange(HEAD_DIM // 2, dtype=F32) * 2.0 / HEAD_DIM)
    positions = jnp.stack([position for _, position in layouts]).astype(F32)
    angles = positions[:, :, None] * inverse
    cosine = jnp.tile(jnp.cos(angles), (1, 1, 4))
    sine = jnp.sin(angles)
    sine = jnp.concatenate([-sine, sine, -sine, sine], -1)

    index = jnp.stack(
        [chip, chip ^ 1, chip ^ 2, chip ^ 3, core, spot % 2, spot, spot]
    ).astype(jnp.int32)
    last_token = [jnp.zeros((8, 128), F32)]

    def run(
        kernel, grid, in_specs, out_specs, out_shape, scratch, *arrays, vmem=SMALL, scalars=index
    ):
        last_token[0], *results = call(
            kernel,
            vmem,
            (grid,) if grid else (),
            in_specs,
            out_specs,
            out_shape,
            scratch,
            scalars,
            last_token[0],
            *arrays,
        )
        return results[0] if len(results) == 1 else results

    def rest():
        run(rest_kernel, 0, [], [], [], [], scalars=None)

    def meet():
        last_token[0] = send(last_token[0], to_core, "order")

    def simple(kernel, outs, *arrays, scalars=index):
        held = pl.BlockSpec(memory_space=pltpu.VMEM)
        return run(
            kernel,
            0,
            [held] * len(arrays),
            [held] * len(outs),
            outs,
            [],
            *arrays,
            scalars=scalars,
        )

    def to_total(kernel, outs):
        return lambda ends, array, got: simple(functools.partial(kernel, ends), outs, array, got)

    def add(*arrays):
        return simple(add_kernel, [shape(*arrays[0].shape)], *arrays, scalars=None)

    def first_step(keep, got):
        return simple(add_two_kernel, [shape(*keep.shape[1:])] * 2, keep, got, scalars=None)

    wide = 2 * OWN_ROWS
    cols_at = lambda height, width: pl.BlockSpec((height, width), lambda s, *_: (0, s))
    cols_of = lambda height, width: pl.BlockSpec((height, width), lambda s, i: (0, i[s]))
    table = whole(tok, PAIR)
    tables = whole(pieces, tok, PAIR)

    down_c = send(reducer, to_core, "w_down_core")
    chunk = expander.shape[1] // CHIPS
    w_down = simple(down_kernel, [shape(2, HIDDEN_ROWS, D)], reducer, down_c).reshape(chunk, D)
    hidden_zero, cot, joined, gain_pre, gain_mid = simple(
        merge_kernel,
        [shape(tok, D, dtype=F32), shape(tok, D), shape(tok, 2 * D)]
        + [shape(1, D, dtype=F32)] * 2,
        left,
        right,
        *mergers,
    )
    joined_c = send(joined, to_core, "joined_core")

    groups = [[c + 2 * at for at in range(CHIPS)] for c in range(2)]
    swap_chunks = lambda parts: lax.all_to_all(
        parts, "fsdp", 0, 0, axis_index_groups=groups, tiled=True
    )
    up_swapped = swap_chunks(
        simple(feed_send_kernel, [shape(CHIPS, OWN_ROWS, chunk)], expander, scalars=None)
    )
    fetched = pl.BlockSpec(memory_space=pltpu.HBM)
    act_first, query, pair, cot_again = run(
        project_kernel,
        1,
        [whole(tok, D), whole(1, D), fetched, table, table, whole(tok, D)],
        [whole(tok, D), whole(tok, D), whole(2, tok, D), whole(tok, D)],
        [shape(tok, D), shape(tok, D), shape(2, tok, D), shape(tok, D)],
        [pltpu.VMEM((3, fsdp, OWN_ROWS, D), BF), pltpu.SemaphoreType.DMA((3,))],
        hidden_zero,
        gain_pre,
        gathered,
        cosine[0],
        sine[0],
        cot,
        vmem=HUGE,
        scalars=None,
    )
    cots = [send(cot_again, route, "cot_around") for route in over_plane]
    up_mine = simple(copy_kernel, [shape(CHIPS, OWN_ROWS, chunk)], up_swapped, scalars=None)
    up_c = send(up_mine, to_core, "w_up_core")
    pairs = [pair] + [send(pair, among(by), "pair_core") for by in range(1, pieces)]
    steps, vmem = (1, LARGE) if pieces == 2 else (CHIPS * 2, HUGE)
    head_cols = cols_at(tok, D // steps)
    pair_cols = lambda count: pl.BlockSpec((count, tok, D // steps), lambda s, *_: (0, 0, s))
    probs_spec = pl.BlockSpec((HEADS // steps, pieces, tok, tok), lambda s, *_: (s, 0, 0, 0))
    combiner_held = [pltpu.VMEM((fsdp, OWN_ROWS, D), BF), pltpu.SemaphoreType.DMA]
    attended, hidden_one, act_second, probs = run(
        functools.partial(attend_kernel, pieces),
        steps,
        [head_cols, whole(1, tok), whole(pieces, tok, 1)]
        + [pair_cols(2)] * pieces
        + [whole(tok, D), fetched, whole(tok, D), whole(1, D)],
        [whole(2, tok, D), whole(tok, D), whole(tok, D), probs_spec],
        [
            shape(2, tok, D),
            shape(tok, D, dtype=F32),
            shape(tok, D),
            shape(HEADS, pieces, tok, tok),
        ],
        combiner_held,
        query,
        query_seg,
        key_segs,
        *pairs,
        act_first,
        gathered,
        hidden_zero,
        gain_mid,
        vmem=vmem,
        scalars=None,
    )
    acts = [act_second] + [send(act_second, route, "act_around") for route in over_plane]
    attended_c = send(attended, to_core, "attended_core")
    w_up = simple(up_kernel, [shape(fsdp, OWN_ROWS, chunk)], up_mine, up_c).reshape(D, chunk)
    cots = [cot] + simple(three_kernel, [shape(tok, D)] * 3, *cots, scalars=None)

    fed = [
        simple(
            feed_kernel,
            [shape(tok, D), shape(tok, chunk), shape(tok, chunk)],
            act,
            grad,
            w_up,
            w_down,
            scalars=None,
        )
        for act, grad in zip(acts, cots)
    ]
    seconds = [fed[0][0]] + [
        send(part[0], route, "second_around") for part, route in zip(fed[1:], over_plane)
    ]
    activs = [part[1] for part in fed]
    down_parts = simple(
        down_grad_kernel, [shape(2, HIDDEN_ROWS, D)], *activs, *cots, scalars=None
    )
    core_groups = [[at, at + 1] for at in range(0, fsdp, 2)]
    down_halves = lax.all_to_all(
        down_parts, "fsdp", 0, 0, axis_index_groups=core_groups, tiled=True
    )
    up_keep, up_send = simple(
        up_grad_kernel, [shape(CHIPS, OWN_ROWS, chunk)] * 2, *acts, *[part[2] for part in fed]
    )
    up_got = send(up_send, to_core, "up_core")

    second = simple(
        sum_kernel, [shape(tok, D, dtype=F32)], seconds[0], seconds[1], scalars=None
    )
    second = simple(sum_kernel, [shape(tok, D, dtype=F32)], second, seconds[2], scalars=None)

    reversed_blocks = [list(reversed(range(blocks)))]
    down_total = lax.psum(
        simple(halves_kernel, [shape(HIDDEN_ROWS, D)], down_halves, scalars=None),
        "blk",
        axis_index_groups=reversed_blocks,
    )
    meet()

    steps = 2 if pieces == 2 else 2 * CHIPS
    head_cols = cols_at(tok, D // steps)
    pair_cols = lambda count: pl.BlockSpec((count, tok, D // steps), lambda s, *_: (0, 0, s))
    probs_spec = pl.BlockSpec((HEADS // steps, pieces, tok, tok), lambda s, *_: (s, 0, 0, 0))
    counts = [4 if by == 1 else 2 for by in range(pieces)]
    back = run(
        functools.partial(attend_back_kernel, pieces),
        steps,
        [head_cols, probs_spec]
        + [pair_cols(2)] * pieces
        + [fetched, whole(tok, D), whole(tok, D), whole(1, D)]
        + [tables, tables]
        + [whole(tok, D)] * 2,
        [whole(tok, D), whole(tok, D), whole(1, D), head_cols] + [pair_cols(n) for n in counts],
        [
            shape(tok, D, dtype=F32),
            shape(tok, D),
            shape(1, D, dtype=F32),
            shape(tok, D),
        ]
        + [shape(n, tok, D) for n in counts],
        combiner_held,
        query,
        probs,
        *pairs,
        gathered,
        hidden_one,
        cot,
        gain_mid,
        cosine,
        sine,
        second,
        seconds[3],
        vmem=HUGE,
        scalars=None,
    )
    one_grad, one_low, mid_grad, query_grad = back[:4]
    pair_grads = [back[4]] + [
        send(part, among(by), "pair_grads_core") for by, part in enumerate(back[5:], 1)
    ]
    up_swapped = swap_chunks(add(up_keep, up_got))
    swapped = run(
        functools.partial(united_kernel, pieces),
        1,
        [whole(tok, D), whole(1, D)]
        + [whole(n, tok, D) for n in counts]
        + [fetched, whole(tok, D), whole(tok, D), whole(1, D)],
        [whole(3 * tok + GAIN_ROWS, D)],
        [shape(3 * tok + GAIN_ROWS, D)],
        [pltpu.VMEM((3, fsdp, OWN_ROWS, D), BF), pltpu.SemaphoreType.DMA((3,))],
        query_grad,
        mid_grad,
        *pair_grads,
        gathered,
        hidden_zero,
        one_grad,
        gain_pre,
        vmem=HUGE,
        scalars=None,
    )
    swapped_c = send(swapped, to_core, "zero_core")

    def slabs_of(kernel, height, *arrays):
        return simple(kernel, [shape(2, height, D)] * 2, *arrays)

    query_keep, query_send = slabs_of(
        query_grad_kernel,
        2 * OWN_ROWS,
        attended,
        attended_c,
        query_grad,
        one_low,
        pair_grads[1],
    )
    query_got = send(query_send, to_x, "query_x")
    other_order = [blocks // 2 + at if at < blocks // 2 else at - blocks // 2 for at in range(blocks)]
    up_total = lax.psum(
        simple(copy_kernel, [shape(CHIPS, OWN_ROWS, chunk)], up_swapped, scalars=None),
        "blk",
        axis_index_groups=[other_order],
    )
    merge_keep, merge_send = slabs_of(
        merge_grad_kernel, MERGE_ROWS + GAIN_ROWS, joined, joined_c, swapped, swapped_c
    )
    merge_got = send(merge_send, to_x, "merge_x")
    pair_keep, pair_send = slabs_of(
        pair_grad_kernel, 2 * OWN_ROWS, attended, attended_c, swapped, swapped_c
    )
    pair_got = send(pair_send, to_y, "pair_y")
    zero_back = [
        send(part, outward(other), "zero_out")
        for other, part in enumerate(
            simple(zero_kernel, [shape(rows, D)] * 2, swapped, scalars=None)
        )
    ]
    result_parts = simple(result_parts_kernel, [shape(CHIPS, tok, D)], *activs, w_down)
    result_sum = lax.psum_scatter(
        result_parts, "fsdp", scatter_dimension=0, axis_index_groups=groups, tiled=True
    )
    query_own, query_other = first_step(query_keep, query_got)
    query_y = send(query_other, to_y, "query_y")
    merge_own, merge_other = first_step(merge_keep, merge_got)
    merge_y = send(merge_other, to_y, "merge_y")
    pair_own, pair_other = first_step(pair_keep, pair_got)
    pair_x = send(pair_other, to_x, "pair_x")
    query_steps = sum_blocks(
        add(query_own, query_y),
        "query_blocks",
        to_total(query_total_kernel, [shape(OWN_ROWS, D, dtype=F32)] * 2),
    )
    next(query_steps)
    frames_grad, skipped_grad = simple(
        joined_grad_kernel, [shape(MB, rows, D, dtype=F32)] * 2, *zero_back, *mergers
    )
    merge_steps = sum_blocks(
        add(merge_own, merge_y),
        "merge_blocks",
        to_total(
            merge_total_kernel,
            [shape(*merger.shape, dtype=F32), shape(8, OWN_ROWS, dtype=F32)],
        ),
    )
    next(merge_steps)
    to_projector = lambda ends, array, got: simple(
        functools.partial(pair_total_kernel, ends),
        [shape(*projector.shape, dtype=F32)],
        array,
        got,
        query_total,
    )
    pair_steps = sum_blocks(add(pair_own, pair_x), "pair_blocks", to_projector)
    next(pair_steps)
    next(query_steps)
    next(merge_steps)
    next(pair_steps)
    next(query_steps)
    next(merge_steps)
    next(pair_steps)
    reducer_grad, expander_grad = simple(
        feed_total_kernel,
        [shape(*reducer.shape, dtype=F32), shape(*expander.shape, dtype=F32)],
        down_total,
        up_total,
        scalars=None,
    )
    results = simple(
        result_kernel, [shape(rows, D)] * 2, result_sum[0], hidden_one, scalars=None
    )
    results = [send(part, outward(other), "result_out") for other, part in enumerate(results)]
    query_total, combiner_grad = finish(query_steps)
    merger_grad, gain_grads = finish(merge_steps)
    projector_grad = finish(pair_steps)
    result_out = simple(by_micro_kernel, [shape(MB, rows, D)], *results)
    return (
        result_out,
        frames_grad,
        skipped_grad,
        merger_grad,
        projector_grad,
        combiner_grad,
        expander_grad,
        reducer_grad,
        gain_grads[0],
        gain_grads[1],
    )


def solution(mesh):
    tokens = P(None, ("fsdp", "blk"), None)
    weight = P("fsdp", None)
    gain = P("fsdp")
    return jax.shard_map(
        local,
        mesh=mesh,
        in_specs=(tokens, tokens, P(None, "fsdp", None))
        + (weight,) * 5
        + (gain, gain, tokens),
        out_specs=(tokens, tokens, tokens) + (weight,) * 5 + (gain, gain),
        check_vma=False,
    )
```
